32 devices in a mesh: grp: 4 (over x, core), freq: 8 (over z, y).
Axes of the slice: x: 2, y: 2, z: 4, core: 2. Of those that a mesh axis runs over, the one named last changes fastest.
Arguments:
- spectra: float32 [32, 2, 4096], P('grp', None, 'freq'), may hold values from -6 to 6
- station_mask: int32 [32], P('grp'), may hold values 0 or 1
- owners: int32 [4, 2, 64, 1], P('grp'), may hold values from 0 to 3; in each aligned block of 64 rows (0 to 63, 64 to 127, ..., all dimensions but the last counted through in order) at most 32 rows name the same one
Outputs:
- inbox: float32 [4, 2, 4, 32, 4096], P('grp', None, None, None, 'freq')
The draws below stay inside these ranges and needn't reach their ends.
Inputs may be any that keep to these rules, and one draw needn't show every extreme that they name: `owners`: in each round, no owner is named by more than 32 of one group's 64 pairs, a bound that some block reaches; every group owns some pair.
All inputs are finite; a program needn't handle non-finite values. No bound on the sum of `station_mask` on one device may be relied on, other than what follows from the above.
Results may differ from the reference program's by a relative error of at most 0.0003.
Values sent between devices are 32-bit elements; how exact they have to be, the bound alone decides.
No kernel may reach another device: no remote copies, remote signals or barrier semaphores. Data moves between devices by JAX's collectives and lax.ppermute only.
A program may use at most 128 MiB of HBM per device.

```python
import math
import jax
import jax.numpy as jnp
import numpy as np
from jax import lax

NF = 4096
LAGS = 4096
STA_DEV = 8
ROUNDS = 2
GROUPS = 4
STATIONS = 32
PAIRS = 64
CAP = 32


def set_ends(entries, own_key, low, top_value):
    extent = entries.shape
    index_at = [jax.random.randint(jax.random.fold_in(own_key, axis), (), 0, extent[axis]) for axis in range(len(extent))]
    entries = entries.at[tuple(index_at)].set(low)
    longest = extent.index(max(extent))
    index_at[longest] = (index_at[longest] + 1) % extent[longest]
    return entries.at[tuple(index_at)].set(top_value)


def steps_of(own_key, dims, split, smallest, largest):
    loudness, own = 1.0, jax.random.fold_in(own_key, 6)
    for axis_at, parts in split:
        draws = jnp.exp(jax.random.uniform(jax.random.fold_in(own, axis_at), (parts,), jnp.float32, smallest / len(split), largest / len(split)))
        loudness = loudness * jnp.repeat(draws, dims[axis_at] // parts).reshape([-1 if axis == axis_at else 1 for axis in range(len(dims))])
    return loudness


def shared_out(stream_key, own, number, rows, amount, top, most, skew):
    sequence = jax.random.permutation(stream_key, amount)
    heavy_load, usual = portions_of(amount, rows * top, most, skew, True), portions_of(amount, rows * top, most, skew, False)
    places = jnp.arange(amount)

    def named(tallies, rotation):
        used = int((tallies > 0).sum())
        fixed = max(1, used // 4)
        passed = fixed + (places - fixed + rotation * (used - fixed)) % max(1, amount - fixed)
        return jnp.zeros((amount,), jnp.int32).at[sequence[jnp.where(places < fixed, places, passed)]].set(jnp.asarray(tallies, jnp.int32))

    tallies = jnp.where(number % 4 == 0, named(heavy_load, number // 4), named(usual, number - number // 4 - 1))
    mixed = jax.random.permutation(jax.random.fold_in(own, 3), amount)
    giver, receiver = mixed[0:amount // 2 * 2:2], mixed[1:amount // 2 * 2:2]
    slack = jnp.minimum(tallies[giver] - 1, most - tallies[receiver]) // 2
    slack = jnp.where((giver == sequence[0]) | (receiver == sequence[0]) | (tallies[receiver] == 0), 0, jnp.maximum(slack, 0))
    passed = jax.random.randint(jax.random.fold_in(own, 4), (amount // 2,), 0, 1 << 20) % (slack + 1)
    tallies = tallies.at[giver].add(-passed).at[receiver].add(passed)
    members = jnp.searchsorted(jnp.cumsum(tallies), jnp.arange(rows * top), side="right").astype(jnp.int32)
    listing = members.reshape(top, rows).T
    listing = listing[jax.random.permutation(jax.random.fold_in(own, 1), rows)]
    rotation = jax.random.randint(jax.random.fold_in(own, 2), (rows, 1), 0, top)
    return jnp.take_along_axis(listing, (jnp.arange(top)[None, :] + rotation) % top, axis=1)


def portions_of(number_of, total, reach, slope, full):
    weights = [(1 << 20) // math.isqrt(grade ** slope) + 1 for grade in range(1, number_of + 1)]
    largest = reach if full else min(reach, max(-(-total // number_of), total * weights[0] // sum(weights)))
    least = 1 if total - largest >= number_of - 1 else 0
    counts, rest = [largest] + [least] * (number_of - 1), total - largest - least * (number_of - 1)
    while rest > 0:
        movable = [i for i in range(1, number_of) if counts[i] < largest] or [i for i in range(1, number_of) if counts[i] < reach]
        pool, remaining = sum([weights[i] for i in movable]), rest
        for i in movable:
            extra = min(reach - counts[i], max(1, remaining * weights[i] // pool), rest)
            counts[i] = counts[i] + extra
            rest = rest - extra
    return np.array(counts)


def noise(own_key, dims, width, limit, shards=(), kind=jnp.bfloat16):
    result = jax.random.normal(own_key, dims, jnp.float32) * width
    if len(shards) > 0:
        result = steps_of(own_key, dims, shards, -0.22, 0.18) * result
    return jnp.clip(result, min=-limit, max=limit).astype(kind)


def setup_inputs(seed: int = 0) -> dict:
    splits = jax.random.split(jax.random.key(seed), 4)
    spectra = noise(splits[0], (STATIONS, 2, NF), 1.0, 6.0, ((0, 4), (2, 8)), jnp.float32)
    station_mask = set_ends((jax.random.randint(splits[1], (STATIONS,), 0, 8) < 7).astype(jnp.int32), jax.random.fold_in(splits[1], 1), 0, 1)
    owners_keys = jax.random.split(jax.random.fold_in(splits[2], 1), GROUPS * ROUNDS * PAIRS // PAIRS)
    owners_turns = jax.random.permutation(jax.random.fold_in(splits[2], 3), GROUPS * ROUNDS * PAIRS // PAIRS)
    owners = jax.vmap(lambda own, number: shared_out(jax.random.fold_in(splits[2], 2), own, number, PAIRS, GROUPS, 1, CAP, 2))(owners_keys, owners_turns).reshape((GROUPS, ROUNDS, PAIRS, 1))
    return {"spectra": spectra, "station_mask": station_mask, "owners": owners}


def lag_tables(first_bin, bin_block):
    bin_ids = first_bin + jnp.arange(bin_block, dtype=jnp.int32)
    lag_ids = jnp.arange(LAGS, dtype=jnp.int32) - LAGS // 2
    phase_turns = jnp.mod(bin_ids[:, None] * lag_ids[None, :], 2 * NF)
    angles = phase_turns.astype(jnp.float32) * (math.pi / NF)
    return (jnp.cos(angles), jnp.sin(angles))

def to_lags(cross_real, cross_imag):
    bin_block = math.gcd(NF, 512)

    def accumulate(running, first_bin):
        cosine_table, sine_table = lag_tables(first_bin, bin_block)
        part_real = lax.dynamic_slice_in_dim(cross_real, first_bin, bin_block, 1)
        part_imag = lax.dynamic_slice_in_dim(cross_imag, first_bin, bin_block, 1)
        running = running + jnp.dot(part_real, cosine_table, precision=lax.Precision.HIGHEST)
        running = running - jnp.dot(part_imag, sine_table, precision=lax.Precision.HIGHEST)
        return (running, None)
    starts = jnp.arange(0, NF, bin_block, dtype=jnp.int32)
    running, _ = lax.scan(accumulate, jnp.zeros((cross_real.shape[0], LAGS), jnp.float32), starts)
    return running / math.sqrt(NF)

def reference(spectra, station_mask, owners):
    grouped = spectra.reshape(GROUPS, STA_DEV, 2, NF)
    weights = station_mask.reshape(GROUPS, STA_DEV).astype(jnp.float32)
    pair_ids = jnp.arange(PAIRS, dtype=jnp.int32)
    earlier = pair_ids[None, :] < pair_ids[:, None]
    slot_ids = jnp.arange(GROUPS * CAP, dtype=jnp.int32)
    results = []
    for round_index in range(ROUNDS):
        shift_by = round_index + 1
        partner = jnp.roll(grouped, shift_by, axis=0)
        partner_weight = jnp.roll(weights, shift_by, axis=0)
        pair_weight = (weights[:, :, None] * partner_weight[:, None, :])[..., None]
        cross_real = (grouped[:, :, None, 0] * partner[:, None, :, 0] + grouped[:, :, None, 1] * partner[:, None, :, 1]) * pair_weight
        cross_imag = (grouped[:, :, None, 1] * partner[:, None, :, 0] - grouped[:, :, None, 0] * partner[:, None, :, 1]) * pair_weight
        correlation = to_lags(cross_real.reshape(GROUPS * PAIRS, NF), cross_imag.reshape(GROUPS * PAIRS, NF))
        correlation = correlation.reshape(GROUPS, PAIRS, LAGS)
        owner_ids = owners[:, round_index, :, 0]
        same_owner = (owner_ids[:, :, None] == owner_ids[:, None, :]) & earlier[None]
        pair_rank = lax.optimization_barrier(jnp.sum(same_owner.astype(jnp.int32), axis=2))
        slot_index = owner_ids * CAP + pair_rank
        placing = (slot_index[:, :, None] == slot_ids[None, None, :]).astype(jnp.float32)
        received = jnp.einsum('gpx,gpl->gxl', placing, correlation, precision=lax.Precision.HIGHEST)
        results.append(received.reshape(GROUPS, GROUPS, CAP, LAGS))
    stacked = jnp.stack(results, axis=0)
    return jnp.transpose(stacked, (2, 0, 1, 3, 4))
```

```python
import functools
import math

import jax
import jax.numpy as jnp
import numpy as np
from jax import lax
from jax.experimental import pallas as pl
from jax.experimental.pallas import tpu as pltpu
from jax.sharding import PartitionSpec as P

LAGS = 4096
LANES = 128
SUBLANES = 8
PARTS = 3


def split_bf16(values, parts):
    pieces = []
    for _ in range(parts - 1):
        piece = values.astype(jnp.bfloat16)
        pieces.append(piece)
        values = values - piece.astype(jnp.float32)
    pieces.append(values.astype(jnp.bfloat16))
    return pieces


def dft_tables(bin_total, half_band):
    turns = (np.arange(bin_total)[:, None] * (2 * np.arange(half_band) + 1)[None, :]) % (4 * bin_total)
    angles = turns * (math.pi / (2 * bin_total))
    tables = []
    for exact in (np.cos(angles), np.sin(angles)):
        high = exact.astype(jnp.bfloat16)
        low = (exact - high.astype(np.float64)).astype(jnp.bfloat16)
        tables += [high, low]
    return tables


def iota(shape, axis):
    return lax.broadcasted_iota(jnp.int32, shape, axis)


def dot(left, right):
    return jnp.dot(left, right, preferred_element_type=jnp.float32)


def pick_matrices(owner_ids, me, groups, stations, rounds, capacity):
    pairs = stations * stations
    listed = rounds * pairs
    rows = rounds * groups * capacity
    mine = owner_ids == me
    before = (iota((listed, listed), 0) < iota((listed, listed), 1)) & (
        iota((listed, listed), 0) // pairs == iota((listed, listed), 1) // pairs
    )
    rank = dot(mine.astype(jnp.bfloat16), before.astype(jnp.bfloat16))
    marked = jnp.where(mine, rank, -1.0).astype(jnp.bfloat16)
    of_group = (iota((rows, groups), 0) // capacity) % groups == iota((rows, groups), 1)
    held = dot(of_group.astype(jnp.bfloat16), marked)
    row_id = iota((rows, listed), 0)
    lane_id = iota((rows, listed), 1)
    chosen = (held == (row_id % capacity).astype(jnp.float32)) & (
        row_id // (groups * capacity) == lane_id // pairs
    )
    chosen = chosen.astype(jnp.bfloat16)
    columns = PARTS * groups * stations
    pair_id = iota((listed, columns), 0) % pairs
    station = iota((listed, columns), 1) % stations
    first = dot(chosen, (pair_id // stations == station).astype(jnp.bfloat16))
    second = dot(chosen, (pair_id % stations == station).astype(jnp.bfloat16))
    row_id = iota((rows, columns), 0)
    row_group = (row_id // capacity) % groups
    row_round = row_id // (groups * capacity)
    column_group = (iota((rows, columns), 1) // stations) % groups
    partner = (row_group + groups - 1 - row_round) % groups
    first = jnp.where(column_group == row_group, first, 0.0)
    second = jnp.where(column_group == partner, second, 0.0)
    return first.astype(jnp.bfloat16), second.astype(jnp.bfloat16)


def stack_kernel(
    sizes, me_ref, block_ref, owners_ref, twist_ref, ch_ref, cl_ref, sh_ref, sl_ref, out_ref,
    pick_a, pick_b, even, odd,
):
    groups, stations, rounds, capacity, band_bins = sizes
    step = pl.program_id(0)
    chunks = band_bins // LANES
    held = groups * stations

    @pl.when(step == 0)
    def _():
        first, second = pick_matrices(
            owners_ref[...], me_ref[0], groups, stations, rounds, capacity
        )
        pick_a[...] = first
        pick_b[...] = second
        even[...] = jnp.zeros_like(even)
        odd[...] = jnp.zeros_like(odd)

    def band(part):
        tiles = [
            block_ref[:, 0, pl.ds((part * chunks + q) * stations, stations), :].reshape(held, LANES)
            for q in range(chunks)
        ]
        return jnp.concatenate(tiles, axis=1)

    real, imag = band(0), band(1)
    turn_cos, turn_sin = twist_ref[0, 0:1, :], twist_ref[0, 1:2, :]
    turned_real = real * turn_cos + imag * turn_sin
    turned_imag = imag * turn_cos - real * turn_sin

    def picked(pick, values):
        return dot(pick[...], jnp.concatenate(split_bf16(values, PARTS), axis=0))

    a_real, a_imag = picked(pick_a, real), picked(pick_a, imag)
    b_real, b_imag = picked(pick_b, turned_real), picked(pick_b, turned_imag)
    cross_real = a_real * b_real + a_imag * b_imag
    cross_imag = a_imag * b_real - a_real * b_imag
    high, low = split_bf16(cross_real, 2)
    even[...] += dot(high, ch_ref[...]) + (dot(high, cl_ref[...]) + dot(low, ch_ref[...]))
    high, low = split_bf16(cross_imag, 2)
    odd[...] += dot(high, sh_ref[...]) + (dot(high, sl_ref[...]) + dot(low, sh_ref[...]))

    @pl.when(step == pl.num_programs(0) - 1)
    def _():
        half = even.shape[1]
        total = even[...] + odd[...]
        mirror = (iota((half, half), 0) + iota((half, half), 1) == half - 1).astype(jnp.bfloat16)
        pieces = [dot(piece, mirror) for piece in split_bf16(total, 3)]
        below = pieces[0] + (pieces[1] + pieces[2])
        out_ref[...] = jnp.concatenate([below, even[...] - odd[...]], axis=1)


def per_device(spectra, station_mask, owners):
    stations, _, band_bins = spectra.shape
    groups = lax.axis_size("grp")
    shards = lax.axis_size("freq")
    rounds = owners.shape[1]
    pairs = stations * stations
    bin_total = band_bins * shards
    capacity = (2 * pairs + groups - 1) // groups
    lag_band = LAGS // shards
    half_band = lag_band // 2
    chunks = band_bins // LANES
    rows = rounds * groups * capacity

    masked = spectra * station_mask.astype(jnp.float32)[:, None, None]
    tiles = masked.reshape(stations, 2, chunks, LANES).transpose(1, 2, 0, 3)
    tiles = tiles.reshape(2 * chunks * stations, LANES)
    listed = owners[0, :, :, 0].reshape(1, rounds * pairs).astype(jnp.float32)
    listed = jnp.broadcast_to(listed, (SUBLANES, rounds * pairs))
    payload = jnp.concatenate([tiles, listed], axis=0)
    gathered = lax.all_gather(payload, ("grp", "freq"), axis=0, tiled=False)
    depth = payload.shape[0]
    gathered = gathered.reshape(groups, shards, depth, LANES)
    owner_ids = gathered[:, 0, depth - SUBLANES, :].astype(jnp.int32)

    me = lax.axis_index("grp").astype(jnp.int32).reshape(1)
    centre = lag_band * (2 * lax.axis_index("freq") + 1) - 1 - LAGS
    turns = jnp.mod(jnp.arange(bin_total, dtype=jnp.int32) * centre, 4 * bin_total)
    angles = turns.astype(jnp.float32) * (math.pi / (2 * bin_total))
    norm = 1.0 / math.sqrt(bin_total)
    twist = jnp.stack([jnp.cos(angles) * norm, jnp.sin(angles) * norm])
    twist = twist.reshape(2, shards, band_bins).transpose(1, 0, 2)
    tables = [jnp.asarray(table) for table in dft_tables(bin_total, half_band)]

    table_spec = pl.BlockSpec((band_bins, half_band), lambda f: (f, 0))
    columns = PARTS * groups * stations
    out = pl.pallas_call(
        functools.partial(stack_kernel, (groups, stations, rounds, capacity, band_bins)),
        grid=(shards,),
        out_shape=jax.ShapeDtypeStruct((rows, lag_band), jnp.float32),
        in_specs=[
            pl.BlockSpec(memory_space=pltpu.SMEM),
            pl.BlockSpec((groups, 1, depth, LANES), lambda f: (0, f, 0, 0)),
            pl.BlockSpec((groups, LANES), lambda f: (0, 0)),
            pl.BlockSpec((1, 2, band_bins), lambda f: (f, 0, 0)),
            table_spec,
            table_spec,
            table_spec,
            table_spec,
        ],
        out_specs=pl.BlockSpec((rows, lag_band), lambda f: (0, 0)),
        scratch_shapes=[
            pltpu.VMEM((rows, columns), jnp.bfloat16),
            pltpu.VMEM((rows, columns), jnp.bfloat16),
            pltpu.VMEM((rows, half_band), jnp.float32),
            pltpu.VMEM((rows, half_band), jnp.float32),
        ],
        compiler_params=pltpu.CompilerParams(
            dimension_semantics=("arbitrary",), vmem_limit_bytes=32 * 1024 * 1024
        ),
        name="owned_stacks",
    )(me, gathered, owner_ids, twist, *tables)
    return out.reshape(1, rounds, groups, capacity, lag_band)


def solution(mesh):
    placed = (P("grp", None, "freq"), P("grp"), P("grp", None, None, None))
    return jax.shard_map(
        per_device,
        mesh=mesh,
        in_specs=placed,
        out_specs=P("grp", None, None, None, "freq"),
        check_vma=False,
    )
```

```python
import functools
import math

import jax
import jax.numpy as jnp
import numpy as np
from jax import lax
from jax.experimental import pallas as pl
from jax.experimental.pallas import tpu as pltpu
from jax.sharding import PartitionSpec as P

LAGS = 4096
LANES = 128
PARTS = 3


def split_bf16(values, parts):
    pieces = []
    for _ in range(parts - 1):
        piece = values.astype(jnp.bfloat16)
        pieces.append(piece)
        values = values - piece.astype(jnp.float32)
    pieces.append(values.astype(jnp.bfloat16))
    return pieces


def dft_tables(bin_total, half_band):
    turns = (np.arange(bin_total)[:, None] * (2 * np.arange(half_band) + 1)[None, :]) % (4 * bin_total)
    angles = turns * (math.pi / (2 * bin_total))
    tables = []
    for exact in (np.cos(angles), np.sin(angles)):
        high = exact.astype(jnp.bfloat16)
        low = (exact - high.astype(np.float64)).astype(jnp.bfloat16)
        tables += [high, low]
    return tables


def iota(shape, axis):
    return lax.broadcasted_iota(jnp.int32, shape, axis)


def dot(left, right):
    return jnp.dot(left, right, preferred_element_type=jnp.float32)


def pick_matrices(owner_ids, column_group, me, groups, stations, rounds, capacity):
    pairs = stations * stations
    listed = rounds * pairs
    rows = rounds * groups * capacity
    mine = owner_ids == me
    before = (iota((listed, listed), 0) < iota((listed, listed), 1)) & (
        iota((listed, listed), 0) // pairs == iota((listed, listed), 1) // pairs
    )
    rank = dot(mine.astype(jnp.bfloat16), before.astype(jnp.bfloat16))
    marked = jnp.where(mine, rank, -1.0).astype(jnp.bfloat16)
    of_group = (iota((rows, groups), 0) // capacity) % groups == iota((rows, groups), 1)
    held = dot(of_group.astype(jnp.bfloat16), marked)
    row_id = iota((rows, listed), 0)
    lane_id = iota((rows, listed), 1)
    chosen = (held == (row_id % capacity).astype(jnp.float32)) & (
        row_id // (groups * capacity) == lane_id // pairs
    )
    chosen = chosen.astype(jnp.bfloat16)
    columns = PARTS * groups * stations
    pair_id = iota((listed, columns), 0) % pairs
    station = iota((listed, columns), 1) % stations
    first = dot(chosen, (pair_id // stations == station).astype(jnp.bfloat16))
    second = dot(chosen, (pair_id % stations == station).astype(jnp.bfloat16))
    row_id = iota((rows, columns), 0)
    row_group = (row_id // capacity) % groups
    row_round = row_id // (groups * capacity)
    partner = (row_group + groups - 1 - row_round) % groups
    first = jnp.where(column_group == row_group, first, 0.0)
    second = jnp.where(column_group == partner, second, 0.0)
    return first.astype(jnp.bfloat16), second.astype(jnp.bfloat16)


def stack_kernel(sizes, bands_ref, me_ref, owners_ref, columns_ref, twist_ref, *refs):
    groups, stations, rounds, capacity, band_bins = sizes
    block_refs, refs = refs[:-9], refs[-9:]
    ch_ref, cl_ref, sh_ref, sl_ref, out_ref, pick_a, pick_b, even, odd = refs
    step = pl.program_id(0)
    chunks = band_bins // LANES

    @pl.when(step == 0)
    def _():
        first, second = pick_matrices(
            owners_ref[...], columns_ref[...], me_ref[0], groups, stations, rounds, capacity
        )
        pick_a[...] = first
        pick_b[...] = second
        even[...] = jnp.zeros_like(even)
        odd[...] = jnp.zeros_like(odd)

    def band(part):
        tiles = []
        for q in range(chunks):
            rows = pl.ds((part * chunks + q) * stations, stations)
            held = [
                ref[group, 0, rows, :] for ref in block_refs for group in range(ref.shape[0])
            ]
            tiles.append(jnp.concatenate(held, axis=0))
        return jnp.concatenate(tiles, axis=1)

    real, imag = band(0), band(1)
    turn_cos, turn_sin = twist_ref[0, 0:1, :], twist_ref[0, 1:2, :]
    turned_real = real * turn_cos + imag * turn_sin
    turned_imag = imag * turn_cos - real * turn_sin

    def picked(pick, values):
        return dot(pick[...], jnp.concatenate(split_bf16(values, PARTS), axis=0))

    a_real, a_imag = picked(pick_a, real), picked(pick_a, imag)
    b_real, b_imag = picked(pick_b, turned_real), picked(pick_b, turned_imag)
    cross_real = a_real * b_real + a_imag * b_imag
    cross_imag = a_imag * b_real - a_real * b_imag
    high, low = split_bf16(cross_real, 2)
    even[...] += dot(high, ch_ref[...]) + (dot(high, cl_ref[...]) + dot(low, ch_ref[...]))
    high, low = split_bf16(cross_imag, 2)
    odd[...] += dot(high, sh_ref[...]) + (dot(high, sl_ref[...]) + dot(low, sh_ref[...]))

    @pl.when(step == pl.num_programs(0) - 1)
    def _():
        half = even.shape[1]
        total = even[...] + odd[...]
        mirror = (iota((half, half), 0) + iota((half, half), 1) == half - 1).astype(jnp.bfloat16)
        pieces = [dot(piece, mirror) for piece in split_bf16(total, 3)]
        below = pieces[0] + (pieces[1] + pieces[2])
        out_ref[...] = jnp.concatenate([below, even[...] - odd[...]], axis=1)


def swapped(block, axis, mask):
    route = [(i ^ mask, i) for i in range(lax.axis_size(axis))]
    return lax.ppermute(block, axis, route)


def shifted(block, axis, distance):
    size = lax.axis_size(axis)
    return lax.ppermute(block, axis, [((i - distance) % size, i) for i in range(size)])


def of_all(block, axis):
    size = lax.axis_size(axis)
    me = lax.axis_index(axis)
    blocks = [block] + [shifted(block, axis, distance) for distance in range(1, size)]
    places = jnp.stack([(me - distance) % size for distance in range(size)])
    return blocks, places.astype(jnp.int32)


def by_halves(block, axis):
    size = lax.axis_size(axis)
    if size & (size - 1):
        return of_all(block, axis)
    me = lax.axis_index(axis)
    blocks, masks = [block], [0]
    bit = size // 2
    while bit:
        blocks += [swapped(held, axis, bit) for held in blocks]
        masks += [mask ^ bit for mask in masks]
        bit //= 2
    places = jnp.stack([me ^ mask for mask in masks])
    return blocks, places.astype(jnp.int32)


def per_device(spectra, station_mask, owners):
    stations, _, band_bins = spectra.shape
    groups = lax.axis_size("grp")
    shards = lax.axis_size("freq")
    rounds = owners.shape[1]
    pairs = stations * stations
    listed = rounds * pairs
    bin_total = band_bins * shards
    capacity = (2 * pairs + groups - 1) // groups
    lag_band = LAGS // shards
    half_band = lag_band // 2
    chunks = band_bins // LANES
    rows = rounds * groups * capacity

    masked = spectra * station_mask.astype(jnp.float32)[:, None, None]
    tiles = masked.reshape(stations, 2, chunks, LANES).transpose(1, 2, 0, 3)
    tiles = tiles.reshape(2 * chunks * stations, LANES)
    own_owners = owners[0, :, :, 0].reshape(1, listed)
    owner_lists, _ = of_all(own_owners, "grp")
    bands, band_places = of_all(tiles, "freq")
    blocks, group_places = by_halves(jnp.stack(bands), "grp")
    blocks = [block[None] for block in blocks]

    me = lax.axis_index("grp").astype(jnp.int32)
    owner_ids = jnp.concatenate(owner_lists, axis=0)
    owner_ids = jnp.roll(owner_ids[::-1], me + 1, axis=0)
    column_group = jnp.tile(jnp.repeat(group_places, stations), PARTS)[None, :]
    centre = lag_band * (2 * lax.axis_index("freq") + 1) - 1 - LAGS
    turns = jnp.mod(jnp.arange(bin_total, dtype=jnp.int32) * centre, 4 * bin_total)
    angles = turns.astype(jnp.float32) * (math.pi / (2 * bin_total))
    norm = 1.0 / math.sqrt(bin_total)
    twist = jnp.stack([jnp.cos(angles) * norm, jnp.sin(angles) * norm])
    twist = twist.reshape(2, shards, band_bins).transpose(1, 0, 2)
    tables = [jnp.asarray(table) for table in dft_tables(bin_total, half_band)]

    columns = PARTS * groups * stations
    depth = tiles.shape[0]
    out = pl.pallas_call(
        functools.partial(stack_kernel, (groups, stations, rounds, capacity, band_bins)),
        grid_spec=pltpu.PrefetchScalarGridSpec(
            num_scalar_prefetch=2,
            grid=(shards,),
            in_specs=[
                pl.BlockSpec((groups, listed), lambda f, *_: (0, 0)),
                pl.BlockSpec((1, columns), lambda f, *_: (0, 0)),
                pl.BlockSpec((1, 2, band_bins), lambda f, places, _: (places[f], 0, 0)),
            ]
            + [pl.BlockSpec((1, 1, depth, LANES), lambda f, *_: (0, f, 0, 0))] * len(blocks)
            + [pl.BlockSpec((band_bins, half_band), lambda f, places, _: (places[f], 0))] * 4,
            out_specs=pl.BlockSpec((rows, lag_band), lambda f, *_: (0, 0)),
            scratch_shapes=[
                pltpu.VMEM((rows, columns), jnp.bfloat16),
                pltpu.VMEM((rows, columns), jnp.bfloat16),
                pltpu.VMEM((rows, half_band), jnp.float32),
                pltpu.VMEM((rows, half_band), jnp.float32),
            ],
        ),
        out_shape=jax.ShapeDtypeStruct((rows, lag_band), jnp.float32),
        compiler_params=pltpu.CompilerParams(
            dimension_semantics=("arbitrary",), vmem_limit_bytes=56 * 1024 * 1024
        ),
        name="owned_stacks",
    )(band_places, me.reshape(1), owner_ids, column_group, twist, *blocks, *tables)
    return out.reshape(1, rounds, groups, capacity, lag_band)


def solution(mesh):
    placed = (P("grp", None, "freq"), P("grp"), P("grp", None, None, None))
    return jax.shard_map(
        per_device,
        mesh=mesh,
        in_specs=placed,
        out_specs=P("grp", None, None, None, "freq"),
        check_vma=False,
    )
```

```python
import functools
import math

import jax
import jax.numpy as jnp
import numpy as np
from jax import lax
from jax.experimental import pallas as pl
from jax.experimental.pallas import tpu as pltpu
from jax.sharding import PartitionSpec as P

LAGS = 4096
LANES = 128
SUBLANES = 8


def split_bf16(values, parts):
    pieces = []
    for _ in range(parts - 1):
        piece = values.astype(jnp.bfloat16)
        pieces.append(piece)
        values = values - piece.astype(jnp.float32)
    pieces.append(values.astype(jnp.bfloat16))
    return pieces


def dft_tables(bin_total, half_band):
    turns = (np.arange(bin_total)[:, None] * (2 * np.arange(half_band) + 1)[None, :]) % (4 * bin_total)
    angles = turns * (math.pi / (2 * bin_total))
    tables = []
    for exact in (np.cos(angles), np.sin(angles)):
        high = exact.astype(jnp.bfloat16)
        low = (exact - high.astype(np.float64)).astype(jnp.bfloat16)
        tables += [high, low]
    return tables


def iota(shape, axis):
    return lax.broadcasted_iota(jnp.int32, shape, axis)


def dot(left, right):
    return jnp.dot(left, right, preferred_element_type=jnp.float32)


def padded(count, multiple):
    return -(-count // multiple) * multiple


def pick_slots(extras, places, me, stations, rounds, slots):
    groups = len(extras)
    pairs = stations * stations
    listed = rounds * pairs
    rows = rounds * groups * slots
    place = iota((groups, groups), 1)
    held_by = jnp.zeros((groups, groups), jnp.int32)
    for position in range(groups):
        held_by = jnp.where(place == position, places[position], held_by)
    lane = iota((1, listed), 1)

    def by_group(row, shift):
        wanted = (iota((groups, groups), 0) + groups - shift) % groups
        held = jnp.concatenate([extra[row : row + 1, :] for extra in extras], axis=0)
        return dot((held_by == wanted).astype(jnp.bfloat16), held.astype(jnp.bfloat16))

    def of_station(values, number):
        spread = iota((LANES, listed), 0) == number
        return dot(values.astype(jnp.bfloat16), spread.astype(jnp.bfloat16))

    owner_ids = jnp.zeros((groups, listed), jnp.float32)
    partner_mask = jnp.zeros((groups, listed), jnp.float32)
    for index in range(rounds):
        of_round = lane // pairs == index
        owner_ids = jnp.where(of_round, by_group(index, 0), owner_ids)
        second = of_station(by_group(rounds, index + 1), lane % stations)
        partner_mask = jnp.where(of_round, second, partner_mask)
    own_mask = of_station(by_group(rounds, 0), lane % pairs // stations)
    pair_weight = own_mask * partner_mask
    mine = owner_ids == me.astype(jnp.float32)
    from_pair, to_pair = iota((listed, listed), 0), iota((listed, listed), 1)
    before = (from_pair < to_pair) & (from_pair // pairs == to_pair // pairs)
    rank = dot(mine.astype(jnp.bfloat16), before.astype(jnp.bfloat16))
    marked = jnp.where(mine, rank, -1.0).astype(jnp.bfloat16)
    of_group = (iota((rows, groups), 0) // slots) % groups == iota((rows, groups), 1)
    of_group = of_group.astype(jnp.bfloat16)
    row_id, lane_id = iota((rows, listed), 0), iota((rows, listed), 1)
    chosen = (dot(of_group, marked) == (row_id % slots).astype(jnp.float32)) & (
        row_id // (groups * slots) == lane_id // pairs
    )
    weighed = jnp.where(chosen, dot(of_group, pair_weight.astype(jnp.bfloat16)), 0.0)
    chosen = chosen.astype(jnp.bfloat16)
    pair_id = iota((listed, LANES), 0) % pairs
    first = dot(chosen, (pair_id // stations).astype(jnp.bfloat16))
    second = dot(chosen, (pair_id % stations).astype(jnp.bfloat16))
    weight = dot(weighed.astype(jnp.bfloat16), jnp.ones((listed, LANES), jnp.bfloat16))
    return first.astype(jnp.int32), second.astype(jnp.int32), weight


def stack_kernel(sizes, bands_ref, places_ref, me_ref, twist_ref, *refs):
    groups, stations, rounds, slots, band_bins = sizes
    block_refs, refs = refs[:groups], refs[groups:]
    ch_ref, cl_ref, sh_ref, sl_ref, out_ref, first, second, weight, even, odd = refs[:10]
    held, turned, real_high, real_low, imag_high, imag_low = refs[10:]
    step = pl.program_id(0)
    shards = pl.num_programs(0)
    chunks = band_bins // LANES
    depth = 2 * chunks * stations

    @pl.when(step == 0)
    def _():
        extras = [ref[ref.shape[0] - SUBLANES :, :] for ref in block_refs]
        places = [places_ref[position] for position in range(groups)]
        first[...], second[...], weight[...] = pick_slots(
            extras, places, me_ref[0], stations, rounds, slots
        )
        even[...] = jnp.zeros_like(even)
        odd[...] = jnp.zeros_like(odd)

    for position, ref in enumerate(block_refs):
        group = places_ref[position]
        for q in range(chunks):
            lanes = slice(q * LANES, (q + 1) * LANES)
            turn_cos, turn_sin = twist_ref[0, 0:1, lanes], twist_ref[0, 1:2, lanes]
            start = pl.multiple_of(step * depth, depth)
            real = ref[pl.ds(start + q * stations, stations), :]
            imag = ref[pl.ds(start + (chunks + q) * stations, stations), :]
            held[group, q] = real
            held[group, chunks + q] = imag
            turned[group, q] = real * turn_cos + imag * turn_sin
            turned[group, chunks + q] = imag * turn_cos - real * turn_sin

    octets = [
        (group, (group + groups - 1 - index) % groups)
        for index in range(rounds)
        for group in range(groups)
        for _ in range(slots // SUBLANES)
    ]
    for q in range(chunks):
        lanes = slice(q * LANES, (q + 1) * LANES)
        for unit in range(len(octets) // 2):
            reals, imags = [], []
            for octet in (2 * unit, 2 * unit + 1):
                group, partner = octets[octet]
                rows = slice(octet * SUBLANES, (octet + 1) * SUBLANES)
                index_a, index_b = first[rows, :], second[rows, :]
                a_real = jnp.take_along_axis(held[group, q], index_a, axis=0)
                a_imag = jnp.take_along_axis(held[group, chunks + q], index_a, axis=0)
                b_real = jnp.take_along_axis(turned[partner, q], index_b, axis=0)
                b_imag = jnp.take_along_axis(turned[partner, chunks + q], index_b, axis=0)
                reals.append(a_real * b_real + a_imag * b_imag)
                imags.append(a_imag * b_real - a_real * b_imag)
            rows = slice(2 * unit * SUBLANES, 2 * (unit + 1) * SUBLANES)
            high, low = split_bf16(jnp.concatenate(reals, axis=0), 2)
            real_high[rows, lanes] = high
            real_low[rows, lanes] = low
            high, low = split_bf16(jnp.concatenate(imags, axis=0), 2)
            imag_high[rows, lanes] = high
            imag_low[rows, lanes] = low

    def product(high, low, table_high, table_low):
        return dot(high[...], table_high[...]) + (
            dot(high[...], table_low[...]) + dot(low[...], table_high[...])
        )

    even[...] += product(real_high, real_low, ch_ref, cl_ref)
    odd[...] += product(imag_high, imag_low, sh_ref, sl_ref)

    @pl.when(step == shards - 1)
    def _():
        half = even.shape[1]
        row_weight = weight[:, 0:1]
        total = (even[...] + odd[...]) * row_weight
        mirror = (iota((half, half), 0) + iota((half, half), 1) == half - 1).astype(jnp.bfloat16)
        pieces = [dot(piece, mirror) for piece in split_bf16(total, 3)]
        below = pieces[0] + (pieces[1] + pieces[2])
        above = (even[...] - odd[...]) * row_weight
        out_ref[...] = jnp.concatenate([below, above], axis=1)


def swapped(block, axis, mask):
    route = [(i ^ mask, i) for i in range(lax.axis_size(axis))]
    return lax.ppermute(block, axis, route)


def shifted(block, axis, distance):
    size = lax.axis_size(axis)
    return lax.ppermute(block, axis, [((i - distance) % size, i) for i in range(size)])


def of_all(block, axis):
    size = lax.axis_size(axis)
    me = lax.axis_index(axis)
    blocks = [block] + [shifted(block, axis, distance) for distance in range(1, size)]
    places = jnp.stack([(me - distance) % size for distance in range(size)])
    return blocks, places.astype(jnp.int32)


def by_halves(block, axis, join):
    size = lax.axis_size(axis)
    if size & (size - 1):
        return of_all(block, axis)
    me = lax.axis_index(axis)
    blocks, masks = [block], [0]
    bit = size // 2
    while bit:
        blocks += [swapped(held, axis, bit) for held in blocks]
        masks += [mask ^ bit for mask in masks]
        bit //= 2
        if join:
            blocks = [jnp.concatenate(blocks, axis=0)]
    places = jnp.stack([me ^ mask for mask in masks])
    return blocks, places.astype(jnp.int32)


def per_device(spectra, station_mask, owners):
    stations, _, band_bins = spectra.shape
    groups = lax.axis_size("grp")
    shards = lax.axis_size("freq")
    rounds = owners.shape[1]
    pairs = stations * stations
    bin_total = band_bins * shards
    capacity = (2 * pairs + groups - 1) // groups
    slots = padded(capacity, SUBLANES)
    lag_band = LAGS // shards
    half_band = lag_band // 2
    chunks = band_bins // LANES
    rows = rounds * groups * slots

    tiles = spectra.reshape(stations, 2, chunks, LANES).transpose(1, 2, 0, 3)
    tiles = tiles.reshape(2 * chunks * stations, LANES)
    bands, band_places = by_halves(tiles, "freq", True)
    listed = [jnp.pad(owners[0, index, :, 0], (index * pairs, LANES - (index + 1) * pairs)) for index in range(rounds)]
    listed.append(jnp.pad(station_mask, (0, LANES - stations)))
    listed = jnp.stack(listed).astype(jnp.float32)
    listed = jnp.pad(listed, ((0, SUBLANES - listed.shape[0]), (0, 0)))
    blocks, group_places = by_halves(jnp.concatenate(bands + [listed], axis=0), "grp", False)

    me = lax.axis_index("grp").astype(jnp.int32)
    centre = lag_band * (2 * lax.axis_index("freq") + 1) - 1 - LAGS
    turns = jnp.mod(jnp.arange(bin_total, dtype=jnp.int32) * centre, 4 * bin_total)
    angles = turns.astype(jnp.float32) * (math.pi / (2 * bin_total))
    norm = 1.0 / math.sqrt(bin_total)
    twist = jnp.stack([jnp.cos(angles) * norm, jnp.sin(angles) * norm])
    twist = twist.reshape(2, shards, band_bins).transpose(1, 0, 2)
    tables = [jnp.asarray(table) for table in dft_tables(bin_total, half_band)]

    whole = pl.BlockSpec(memory_space=pltpu.VMEM)
    spectrum = pltpu.VMEM((groups, 2 * chunks, stations, LANES), jnp.float32)
    cross = pltpu.VMEM((rows, band_bins), jnp.bfloat16)
    out = pl.pallas_call(
        functools.partial(stack_kernel, (groups, stations, rounds, slots, band_bins)),
        grid_spec=pltpu.PrefetchScalarGridSpec(
            num_scalar_prefetch=3,
            grid=(shards,),
            in_specs=[pl.BlockSpec((1, 2, band_bins), lambda f, places, *_: (places[f], 0, 0))]
            + [whole] * len(blocks)
            + [pl.BlockSpec((band_bins, half_band), lambda f, places, *_: (places[f], 0))] * 4,
            out_specs=pl.BlockSpec((rows, lag_band), lambda f, *_: (0, 0)),
            scratch_shapes=[
                pltpu.VMEM((rows, LANES), jnp.int32),
                pltpu.VMEM((rows, LANES), jnp.int32),
                pltpu.VMEM((rows, LANES), jnp.float32),
                pltpu.VMEM((rows, half_band), jnp.float32),
                pltpu.VMEM((rows, half_band), jnp.float32),
                spectrum,
                spectrum,
                cross,
                cross,
                cross,
                cross,
            ],
        ),
        out_shape=jax.ShapeDtypeStruct((rows, lag_band), jnp.float32),
        compiler_params=pltpu.CompilerParams(
            dimension_semantics=("arbitrary",), vmem_limit_bytes=20 * 1024 * 1024
        ),
        name="owned_stacks",
    )(band_places, group_places, me.reshape(1), twist, *blocks, *tables)
    out = out.reshape(1, rounds, groups, slots, lag_band)
    return out[:, :, :, :capacity]


def solution(mesh):
    placed = (P("grp", None, "freq"), P("grp"), P("grp", None, None, None))
    return jax.shard_map(
        per_device,
        mesh=mesh,
        in_specs=placed,
        out_specs=P("grp", None, None, None, "freq"),
        check_vma=False,
    )
```

```python
import functools
import math

import jax
import jax.numpy as jnp
import numpy as np
from jax import lax
from jax.experimental import pallas as pl
from jax.experimental.pallas import tpu as pltpu
from jax.sharding import PartitionSpec as P

LAGS = 4096
LANES = 128
SUBLANES = 8


def split_bf16(values, parts):
    pieces = []
    for _ in range(parts - 1):
        piece = values.astype(jnp.bfloat16)
        pieces.append(piece)
        values = values - piece.astype(jnp.float32)
    pieces.append(values.astype(jnp.bfloat16))
    return pieces


def base_tables(bin_total, half_band, fine):
    odd = 2 * np.arange(half_band) + 1
    tables = []
    for bins in (np.arange(0, bin_total, fine)[:, None, None], np.arange(fine)[:, None]):
        angles = (bins * odd % (4 * bin_total)) * (math.pi / (2 * bin_total))
        tables += [np.cos(angles).astype(np.float32), np.sin(angles).astype(np.float32)]
    return tables


def iota(shape, axis):
    return lax.broadcasted_iota(jnp.int32, shape, axis)


def dot(left, right):
    return jnp.dot(left, right, preferred_element_type=jnp.float32)


def padded(count, multiple):
    return -(-count // multiple) * multiple


def pick_slots(extras, places, me, stations, rounds, slots):
    groups = len(extras)
    pairs = stations * stations
    listed = rounds * pairs
    rows = rounds * groups * slots
    place = iota((groups, groups), 1)
    held_by = jnp.zeros((groups, groups), jnp.int32)
    for position in range(groups):
        held_by = jnp.where(place == position, places[position], held_by)
    lane = iota((1, listed), 1)

    def by_group(row, shift):
        wanted = (iota((groups, groups), 0) + groups - shift) % groups
        held = jnp.concatenate([extra[row : row + 1, :] for extra in extras], axis=0)
        return dot((held_by == wanted).astype(jnp.bfloat16), held.astype(jnp.bfloat16))

    def of_station(values, number):
        spread = iota((LANES, listed), 0) == number
        return dot(values.astype(jnp.bfloat16), spread.astype(jnp.bfloat16))

    owner_ids = jnp.zeros((groups, listed), jnp.float32)
    partner_mask = jnp.zeros((groups, listed), jnp.float32)
    for index in range(rounds):
        of_round = lane // pairs == index
        owner_ids = jnp.where(of_round, by_group(index, 0), owner_ids)
        second = of_station(by_group(rounds, index + 1), lane % stations)
        partner_mask = jnp.where(of_round, second, partner_mask)
    own_mask = of_station(by_group(rounds, 0), lane % pairs // stations)
    pair_weight = own_mask * partner_mask
    mine = owner_ids == me.astype(jnp.float32)
    from_pair, to_pair = iota((listed, listed), 0), iota((listed, listed), 1)
    before = (from_pair < to_pair) & (from_pair // pairs == to_pair // pairs)
    rank = dot(mine.astype(jnp.bfloat16), before.astype(jnp.bfloat16))
    marked = jnp.where(mine, rank, -1.0).astype(jnp.bfloat16)
    of_group = (iota((rows, groups), 0) // slots) % groups == iota((rows, groups), 1)
    of_group = of_group.astype(jnp.bfloat16)
    row_id, lane_id = iota((rows, listed), 0), iota((rows, listed), 1)
    chosen = (dot(of_group, marked) == (row_id % slots).astype(jnp.float32)) & (
        row_id // (groups * slots) == lane_id // pairs
    )
    weighed = jnp.where(chosen, dot(of_group, pair_weight.astype(jnp.bfloat16)), 0.0)
    chosen = chosen.astype(jnp.bfloat16)
    pair_id = iota((listed, LANES), 0) % pairs
    first = dot(chosen, (pair_id // stations).astype(jnp.bfloat16))
    second = dot(chosen, (pair_id % stations).astype(jnp.bfloat16))
    weight = dot(weighed.astype(jnp.bfloat16), jnp.ones((listed, LANES), jnp.bfloat16))
    return first.astype(jnp.int32), second.astype(jnp.int32), weight


def table_kernel(me_ref, far_cos, far_sin, near_cos, near_sin, *refs):
    cos_high, cos_low, sin_high, sin_low, turn_cos, turn_sin = refs
    fine = near_cos.shape[0]
    shards, _, band_bins = turn_cos.shape
    bin_total = shards * band_bins

    @pl.loop(0, far_cos.shape[0])
    def _(index):
        rows = pl.ds(pl.multiple_of(index * fine, fine), fine)
        cos, sin = far_cos[index], far_sin[index]
        cos_high[rows, :], cos_low[rows, :] = split_bf16(
            cos * near_cos[...] - sin * near_sin[...], 2
        )
        sin_high[rows, :], sin_low[rows, :] = split_bf16(
            sin * near_cos[...] + cos * near_sin[...], 2
        )

    lag_band = 2 * near_cos.shape[1]
    centre = lag_band * (2 * me_ref[1] + 1) - 1 - LAGS
    bins = iota((shards, band_bins), 0) * band_bins + iota((shards, band_bins), 1)
    turns = (bins * centre) & (4 * bin_total - 1)
    angles = turns.astype(jnp.float32) * (math.pi / (2 * bin_total))
    norm = 1.0 / math.sqrt(bin_total)
    cos, sin = jnp.cos(angles) * norm, jnp.sin(angles) * norm
    for shard in range(shards):
        turn_cos[shard] = cos[shard : shard + 1, :]
        turn_sin[shard] = sin[shard : shard + 1, :]


def add_bands(sizes, bands_ref, places, turn_refs, table_refs, block_refs, picks, sums, scratch):
    groups, stations, rounds, slots, band_bins, band_count = sizes
    turn_cos_ref, turn_sin_ref = turn_refs
    cos_high, cos_low, sin_high, sin_low = table_refs
    first, second = picks
    even, odd = sums
    held, turned, real_high, real_low, imag_high, imag_low = scratch
    chunks = band_bins // LANES
    depth = 2 * chunks * stations
    octets = [
        (group, (group + groups - 1 - index) % groups)
        for index in range(rounds)
        for group in range(groups)
        for _ in range(slots // SUBLANES)
    ]

    @pl.loop(0, band_count)
    def _(step):
        band = bands_ref[step]
        for position, ref in enumerate(block_refs):
            group = places[position]
            for q in range(chunks):
                lanes = slice(q * LANES, (q + 1) * LANES)
                turn_cos = turn_cos_ref[band, :, lanes]
                turn_sin = turn_sin_ref[band, :, lanes]
                start = pl.multiple_of(step * depth, depth)
                real = ref[pl.ds(start + q * stations, stations), :]
                imag = ref[pl.ds(start + (chunks + q) * stations, stations), :]
                held[group, q] = real
                held[group, chunks + q] = imag
                turned[group, q] = real * turn_cos + imag * turn_sin
                turned[group, chunks + q] = imag * turn_cos - real * turn_sin

        for q in range(chunks):
            lanes = slice(q * LANES, (q + 1) * LANES)
            for unit in range(len(octets) // 2):
                reals, imags = [], []
                for octet in (2 * unit, 2 * unit + 1):
                    group, partner = octets[octet]
                    rows = slice(octet * SUBLANES, (octet + 1) * SUBLANES)
                    index_a, index_b = first[rows, :], second[rows, :]
                    a_real = jnp.take_along_axis(held[group, q], index_a, axis=0)
                    a_imag = jnp.take_along_axis(held[group, chunks + q], index_a, axis=0)
                    b_real = jnp.take_along_axis(turned[partner, q], index_b, axis=0)
                    b_imag = jnp.take_along_axis(turned[partner, chunks + q], index_b, axis=0)
                    reals.append(a_real * b_real + a_imag * b_imag)
                    imags.append(a_imag * b_real - a_real * b_imag)
                rows = slice(2 * unit * SUBLANES, 2 * (unit + 1) * SUBLANES)
                high, low = split_bf16(jnp.concatenate(reals, axis=0), 2)
                real_high[rows, lanes] = high
                real_low[rows, lanes] = low
                high, low = split_bf16(jnp.concatenate(imags, axis=0), 2)
                imag_high[rows, lanes] = high
                imag_low[rows, lanes] = low

        rows = pl.ds(pl.multiple_of(band * band_bins, band_bins), band_bins)

        def product(high, low, table_high, table_low):
            return dot(high[...], table_high[rows, :]) + (
                dot(high[...], table_low[rows, :]) + dot(low[...], table_high[rows, :])
            )

        even[...] += product(real_high, real_low, cos_high, cos_low)
        odd[...] += product(imag_high, imag_low, sin_high, sin_low)


def first_kernel(sizes, moves, bands_ref, me_ref, *refs):
    groups, stations, rounds, slots = sizes[:4]
    turn_refs, table_refs, refs = refs[:2], refs[2:6], refs[6:]
    block_refs, refs = refs[:groups], refs[groups:]
    (first, second, weight, even, odd), scratch = refs[:5], refs[5:]
    places = [moved(me_ref[0], move, groups) for move in moves]
    extras = [ref[ref.shape[0] - SUBLANES :, :] for ref in block_refs]
    first[...], second[...], weight[...] = pick_slots(
        extras, places, me_ref[0], stations, rounds, slots
    )
    even[...] = jnp.zeros_like(even)
    odd[...] = jnp.zeros_like(odd)
    add_bands(
        sizes, bands_ref, places, turn_refs, table_refs, block_refs,
        (first, second), (even, odd), scratch,
    )


def last_kernel(sizes, moves, bands_ref, me_ref, *refs):
    groups = sizes[0]
    turn_refs, table_refs, refs = refs[:2], refs[2:6], refs[6:]
    block_refs, refs = refs[:groups], refs[groups:]
    (first, second, weight, even_in, odd_in, out_ref, even, odd), scratch = refs[:8], refs[8:]
    even[...] = even_in[...]
    odd[...] = odd_in[...]
    places = [moved(me_ref[0], move, groups) for move in moves]
    add_bands(
        sizes, bands_ref, places, turn_refs, table_refs, block_refs,
        (first, second), (even, odd), scratch,
    )
    half = even.shape[1]
    row_weight = weight[:, 0:1]
    total = (even[...] + odd[...]) * row_weight
    mirror = (iota((half, half), 0) + iota((half, half), 1) == half - 1).astype(jnp.bfloat16)
    pieces = [dot(piece, mirror) for piece in split_bf16(total, 3)]
    below = pieces[0] + (pieces[1] + pieces[2])
    above = (even[...] - odd[...]) * row_weight
    out_ref[...] = jnp.concatenate([below, above], axis=1)


def moved(me, move, size):
    return me ^ move if size & (size - 1) == 0 else lax.rem(me + size - move, size)


def fetched(block, axis, move):
    size = lax.axis_size(axis)
    return lax.ppermute(block, axis, [(moved_index(i, move, size), i) for i in range(size)])


def moved_index(i, move, size):
    return i ^ move if size & (size - 1) == 0 else (i - move) % size


def gathered(block, axis, bits):
    size = lax.axis_size(axis)
    if size & (size - 1):
        moves = list(range(size))
        return [block] + [fetched(block, axis, move) for move in moves[1:]], moves
    blocks, moves = [block], [0]
    for bit in bits:
        blocks += [fetched(held, axis, bit) for held in blocks]
        moves += [move ^ bit for move in moves]
    return blocks, moves


def exchange(tiles, extras):
    groups, shards = lax.axis_size("grp"), lax.axis_size("freq")
    half = shards // 2
    own, band_moves = tiles, [0]
    bit = half
    while bit > 1:
        own = jnp.concatenate([own, fetched(own, "freq", bit)], axis=0)
        band_moves += [move ^ bit for move in band_moves]
        bit //= 2
    with_extras = jnp.concatenate([own, extras], axis=0)
    beside = fetched(own, "freq", 1)
    if groups != 4:
        near, group_moves = gathered(with_extras, "grp", [])
        far, _ = gathered(beside, "grp", [])
        return near, far, band_moves, group_moves
    rows = own.shape[0]
    across = fetched(with_extras, "grp", 2)
    near = [with_extras, across, fetched(with_extras, "grp", 1), fetched(across, "grp", 1)]
    upper = fetched(beside[: rows // 2], "grp", 2)
    lower = fetched(across[rows // 2 : rows], "freq", 1)
    diagonal = jnp.concatenate([upper, lower], axis=0)
    far = [beside, diagonal, fetched(beside, "grp", 1), fetched(diagonal, "grp", 1)]
    return near, far, band_moves, [0, 2, 1, 3]


def per_device(spectra, station_mask, owners):
    stations, _, band_bins = spectra.shape
    groups = lax.axis_size("grp")
    shards = lax.axis_size("freq")
    rounds = owners.shape[1]
    pairs = stations * stations
    bin_total = band_bins * shards
    capacity = (2 * pairs + groups - 1) // groups
    slots = padded(capacity, SUBLANES)
    lag_band = LAGS // shards
    half_band = lag_band // 2
    chunks = band_bins // LANES
    rows = rounds * groups * slots

    tiles = spectra.reshape(stations, 2, chunks, LANES).transpose(1, 2, 0, 3)
    tiles = tiles.reshape(2 * chunks * stations, LANES)
    listed = [
        jnp.pad(owners[0, index, :, 0], (index * pairs, LANES - (index + 1) * pairs))
        for index in range(rounds)
    ]
    listed.append(jnp.pad(station_mask, (0, LANES - stations)))
    listed = jnp.stack(listed).astype(jnp.float32)
    extras = jnp.pad(listed, ((0, SUBLANES - listed.shape[0]), (0, 0)))
    near, far, band_moves, group_moves = exchange(tiles, extras)

    me = jnp.stack([lax.axis_index("grp"), lax.axis_index("freq")]).astype(jnp.int32)
    near_bands = me[1] ^ jnp.asarray(band_moves, jnp.int32)
    far_bands = near_bands ^ 1

    scalar = pl.BlockSpec(memory_space=pltpu.SMEM)
    vector = pl.BlockSpec(memory_space=pltpu.VMEM)

    def in_vmem(shape, kind):
        return pltpu.VMEM(shape, kind)

    def call(kernel, name, scalars, arrays, out_shape, scratch, cost):
        arrays = [pltpu.with_memory_space_constraint(array, pltpu.VMEM) for array in arrays]
        return pl.pallas_call(
            kernel,
            out_shape=out_shape,
            in_specs=[scalar] * len(scalars) + [vector] * len(arrays),
            out_specs=[vector] * len(out_shape),
            scratch_shapes=scratch,
            compiler_params=pltpu.CompilerParams(vmem_limit_bytes=16 * 1024 * 1024),
            cost_estimate=cost,
            name=name,
        )(*scalars, *arrays)

    table = in_vmem((bin_total, half_band), jnp.bfloat16)
    turn = in_vmem((shards, 1, band_bins), jnp.float32)
    tables = call(
        table_kernel,
        "tables",
        [me],
        [jnp.asarray(base) for base in base_tables(bin_total, half_band, 64)],
        [table] * 4 + [turn] * 2,
        [],
        pl.CostEstimate(flops=0, bytes_accessed=8 * bin_total * half_band, transcendentals=0),
    )
    turns, tables = tables[4:], tables[:4]

    sizes = (groups, stations, rounds, slots, band_bins, len(band_moves))
    spectrum = pltpu.VMEM((groups, 2 * chunks, stations, LANES), jnp.float32)
    cross = pltpu.VMEM((rows, band_bins), jnp.bfloat16)
    scratch = [spectrum] * 2 + [cross] * 4
    flops = 6 * rows * bin_total * lag_band // 2
    cost = pl.CostEstimate(flops=flops, bytes_accessed=8 * 1024 * 1024, transcendentals=0)
    picks = [in_vmem((rows, LANES), kind) for kind in (jnp.int32, jnp.int32, jnp.float32)]
    total = in_vmem((rows, half_band), jnp.float32)
    held = call(
        functools.partial(first_kernel, sizes, group_moves),
        "near_bands",
        [near_bands, me],
        [*turns, *tables, *near],
        picks + [total] * 2,
        scratch,
        cost,
    )
    (out,) = call(
        functools.partial(last_kernel, sizes, group_moves),
        "far_bands",
        [far_bands, me],
        [*turns, *tables, *far, *held],
        [in_vmem((rows, lag_band), jnp.float32)],
        [pltpu.VMEM((rows, half_band), jnp.float32)] * 2 + scratch,
        cost,
    )
    out = out.reshape(1, rounds, groups, slots, lag_band)
    return out[:, :, :, :capacity]


def solution(mesh):
    placed = (P("grp", None, "freq"), P("grp"), P("grp", None, None, None))
    return jax.shard_map(
        per_device,
        mesh=mesh,
        in_specs=placed,
        out_specs=P("grp", None, None, None, "freq"),
        check_vma=False,
    )
```

```python
import functools
import math

import jax
import jax.numpy as jnp
from jax import lax
from jax.experimental import pallas as pl
from jax.experimental.pallas import tpu as pltpu
from jax.sharding import PartitionSpec as P

LAGS = 4096
LANES = 128
SUBLANES = 8


def split_bf16(values, parts):
    pieces = []
    for _ in range(parts - 1):
        piece = values.astype(jnp.bfloat16)
        pieces.append(piece)
        values = values - piece.astype(jnp.float32)
    pieces.append(values.astype(jnp.bfloat16))
    return pieces


def iota(shape, axis):
    return lax.broadcasted_iota(jnp.int32, shape, axis)


def dot(left, right):
    return jnp.dot(left, right, preferred_element_type=jnp.float32)


def padded(count, multiple):
    return -(-count // multiple) * multiple


def pick_slots(extras, places, me, stations, rounds, slots):
    groups = len(extras)
    pairs = stations * stations
    listed = rounds * pairs
    rows = rounds * groups * slots
    place = iota((groups, groups), 1)
    held_by = jnp.zeros((groups, groups), jnp.int32)
    for position in range(groups):
        held_by = jnp.where(place == position, places[position], held_by)
    lane = iota((1, listed), 1)

    def by_group(row, shift):
        wanted = (iota((groups, groups), 0) + groups - shift) % groups
        held = jnp.concatenate([extra[row : row + 1, :] for extra in extras], axis=0)
        return dot((held_by == wanted).astype(jnp.bfloat16), held.astype(jnp.bfloat16))

    def of_station(values, number):
        spread = iota((LANES, listed), 0) == number
        return dot(values.astype(jnp.bfloat16), spread.astype(jnp.bfloat16))

    owner_ids = jnp.zeros((groups, listed), jnp.float32)
    partner_mask = jnp.zeros((groups, listed), jnp.float32)
    for index in range(rounds):
        of_round = lane // pairs == index
        owner_ids = jnp.where(of_round, by_group(index, 0), owner_ids)
        second = of_station(by_group(rounds, index + 1), lane % stations)
        partner_mask = jnp.where(of_round, second, partner_mask)
    own_mask = of_station(by_group(rounds, 0), lane % pairs // stations)
    pair_weight = own_mask * partner_mask
    mine = owner_ids == me.astype(jnp.float32)
    from_pair, to_pair = iota((listed, listed), 0), iota((listed, listed), 1)
    before = (from_pair < to_pair) & (from_pair // pairs == to_pair // pairs)
    rank = dot(mine.astype(jnp.bfloat16), before.astype(jnp.bfloat16))
    marked = jnp.where(mine, rank, -1.0).astype(jnp.bfloat16)
    of_group = (iota((rows, groups), 0) // slots) % groups == iota((rows, groups), 1)
    of_group = of_group.astype(jnp.bfloat16)
    row_id, lane_id = iota((rows, listed), 0), iota((rows, listed), 1)
    chosen = (dot(of_group, marked) == (row_id % slots).astype(jnp.float32)) & (
        row_id // (groups * slots) == lane_id // pairs
    )
    weighed = jnp.where(chosen, dot(of_group, pair_weight.astype(jnp.bfloat16)), 0.0)
    weight = dot(weighed.astype(jnp.bfloat16), jnp.ones((listed, LANES), jnp.bfloat16))
    is_first = iota((SUBLANES, listed), 0) == 0
    pair_id = iota((SUBLANES, listed), 1) % pairs
    number = jnp.where(is_first, pair_id // stations, pair_id % stations).astype(jnp.bfloat16)
    picked = lax.dot_general(
        number, chosen.astype(jnp.bfloat16), (((1,), (1,)), ((), ())),
        preferred_element_type=jnp.float32,
    )
    slot_id = iota((SUBLANES, rows), 1)
    group = (slot_id // slots) % groups
    partner = (group + groups - 1 - slot_id // (groups * slots)) % groups
    group = jnp.where(iota((SUBLANES, rows), 0) == 0, group, partner)
    return picked.astype(jnp.int32) + group * stations, weight


def table_kernel(me_ref, owners_ref, mask_ref, *refs):
    cos_high, cos_low, sin_high, sin_low, turn_cos, turn_sin, extras = refs[:7]
    near_cos, near_sin, far_cos, far_sin = refs[7:]
    bin_total, half_band = cos_high.shape
    shards, chunks, _ = turn_cos.shape
    fine = near_cos.shape[0]
    coarse = fine * SUBLANES

    extras[...] = jnp.zeros_like(extras)
    rounds, pairs = owners_ref.shape[1], owners_ref.shape[3]
    for index in range(rounds):
        lanes = slice(index * pairs, (index + 1) * pairs)
        extras[index : index + 1, lanes] = owners_ref[0, index].astype(jnp.float32)
    extras[rounds : rounds + 1, : mask_ref.shape[1]] = mask_ref[...].astype(jnp.float32)

    def circle(turns):
        angles = (turns & (4 * bin_total - 1)).astype(jnp.float32) * (math.pi / (2 * bin_total))
        return jnp.cos(angles), jnp.sin(angles)

    def eight(count, step):
        return circle(iota((count, half_band), 0) * step * (2 * iota((count, half_band), 1) + 1))

    def added(cos, sin, other_cos, other_sin):
        return cos * other_cos - sin * other_sin, sin * other_cos + cos * other_sin

    low_cos, low_sin = eight(SUBLANES, 1)
    high_cos, high_sin = eight(fine // SUBLANES, SUBLANES)
    for index in range(fine // SUBLANES):
        rows, one = slice(index * SUBLANES, (index + 1) * SUBLANES), slice(index, index + 1)
        near_cos[rows, :], near_sin[rows, :] = added(
            high_cos[one], high_sin[one], low_cos, low_sin
        )
    mid_cos, mid_sin = eight(SUBLANES, fine)
    top_cos, top_sin = eight(bin_total // coarse, coarse)
    for index in range(bin_total // coarse):
        far_cos[index] = top_cos[index : index + 1]
        far_sin[index] = top_sin[index : index + 1]

    @pl.loop(0, bin_total // coarse)
    def _(index):
        cos, sin = added(far_cos[index], far_sin[index], mid_cos, mid_sin)
        for part in range(SUBLANES):
            rows = pl.ds(pl.multiple_of(index * coarse, coarse) + part * fine, fine)
            one = slice(part, part + 1)
            cosines, sines = added(cos[one], sin[one], near_cos[...], near_sin[...])
            cos_high[rows, :], cos_low[rows, :] = split_bf16(cosines, 2)
            sin_high[rows, :], sin_low[rows, :] = split_bf16(sines, 2)

    centre = 2 * half_band * (2 * me_ref[1] + 1) - 1 - LAGS
    bins = iota((shards * chunks, LANES), 0) * LANES + iota((shards * chunks, LANES), 1)
    norm = 1.0 / math.sqrt(bin_total)
    cos, sin = circle(bins * centre)
    for shard in range(shards):
        rows = slice(shard * chunks, (shard + 1) * chunks)
        turn_cos[shard] = cos[rows] * norm
        turn_sin[shard] = sin[rows] * norm


def add_bands(sizes, bands_ref, places, turn_refs, table_refs, block_refs, pick, sums, scratch):
    groups, stations, rounds, slots, band_bins, band_count = sizes
    cos_high, cos_low, sin_high, sin_low = table_refs
    even, odd = sums
    chunks = band_bins // LANES
    depth = 2 * chunks * stations
    rows = rounds * groups * slots
    per_tile = SUBLANES // chunks
    tiles = band_count // per_tile
    width = min(chunks, 2)
    parts = SUBLANES // width
    sets = [scratch[8 * tile : 8 * (tile + 1)] for tile in range(2)]

    def prepare(tile):
        held_real, held_imag, turned_real, turned_imag, cos, sin = sets[tile % 2][:6]
        for index in range(per_tile):
            step = tile * per_tile + index
            lines = slice(index * chunks, (index + 1) * chunks)
            cos[lines, :] = turn_refs[0][bands_ref[step]]
            sin[lines, :] = turn_refs[1][bands_ref[step]]
            for position, ref in enumerate(block_refs):
                for station in range(stations):
                    place = places[position] * stations + station
                    start = step * depth + station * 2 * chunks
                    held_real[place, lines, :] = ref[start : start + chunks, :]
                    held_imag[place, lines, :] = ref[start + chunks : start + 2 * chunks, :]
        for place in range(groups * stations):
            real, imag = held_real[place], held_imag[place]
            turned_real[place] = real * cos[...] + imag * sin[...]
            turned_imag[place] = imag * cos[...] - real * sin[...]

    def multiply(tile, part):
        held_real, held_imag, turned_real, turned_imag, _, _, cross_real, cross_imag = sets[tile % 2]
        for slot in range(part * rows // parts, (part + 1) * rows // parts):
            first, second = pick[0, slot], pick[1, slot]
            a_real, a_imag = held_real[first], held_imag[first]
            b_real, b_imag = turned_real[second], turned_imag[second]
            lines = slice(slot * SUBLANES, (slot + 1) * SUBLANES)
            cross_real[lines, :] = a_real * b_real + a_imag * b_imag
            cross_imag[lines, :] = a_imag * b_real - a_real * b_imag

    def transform(tile, part):
        line = part * width
        band = bands_ref[tile * per_tile + line // chunks]
        start = pl.multiple_of(band * band_bins + line % chunks * LANES, LANES)
        bins = pl.ds(start, width * LANES)

        def product(ref, table_high, table_low):
            cross = jnp.concatenate(
                [ref[pl.ds(line + index, rows, stride=SUBLANES), :] for index in range(width)],
                axis=1,
            )
            high, low = split_bf16(cross, 2)
            table = table_high[bins, :]
            return dot(
                jnp.concatenate([high, high, low], axis=1),
                jnp.concatenate([table, table_low[bins, :], table], axis=0),
            )

        cross_real, cross_imag = sets[tile % 2][6:]
        even[...] += product(cross_real, cos_high, cos_low)
        odd[...] += product(cross_imag, sin_high, sin_low)

    prepare(0)
    for part in range(parts):
        multiply(0, part)
    for tile in range(tiles):
        if tile + 1 < tiles:
            prepare(tile + 1)
        for part in range(parts):
            if tile + 1 < tiles:
                multiply(tile + 1, part)
            transform(tile, part)


def near_kernel(sizes, moves, bands_ref, me_ref, *refs):
    groups, stations, rounds, slots = sizes[:4]
    turn_refs, table_refs, refs = refs[:2], refs[2:6], refs[6:]
    block_refs, refs = refs[:groups], refs[groups:]
    (pick_out, weight, even, odd, pick, sem), scratch = refs[:6], refs[6:]
    places = [moved(me_ref[0], move, groups) for move in moves]
    extras = [ref[ref.shape[0] - SUBLANES :, :] for ref in block_refs]
    pick_out[...], weight[...] = pick_slots(extras, places, me_ref[0], stations, rounds, slots)
    copy = pltpu.make_async_copy(pick_out, pick, sem)
    copy.start()
    even[...] = jnp.zeros_like(even)
    odd[...] = jnp.zeros_like(odd)
    copy.wait()
    add_bands(
        sizes, bands_ref, places, turn_refs, table_refs, block_refs, pick, (even, odd), scratch
    )


def far_kernel(sizes, moves, bands_ref, me_ref, *refs):
    groups = sizes[0]
    turn_refs, table_refs, refs = refs[:2], refs[2:6], refs[6:]
    block_refs, refs = refs[:groups], refs[groups:]
    pick_in, weight, even_in, odd_in, out_ref, pick, sem, even, odd, result, out_sem = refs[:11]
    copy = pltpu.make_async_copy(pick_in, pick, sem)
    copy.start()
    even[...] = even_in[...]
    odd[...] = odd_in[...]
    places = [moved(me_ref[0], move, groups) for move in moves]
    copy.wait()
    add_bands(
        sizes, bands_ref, places, turn_refs, table_refs, block_refs, pick, (even, odd), refs[11:]
    )
    half = even.shape[1]
    row_weight = weight[:, 0:1]
    result[:, half:] = (even[...] - odd[...]) * row_weight
    total = (even[...] + odd[...]) * row_weight
    mirror = (iota((half, half), 0) + iota((half, half), 1) == half - 1).astype(jnp.bfloat16)
    pieces = [dot(piece, mirror) for piece in split_bf16(total, 3)]
    result[:, :half] = pieces[0] + (pieces[1] + pieces[2])
    copy = pltpu.make_async_copy(result, out_ref, out_sem)
    copy.start()
    copy.wait()


def moved(me, move, size):
    return me ^ move if size & (size - 1) == 0 else lax.rem(me + size - move, size)


def moved_index(me, move, size):
    return me ^ move if size & (size - 1) == 0 else (me - move) % size


def fetched(block, group_move, band_move):
    groups, shards = lax.axis_size("grp"), lax.axis_size("freq")
    route = [
        (
            moved_index(group, group_move, groups) * shards + moved_index(band, band_move, shards),
            group * shards + band,
        )
        for group in range(groups)
        for band in range(shards)
    ]
    return lax.ppermute(block, ("grp", "freq"), route)


def per_device(spectra, station_mask, owners):
    stations, _, band_bins = spectra.shape
    groups = lax.axis_size("grp")
    shards = lax.axis_size("freq")
    rounds = owners.shape[1]
    pairs = stations * stations
    bin_total = band_bins * shards
    capacity = (2 * pairs + groups - 1) // groups
    slots = padded(capacity, SUBLANES)
    lag_band = LAGS // shards
    half_band = lag_band // 2
    chunks = band_bins // LANES
    rows = rounds * groups * slots

    scalar = pl.BlockSpec(memory_space=pltpu.SMEM)
    vector = pl.BlockSpec(memory_space=pltpu.VMEM)

    def call(kernel, name, scalars, arrays, out_shape, scratch, cost):
        arrays = [pltpu.with_memory_space_constraint(array, pltpu.VMEM) for array in arrays]
        in_hbm = isinstance(out_shape, jax.ShapeDtypeStruct)
        return pl.pallas_call(
            kernel,
            out_shape=out_shape,
            in_specs=[scalar] * len(scalars) + [vector] * len(arrays),
            out_specs=pl.BlockSpec(memory_space=pl.ANY) if in_hbm else [vector] * len(out_shape),
            scratch_shapes=scratch,
            compiler_params=pltpu.CompilerParams(vmem_limit_bytes=24 * 1024 * 1024),
            cost_estimate=cost,
            name=name,
        )(*scalars, *arrays)

    tiles = spectra.reshape(2 * chunks * stations, LANES)
    moves = range(2, shards, 2)
    column = [tiles] + [fetched(tiles, 0, move) for move in moves]
    me = jnp.stack([lax.axis_index("grp"), lax.axis_index("freq")]).astype(jnp.int32)
    table = pltpu.VMEM((bin_total, half_band), jnp.bfloat16)
    turn = pltpu.VMEM((shards, chunks, LANES), jnp.float32)
    base = pltpu.VMEM((64, half_band), jnp.float32)
    far_base = pltpu.VMEM((bin_total // (64 * SUBLANES), 1, half_band), jnp.float32)
    *tables, turn_cos, turn_sin, extras = call(
        table_kernel,
        "tables",
        [me],
        [owners.transpose(0, 1, 3, 2), station_mask.reshape(1, stations)],
        [table] * 4 + [turn] * 2 + [pltpu.VMEM((SUBLANES, LANES), jnp.float32)],
        [base] * 2 + [far_base] * 2,
        pl.CostEstimate(flops=0, bytes_accessed=8 * bin_total * half_band, transcendentals=0),
    )
    column = jnp.concatenate(column + [extras], axis=0)
    near = [column] + [fetched(column, move, 0) for move in range(1, groups)]
    far = [fetched(column, move, 1) for move in range(groups)]

    near_bands = me[1] ^ jnp.arange(0, shards, 2, dtype=jnp.int32)
    far_bands = near_bands ^ 1
    sizes = (groups, stations, rounds, slots, band_bins, shards // 2)
    spectrum = pltpu.VMEM((groups * stations, SUBLANES, LANES), jnp.float32)
    turn_tile = pltpu.VMEM((SUBLANES, LANES), jnp.float32)
    cross = pltpu.VMEM((rows * SUBLANES, LANES), jnp.float32)
    scratch = ([spectrum] * 4 + [turn_tile] * 2 + [cross] * 2) * 2
    flops = 6 * rows * bin_total * lag_band // 2
    cost = pl.CostEstimate(flops=flops, bytes_accessed=8 * 1024 * 1024, transcendentals=0)
    total = pltpu.VMEM((rows, half_band), jnp.float32)
    pick_in_smem = [pltpu.SMEM((SUBLANES, rows), jnp.int32), pltpu.SemaphoreType.DMA]
    held = call(
        functools.partial(near_kernel, sizes, range(groups)),
        "near_bands",
        [near_bands, me],
        [turn_cos, turn_sin, *tables, *near],
        [pltpu.VMEM((SUBLANES, rows), jnp.int32), pltpu.VMEM((rows, LANES), jnp.float32)]
        + [total] * 2,
        pick_in_smem + scratch,
        cost,
    )
    out = call(
        functools.partial(far_kernel, sizes, range(groups)),
        "far_bands",
        [far_bands, me],
        [turn_cos, turn_sin, *tables, *far, *held],
        jax.ShapeDtypeStruct((rows, lag_band), jnp.float32),
        pick_in_smem
        + [total] * 2
        + [pltpu.VMEM((rows, lag_band), jnp.float32), pltpu.SemaphoreType.DMA]
        + scratch,
        cost,
    )
    out = out.reshape(1, rounds, groups, slots, lag_band)
    return out[:, :, :, :capacity]


def solution(mesh):
    placed = (P("grp", None, "freq"), P("grp"), P("grp", None, None, None))
    return jax.shard_map(
        per_device,
        mesh=mesh,
        in_specs=placed,
        out_specs=P("grp", None, None, None, "freq"),
        check_vma=False,
    )
```

```python
import functools
import math

import jax
import jax.numpy as jnp
from jax import lax
from jax.experimental import pallas as pl
from jax.experimental.pallas import tpu as pltpu
from jax.sharding import PartitionSpec as P

LAGS = 4096
LANES = 128
SUBLANES = 8


def split_bf16(values, parts):
    pieces = []
    for _ in range(parts - 1):
        piece = values.astype(jnp.bfloat16)
        pieces.append(piece)
        values = values - piece.astype(jnp.float32)
    pieces.append(values.astype(jnp.bfloat16))
    return pieces


def iota(shape, axis):
    return lax.broadcasted_iota(jnp.int32, shape, axis)


def dot(left, right):
    return jnp.dot(left, right, preferred_element_type=jnp.float32)


def padded(count, multiple):
    return -(-count // multiple) * multiple


def pick_slots(extras, places, me, stations, rounds, slots):
    groups = len(extras)
    pairs = stations * stations
    listed = rounds * pairs
    rows = rounds * groups * slots
    place = iota((groups, groups), 1)
    held_by = jnp.zeros((groups, groups), jnp.int32)
    for position in range(groups):
        held_by = jnp.where(place == position, places[position], held_by)
    lane = iota((1, listed), 1)

    def by_group(row, shift):
        wanted = (iota((groups, groups), 0) + groups - shift) % groups
        held = jnp.concatenate([extra[row : row + 1, :] for extra in extras], axis=0)
        return dot((held_by == wanted).astype(jnp.bfloat16), held.astype(jnp.bfloat16))

    def of_station(values, number):
        spread = iota((LANES, listed), 0) == number
        return dot(values.astype(jnp.bfloat16), spread.astype(jnp.bfloat16))

    owner_ids = jnp.zeros((groups, listed), jnp.float32)
    partner_mask = jnp.zeros((groups, listed), jnp.float32)
    for index in range(rounds):
        of_round = lane // pairs == index
        owner_ids = jnp.where(of_round, by_group(index, 0), owner_ids)
        second = of_station(by_group(rounds, index + 1), lane % stations)
        partner_mask = jnp.where(of_round, second, partner_mask)
    own_mask = of_station(by_group(rounds, 0), lane % pairs // stations)
    pair_weight = own_mask * partner_mask
    mine = owner_ids == me.astype(jnp.float32)
    from_pair, to_pair = iota((listed, listed), 0), iota((listed, listed), 1)
    before = (from_pair < to_pair) & (from_pair // pairs == to_pair // pairs)
    rank = dot(mine.astype(jnp.bfloat16), before.astype(jnp.bfloat16))
    marked = jnp.where(mine, rank, -1.0).astype(jnp.bfloat16)
    of_group = (iota((rows, groups), 0) // slots) % groups == iota((rows, groups), 1)
    of_group = of_group.astype(jnp.bfloat16)
    row_id, lane_id = iota((rows, listed), 0), iota((rows, listed), 1)
    chosen = (dot(of_group, marked) == (row_id % slots).astype(jnp.float32)) & (
        row_id // (groups * slots) == lane_id // pairs
    )
    weighed = jnp.where(chosen, dot(of_group, pair_weight.astype(jnp.bfloat16)), 0.0)
    weight = dot(weighed.astype(jnp.bfloat16), jnp.ones((listed, LANES), jnp.bfloat16))
    is_first = iota((SUBLANES, listed), 0) == 0
    pair_id = iota((SUBLANES, listed), 1) % pairs
    number = jnp.where(is_first, pair_id // stations, pair_id % stations).astype(jnp.bfloat16)
    picked = lax.dot_general(
        number, chosen.astype(jnp.bfloat16), (((1,), (1,)), ((), ())),
        preferred_element_type=jnp.float32,
    )
    slot_id = iota((SUBLANES, rows), 1)
    group = (slot_id // slots) % groups
    partner = (group + groups - 1 - slot_id // (groups * slots)) % groups
    group = jnp.where(iota((SUBLANES, rows), 0) == 0, group, partner)
    return picked.astype(jnp.int32) + group * stations, weight


def table_kernel(me_ref, owners_hbm, mask_hbm, *refs):
    cos_table, sin_table, turn_cos, turn_sin, extras = refs[:5]
    near_cos, near_sin, far_cos, far_sin, owners_ref, mask_ref, sems = refs[5:]
    bin_total, half_band = cos_table.shape[0], cos_table.shape[1] // 2
    copies = [
        pltpu.make_async_copy(owners_hbm, owners_ref, sems.at[0]),
        pltpu.make_async_copy(mask_hbm, mask_ref, sems.at[1]),
    ]
    for copy in copies:
        copy.start()
    shards, chunks, _ = turn_cos.shape
    fine = near_cos.shape[0]
    coarse = fine * SUBLANES

    def circle(turns):
        angles = (turns & (4 * bin_total - 1)).astype(jnp.float32) * (math.pi / (2 * bin_total))
        return jnp.cos(angles), jnp.sin(angles)

    def eight(count, step):
        return circle(iota((count, half_band), 0) * step * (2 * iota((count, half_band), 1) + 1))

    def added(cos, sin, other_cos, other_sin):
        return cos * other_cos - sin * other_sin, sin * other_cos + cos * other_sin

    low_cos, low_sin = eight(SUBLANES, 1)
    high_cos, high_sin = eight(fine // SUBLANES, SUBLANES)
    for index in range(fine // SUBLANES):
        rows, one = slice(index * SUBLANES, (index + 1) * SUBLANES), slice(index, index + 1)
        near_cos[rows, :], near_sin[rows, :] = added(
            high_cos[one], high_sin[one], low_cos, low_sin
        )
    mid_cos, mid_sin = eight(SUBLANES, fine)
    top_cos, top_sin = eight(bin_total // coarse, coarse)
    for index in range(bin_total // coarse):
        far_cos[index] = top_cos[index : index + 1]
        far_sin[index] = top_sin[index : index + 1]

    @pl.loop(0, bin_total // coarse)
    def _(index):
        cos, sin = added(far_cos[index], far_sin[index], mid_cos, mid_sin)
        for part in range(SUBLANES):
            rows = pl.ds(pl.multiple_of(index * coarse, coarse) + part * fine, fine)
            one = slice(part, part + 1)
            cosines, sines = added(cos[one], sin[one], near_cos[...], near_sin[...])
            for table, values in ((cos_table, cosines), (sin_table, sines)):
                table[rows, :half_band], table[rows, half_band:] = split_bf16(values, 2)

    centre = 2 * half_band * (2 * me_ref[1] + 1) - 1 - LAGS
    bins = iota((shards * chunks, LANES), 0) * LANES + iota((shards * chunks, LANES), 1)
    norm = 1.0 / math.sqrt(bin_total)
    cos, sin = circle(bins * centre)
    for shard in range(shards):
        rows = slice(shard * chunks, (shard + 1) * chunks)
        turn_cos[shard] = cos[rows] * norm
        turn_sin[shard] = sin[rows] * norm

    for copy in copies:
        copy.wait()
    extras[...] = jnp.zeros_like(extras)
    rounds, pairs = owners_ref.shape[1], owners_ref.shape[3]
    for index in range(rounds):
        lanes = slice(index * pairs, (index + 1) * pairs)
        extras[index : index + 1, lanes] = owners_ref[0, index].astype(jnp.float32)
    extras[rounds : rounds + 1, : mask_ref.shape[1]] = mask_ref[...].astype(jnp.float32)


def add_bands(sizes, tiles, bands_ref, places, turn_refs, table_refs, blocks, pick, sums, scratch):
    groups, stations, rounds, slots, band_bins = sizes
    chunks = band_bins // LANES
    depth = 2 * chunks * stations
    rows = rounds * groups * slots
    per_tile = SUBLANES // chunks
    half = sums[0].shape[1]
    sets = [scratch[8 * index : 8 * (index + 1)] for index in range(len(tiles))]

    def prepare(index):
        held_real, held_imag, turned_real, turned_imag, cos, sin = sets[index][:6]
        for part in range(per_tile):
            step = tiles[index] * per_tile + part
            lines = slice(part * chunks, (part + 1) * chunks)
            cos[lines, :] = turn_refs[0][bands_ref[step]]
            sin[lines, :] = turn_refs[1][bands_ref[step]]
            for position, (ref, offset) in enumerate(blocks):
                for station in range(stations):
                    place = places[position] * stations + station
                    start = offset + step * depth + station * 2 * chunks
                    held_real[place, lines, :] = ref[start : start + chunks, :]
                    held_imag[place, lines, :] = ref[start + chunks : start + 2 * chunks, :]
        for place in range(groups * stations):
            real, imag = held_real[place], held_imag[place]
            turned_real[place] = real * cos[...] + imag * sin[...]
            turned_imag[place] = imag * cos[...] - real * sin[...]

    def multiply(index, part):
        held_real, held_imag, turned_real, turned_imag, _, _, cross_real, cross_imag = sets[index]
        for slot in range(part * rows // per_tile, (part + 1) * rows // per_tile):
            first, second = pick[0, slot], pick[1, slot]
            a_real, a_imag = held_real[first], held_imag[first]
            b_real, b_imag = turned_real[second], turned_imag[second]
            lines = slice(slot * SUBLANES, (slot + 1) * SUBLANES)
            cross_real[lines, :] = a_real * b_real + a_imag * b_imag
            cross_imag[lines, :] = a_imag * b_real - a_real * b_imag

    def transform(index, part):
        band = bands_ref[tiles[index] * per_tile + part]
        bins = pl.ds(pl.multiple_of(band * band_bins, band_bins), band_bins)
        for cross_ref, table_ref, total in zip(sets[index][6:], table_refs, sums):
            cross = jnp.concatenate(
                [
                    cross_ref[pl.ds(part * chunks + chunk, rows, stride=SUBLANES), :]
                    for chunk in range(chunks)
                ],
                axis=1,
            )
            high, low = split_bf16(cross, 2)
            by_high = dot(high, table_ref[bins, :])
            by_low = dot(low, table_ref[bins, :half])
            total[...] += by_high[:, :half] + (by_high[:, half:] + by_low)

    prepare(0)
    for part in range(per_tile):
        multiply(0, part)
    for index in range(len(tiles)):
        if index + 1 < len(tiles):
            prepare(index + 1)
        for part in range(per_tile):
            if index + 1 < len(tiles):
                multiply(index + 1, part)
            transform(index, part)


def placed_blocks(array_refs, layout, me, groups):
    blocks = [(array_refs[index], offset) for index, offset, _ in layout]
    return blocks, [moved(me, move, groups) for _, _, move in layout]


def near_kernel(sizes, layout, array_count, depth, bands_ref, me_ref, *refs):
    groups, stations, rounds, slots = sizes[:4]
    turn_refs, table_refs, refs = refs[:2], refs[2:4], refs[4:]
    array_refs, refs = refs[:array_count], refs[array_count:]
    (pick_out, weight, even, odd, pick, sem), scratch = refs[:6], refs[6:]
    blocks, places = placed_blocks(array_refs, layout, me_ref[0], groups)
    extras = [ref[offset + depth : offset + depth + SUBLANES, :] for ref, offset in blocks]
    pick_out[...], weight[...] = pick_slots(extras, places, me_ref[0], stations, rounds, slots)
    copy = pltpu.make_async_copy(pick_out, pick, sem)
    copy.start()
    even[...] = jnp.zeros_like(even)
    odd[...] = jnp.zeros_like(odd)
    copy.wait()
    add_bands(
        sizes, [0], bands_ref, places, turn_refs, table_refs, blocks, pick, (even, odd), scratch
    )


def next_kernel(sizes, layout, array_count, tiles, bands_ref, me_ref, *refs):
    turn_refs, table_refs, refs = refs[:2], refs[2:4], refs[4:]
    array_refs, refs = refs[:array_count], refs[array_count:]
    (pick_in, even_in, odd_in, even, odd, pick, sem), scratch = refs[:7], refs[7:]
    copy = pltpu.make_async_copy(pick_in, pick, sem)
    copy.start()
    even[...] = even_in[...]
    odd[...] = odd_in[...]
    blocks, places = placed_blocks(array_refs, layout, me_ref[0], sizes[0])
    copy.wait()
    add_bands(
        sizes, tiles, bands_ref, places, turn_refs, table_refs, blocks, pick, (even, odd), scratch
    )


def last_kernel(sizes, layout, array_count, tiles, bands_ref, me_ref, *refs):
    turn_refs, table_refs, refs = refs[:2], refs[2:4], refs[4:]
    array_refs, refs = refs[:array_count], refs[array_count:]
    pick_in, even_in, odd_in, weight, out_ref, pick, sem, even, odd, above, below, sems = refs[:12]
    copy = pltpu.make_async_copy(pick_in, pick, sem)
    copy.start()
    even[...] = even_in[...]
    odd[...] = odd_in[...]
    blocks, places = placed_blocks(array_refs, layout, me_ref[0], sizes[0])
    copy.wait()
    add_bands(
        sizes, tiles, bands_ref, places, turn_refs, table_refs, blocks, pick, (even, odd), refs[12:]
    )
    half = even.shape[1]
    row_weight = weight[:, 0:1]
    mirror = (iota((half, half), 0) + iota((half, half), 1) == half - 1).astype(jnp.bfloat16)

    def mirrored():
        pieces = [dot(piece, mirror) for piece in split_bf16((even[...] + odd[...]) * row_weight, 3)]
        return pieces[0] + (pieces[1] + pieces[2])

    if half % LANES:
        above[:, half:] = (even[...] - odd[...]) * row_weight
        above[:, :half] = mirrored()
        copies = [pltpu.make_async_copy(above, out_ref, sems.at[0])]
        copies[0].start()
    else:
        above[...] = (even[...] - odd[...]) * row_weight
        copies = [pltpu.make_async_copy(above, out_ref.at[:, half:], sems.at[0])]
        copies[0].start()
        below[...] = mirrored()
        copies.append(pltpu.make_async_copy(below, out_ref.at[:, :half], sems.at[1]))
        copies[1].start()
    for copy in copies:
        copy.wait()


def moved(me, move, size):
    return me ^ move if size & (size - 1) == 0 else lax.rem(me + size - move, size)


def moved_index(me, move, size):
    return me ^ move if size & (size - 1) == 0 else (me - move) % size


def fetched(block, group_move, band_move):
    groups, shards = lax.axis_size("grp"), lax.axis_size("freq")
    route = [
        (
            moved_index(group, group_move, groups) * shards + moved_index(band, band_move, shards),
            group * shards + band,
        )
        for group in range(groups)
        for band in range(shards)
    ]
    return lax.ppermute(block, ("grp", "freq"), route)


def exchange(column):
    groups = lax.axis_size("grp")
    rows = column.shape[0]
    if groups != 4:
        near = [column] + [fetched(column, move, 0) for move in range(1, groups)]
        far = [fetched(column, move, 1) for move in range(groups)]
        return near, far, [(move, 0, move) for move in range(groups)]
    across = fetched(column, 2, 0)
    beside = fetched(column, 0, 1)
    across, beside = lax.optimization_barrier((across, beside))
    near = jnp.concatenate([column, across], axis=0)
    near = [near, fetched(near, 1, 0)]
    far = [beside, fetched(beside, 2, 0)]
    return near, far, [(0, 0, 0), (0, rows, 2), (1, 0, 1), (1, rows, 3)]


def across_cores(far):
    if lax.axis_size("grp") != 4:
        return far
    far = jnp.concatenate(far, axis=0)
    return [far, fetched(far, 1, 0)]


def per_device(spectra, station_mask, owners):
    stations, _, band_bins = spectra.shape
    groups = lax.axis_size("grp")
    shards = lax.axis_size("freq")
    rounds = owners.shape[1]
    pairs = stations * stations
    bin_total = band_bins * shards
    capacity = (2 * pairs + groups - 1) // groups
    slots = padded(capacity, SUBLANES)
    lag_band = LAGS // shards
    half_band = lag_band // 2
    chunks = band_bins // LANES
    rows = rounds * groups * slots

    scalar = pl.BlockSpec(memory_space=pltpu.SMEM)
    vector = pl.BlockSpec(memory_space=pltpu.VMEM)
    anywhere = pl.BlockSpec(memory_space=pl.ANY)

    def call(kernel, name, scalars, arrays, out_shape, scratch, cost, others=()):
        arrays = [pltpu.with_memory_space_constraint(array, pltpu.VMEM) for array in arrays]
        in_hbm = isinstance(out_shape, jax.ShapeDtypeStruct)
        return pl.pallas_call(
            kernel,
            out_shape=out_shape,
            in_specs=[scalar] * len(scalars) + [anywhere] * len(others) + [vector] * len(arrays),
            out_specs=anywhere if in_hbm else [vector] * len(out_shape),
            scratch_shapes=scratch,
            compiler_params=pltpu.CompilerParams(vmem_limit_bytes=24 * 1024 * 1024),
            cost_estimate=cost,
            name=name,
        )(*scalars, *others, *arrays)

    tiles = spectra.reshape(2 * chunks * stations, LANES)
    column = [tiles] + [fetched(tiles, 0, move) for move in range(2, shards, 2)]
    me = jnp.stack([lax.axis_index("grp"), lax.axis_index("freq")]).astype(jnp.int32)
    table = pltpu.VMEM((bin_total, lag_band), jnp.bfloat16)
    turn = pltpu.VMEM((shards, chunks, LANES), jnp.float32)
    base = pltpu.VMEM((64, half_band), jnp.float32)
    far_base = pltpu.VMEM((bin_total // (64 * SUBLANES), 1, half_band), jnp.float32)
    *tables, turn_cos, turn_sin, extras = call(
        table_kernel,
        "tables",
        [me],
        [],
        [table] * 2 + [turn] * 2 + [pltpu.VMEM((SUBLANES, LANES), jnp.float32)],
        [base] * 2
        + [far_base] * 2
        + [
            pltpu.VMEM((1, rounds, 1, pairs), jnp.int32),
            pltpu.VMEM((1, stations), jnp.int32),
            pltpu.SemaphoreType.DMA((2,)),
        ],
        pl.CostEstimate(flops=0, bytes_accessed=8 * bin_total * half_band, transcendentals=0),
        [owners.transpose(0, 1, 3, 2), station_mask.reshape(1, stations)],
    )
    column = jnp.concatenate(column + [extras], axis=0)
    near, far, layout = exchange(column)

    near_bands = me[1] ^ jnp.arange(0, shards, 2, dtype=jnp.int32)
    far_bands = near_bands ^ 1
    sizes = (groups, stations, rounds, slots, band_bins)
    depth = column.shape[0] - SUBLANES
    spectrum = pltpu.VMEM((groups * stations, SUBLANES, LANES), jnp.float32)
    turn_tile = pltpu.VMEM((SUBLANES, LANES), jnp.float32)
    cross = pltpu.VMEM((rows * SUBLANES, LANES), jnp.float32)
    one_set = [spectrum] * 4 + [turn_tile] * 2 + [cross] * 2
    tile_count = shards // 2 * chunks // SUBLANES

    def cost(tiles):
        flops = 6 * rows * bin_total * lag_band * tiles // (2 * tile_count)
        return pl.CostEstimate(flops=flops, bytes_accessed=4 * 1024 * 1024, transcendentals=0)

    total = pltpu.VMEM((rows, half_band), jnp.float32)
    half_result = total if half_band % LANES == 0 else pltpu.VMEM((rows, lag_band), jnp.float32)
    pick_in_smem = [pltpu.SMEM((SUBLANES, rows), jnp.int32), pltpu.SemaphoreType.DMA]
    shared = [turn_cos, turn_sin, *tables]
    pick, weight, even, odd = call(
        functools.partial(near_kernel, sizes, layout, len(near), depth),
        "near_first",
        [near_bands, me],
        [*shared, *near],
        [pltpu.VMEM((SUBLANES, rows), jnp.int32), pltpu.VMEM((rows, LANES), jnp.float32)]
        + [total] * 2,
        pick_in_smem + one_set,
        cost(1),
    )
    *far, even = lax.optimization_barrier((*far, even))
    far = across_cores(far)
    later = list(range(1, tile_count))
    even, odd = call(
        functools.partial(next_kernel, sizes, layout, len(near), later),
        "near_next",
        [near_bands, me],
        [*shared, *near, pick, even, odd],
        [total] * 2,
        pick_in_smem + one_set * len(later),
        cost(len(later)),
    )
    out = call(
        functools.partial(last_kernel, sizes, layout, len(far), list(range(tile_count))),
        "far_bands",
        [far_bands, me],
        [*shared, *far, pick, even, odd, weight],
        jax.ShapeDtypeStruct((rows, lag_band), jnp.float32),
        pick_in_smem
        + [total] * 2
        + [half_result] * 2
        + [pltpu.SemaphoreType.DMA((2,))]
        + one_set * tile_count,
        cost(tile_count),
    )
    out = out.reshape(1, rounds, groups, slots, lag_band)
    return out[:, :, :, :capacity]


def solution(mesh):
    placed = (P("grp", None, "freq"), P("grp"), P("grp", None, None, None))
    return jax.shard_map(
        per_device,
        mesh=mesh,
        in_specs=placed,
        out_specs=P("grp", None, None, None, "freq"),
        check_vma=False,
    )
```

```python
import functools
import math

import jax
import jax.numpy as jnp
from jax import lax
from jax.experimental import pallas as pl
from jax.experimental.pallas import tpu as pltpu
from jax.sharding import PartitionSpec as P

LAGS = 4096
LANES = 128
SUBLANES = 8


def split_bf16(values, parts):
    pieces = []
    for _ in range(parts - 1):
        piece = values.astype(jnp.bfloat16)
        pieces.append(piece)
        values = values - piece.astype(jnp.float32)
    pieces.append(values.astype(jnp.bfloat16))
    return pieces


def iota(shape, axis):
    return lax.broadcasted_iota(jnp.int32, shape, axis)


def dot(left, right):
    return jnp.dot(left, right, preferred_element_type=jnp.float32)


def padded(count, multiple):
    return -(-count // multiple) * multiple


def pick_slots(extras, places, me, stations, rounds, slots):
    groups = len(extras)
    pairs = stations * stations
    listed = rounds * pairs
    rows = rounds * groups * slots
    place = iota((groups, groups), 1)
    held_by = jnp.zeros((groups, groups), jnp.int32)
    for position in range(groups):
        held_by = jnp.where(place == position, places[position], held_by)
    lane = iota((1, listed), 1)

    def by_group(row, shift):
        wanted = (iota((groups, groups), 0) + groups - shift) % groups
        held = jnp.concatenate([extra[row : row + 1, :] for extra in extras], axis=0)
        return dot((held_by == wanted).astype(jnp.bfloat16), held.astype(jnp.bfloat16))

    def of_station(values, number):
        spread = iota((LANES, listed), 0) == number
        return dot(values.astype(jnp.bfloat16), spread.astype(jnp.bfloat16))

    owner_ids = jnp.zeros((groups, listed), jnp.float32)
    partner_mask = jnp.zeros((groups, listed), jnp.float32)
    for index in range(rounds):
        of_round = lane // pairs == index
        owner_ids = jnp.where(of_round, by_group(index, 0), owner_ids)
        second = of_station(by_group(rounds, index + 1), lane % stations)
        partner_mask = jnp.where(of_round, second, partner_mask)
    own_mask = of_station(by_group(rounds, 0), lane % pairs // stations)
    pair_weight = own_mask * partner_mask
    mine = owner_ids == me.astype(jnp.float32)
    from_pair, to_pair = iota((listed, listed), 0), iota((listed, listed), 1)
    before = (from_pair < to_pair) & (from_pair // pairs == to_pair // pairs)
    rank = dot(mine.astype(jnp.bfloat16), before.astype(jnp.bfloat16))
    marked = jnp.where(mine, rank, -1.0).astype(jnp.bfloat16)
    of_group = (iota((rows, groups), 0) // slots) % groups == iota((rows, groups), 1)
    of_group = of_group.astype(jnp.bfloat16)
    row_id, lane_id = iota((rows, listed), 0), iota((rows, listed), 1)
    chosen = (dot(of_group, marked) == (row_id % slots).astype(jnp.float32)) & (
        row_id // (groups * slots) == lane_id // pairs
    )
    weighed = jnp.where(chosen, dot(of_group, pair_weight.astype(jnp.bfloat16)), 0.0)
    weight = dot(weighed.astype(jnp.bfloat16), jnp.ones((listed, LANES), jnp.bfloat16))
    chosen = chosen.astype(jnp.bfloat16)
    pair_id = iota((listed, LANES), 0) % pairs
    first = dot(chosen, (pair_id // stations).astype(jnp.bfloat16))
    second = dot(chosen, (pair_id % stations).astype(jnp.bfloat16))
    return first.astype(jnp.int32), second.astype(jnp.int32), weight


def make_tables(bands_ref, place, table_refs, turn_refs, base_refs, bin_total):
    near_cos, near_sin = base_refs
    fine, half_band = near_cos.shape
    steps, chunks, _ = turn_refs[0].shape
    band_bins = chunks * LANES

    def circle(turns):
        angles = (turns & (4 * bin_total - 1)).astype(jnp.float32) * (math.pi / (2 * bin_total))
        return jnp.cos(angles), jnp.sin(angles)

    def every(count, start, step):
        bins = start + iota((count, half_band), 0) * step
        return circle(bins * (2 * iota((count, half_band), 1) + 1))

    def added(cos, sin, other_cos, other_sin):
        return cos * other_cos - sin * other_sin, sin * other_cos + cos * other_sin

    low_cos, low_sin = every(SUBLANES, 0, 1)
    high_cos, high_sin = every(fine // SUBLANES, 0, SUBLANES)
    for index in range(fine // SUBLANES):
        rows, one = slice(index * SUBLANES, (index + 1) * SUBLANES), slice(index, index + 1)
        near_cos[rows, :], near_sin[rows, :] = added(
            high_cos[one], high_sin[one], low_cos, low_sin
        )

    centre = 2 * half_band * (2 * place + 1) - 1 - LAGS
    norm = 1.0 / math.sqrt(bin_total)
    for step in range(steps):
        start = bands_ref[step] * band_bins
        cos, sin = every(band_bins // fine, start, fine)
        for part in range(band_bins // fine):
            one = slice(part, part + 1)
            values = added(cos[one], sin[one], near_cos[...], near_sin[...])
            rows = slice(step * band_bins + part * fine, step * band_bins + (part + 1) * fine)
            for table, value in zip(table_refs, values):
                table[rows, :half_band], table[rows, half_band:] = split_bf16(value, 2)
        bins = start + iota((chunks, LANES), 0) * LANES + iota((chunks, LANES), 1)
        for turn, value in zip(turn_refs, circle(bins * centre)):
            turn[step] = value * norm


def near_tables(bin_total, bands_ref, me_ref, owners_hbm, mask_hbm, *refs):
    table_refs, turn_refs, extras = refs[:2], refs[2:4], refs[4]
    base_refs, (owners_ref, mask_ref, sems) = refs[5:7], refs[7:]
    copies = [
        pltpu.make_async_copy(owners_hbm, owners_ref, sems.at[0]),
        pltpu.make_async_copy(mask_hbm, mask_ref, sems.at[1]),
    ]
    for copy in copies:
        copy.start()
    make_tables(bands_ref, me_ref[1], table_refs, turn_refs, base_refs, bin_total)
    for copy in copies:
        copy.wait()
    extras[...] = jnp.zeros_like(extras)
    rounds, pairs = owners_ref.shape[1], owners_ref.shape[3]
    for index in range(rounds):
        lanes = slice(index * pairs, (index + 1) * pairs)
        extras[index : index + 1, lanes] = owners_ref[0, index].astype(jnp.float32)
    extras[rounds : rounds + 1, : mask_ref.shape[1]] = mask_ref[...].astype(jnp.float32)


def far_tables(bin_total, bands_ref, me_ref, *refs):
    make_tables(bands_ref, me_ref[1], refs[:2], refs[2:4], refs[4:], bin_total)


def add_bands(sizes, steps, places, turn_refs, table_refs, blocks, picks, sums, scratch):
    groups, stations, rounds, slots, band_bins = sizes
    chunks = band_bins // LANES
    depth = 2 * chunks * stations
    half = sums[0].shape[1]
    first, second = picks
    sets = [scratch[6 * index : 6 * (index + 1)] for index in range(2)]
    octets = [
        (group, (group + groups - 1 - index) % groups)
        for index in range(rounds)
        for group in range(groups)
        for _ in range(slots // SUBLANES)
    ]
    units = len(octets) // 2

    def prepare(index):
        step, (held, turned) = steps[index], sets[index % 2][:2]
        for position, (ref, offset) in enumerate(blocks):
            group = places[position]
            for q in range(chunks):
                turn_cos, turn_sin = [turn[step, q : q + 1, :] for turn in turn_refs]
                start = offset + step * depth + q * stations
                real = ref[start : start + stations, :]
                start += chunks * stations
                imag = ref[start : start + stations, :]
                held[group, q] = real
                held[group, chunks + q] = imag
                turned[group, q] = real * turn_cos + imag * turn_sin
                turned[group, chunks + q] = imag * turn_cos - real * turn_sin

    def multiply(index, part, parts):
        held, turned, *cross = sets[index % 2]
        for unit in range(part * units // parts, (part + 1) * units // parts):
            rows = slice(2 * unit * SUBLANES, 2 * (unit + 1) * SUBLANES)
            for q in range(chunks):
                lanes = slice(q * LANES, (q + 1) * LANES)
                reals, imags = [], []
                for octet in (2 * unit, 2 * unit + 1):
                    group, partner = octets[octet]
                    lines = slice(octet * SUBLANES, (octet + 1) * SUBLANES)
                    index_a, index_b = first[lines, :], second[lines, :]
                    a_real = jnp.take_along_axis(held[group, q], index_a, axis=0)
                    a_imag = jnp.take_along_axis(held[group, chunks + q], index_a, axis=0)
                    b_real = jnp.take_along_axis(turned[partner, q], index_b, axis=0)
                    b_imag = jnp.take_along_axis(turned[partner, chunks + q], index_b, axis=0)
                    reals.append(a_real * b_real + a_imag * b_imag)
                    imags.append(a_imag * b_real - a_real * b_imag)
                for place, values in ((0, reals), (2, imags)):
                    high, low = split_bf16(jnp.concatenate(values, axis=0), 2)
                    cross[place][rows, lanes] = high
                    cross[place + 1][rows, lanes] = low

    def transform(index, which):
        step, (high, low) = steps[index], sets[index % 2][2 + 2 * which : 4 + 2 * which]
        bins = slice(step * band_bins, (step + 1) * band_bins)
        table, total = table_refs[which], sums[which]
        by_high = dot(high[...], table[bins, :])
        by_low = dot(low[...], table[bins, :half])
        total[...] += by_high[:, :half] + (by_high[:, half:] + by_low)

    prepare(0)
    multiply(0, 0, 1)
    for index in range(len(steps)):
        more = index + 1 < len(steps)
        if more:
            prepare(index + 1)
        for which in range(2):
            if more:
                multiply(index + 1, which, 2)
            transform(index, which)


def placed_blocks(array_refs, layout, me, groups):
    blocks = [(array_refs[index], offset) for index, offset, _ in layout]
    return blocks, [moved(me, move, groups) for _, _, move in layout]


def near_kernel(sizes, layout, array_count, depth, steps, me_ref, *refs):
    groups, stations, rounds, slots = sizes[:4]
    turn_refs, table_refs, refs = refs[:2], refs[2:4], refs[4:]
    array_refs, refs = refs[:array_count], refs[array_count:]
    (first, second, weight, even, odd), scratch = refs[:5], refs[5:]
    blocks, places = placed_blocks(array_refs, layout, me_ref[0], groups)
    extras = [ref[offset + depth : offset + depth + SUBLANES, :] for ref, offset in blocks]
    first[...], second[...], weight[...] = pick_slots(
        extras, places, me_ref[0], stations, rounds, slots
    )
    even[...] = jnp.zeros_like(even)
    odd[...] = jnp.zeros_like(odd)
    add_bands(
        sizes, steps, places, turn_refs, table_refs, blocks, (first, second), (even, odd), scratch
    )


def next_kernel(sizes, layout, array_count, steps, me_ref, *refs):
    turn_refs, table_refs, refs = refs[:2], refs[2:4], refs[4:]
    array_refs, refs = refs[:array_count], refs[array_count:]
    (first, second, even_in, odd_in, even, odd), scratch = refs[:6], refs[6:]
    even[...] = even_in[...]
    odd[...] = odd_in[...]
    blocks, places = placed_blocks(array_refs, layout, me_ref[0], sizes[0])
    add_bands(
        sizes, steps, places, turn_refs, table_refs, blocks, (first, second), (even, odd), scratch
    )


def last_kernel(sizes, layout, array_count, steps, me_ref, *refs):
    turn_refs, table_refs, refs = refs[:2], refs[2:4], refs[4:]
    array_refs, refs = refs[:array_count], refs[array_count:]
    first, second, even_in, odd_in, weight, out_ref, even, odd, above, below, sems = refs[:11]
    even[...] = even_in[...]
    odd[...] = odd_in[...]
    blocks, places = placed_blocks(array_refs, layout, me_ref[0], sizes[0])
    add_bands(
        sizes, steps, places, turn_refs, table_refs, blocks, (first, second), (even, odd), refs[11:]
    )
    half = even.shape[1]
    row_weight = weight[:, 0:1]
    mirror = (iota((half, half), 0) + iota((half, half), 1) == half - 1).astype(jnp.bfloat16)

    def mirrored():
        pieces = [dot(piece, mirror) for piece in split_bf16((even[...] + odd[...]) * row_weight, 3)]
        return pieces[0] + (pieces[1] + pieces[2])

    if half % LANES:
        above[:, half:] = (even[...] - odd[...]) * row_weight
        above[:, :half] = mirrored()
        copies = [pltpu.make_async_copy(above, out_ref, sems.at[0])]
        copies[0].start()
    else:
        above[...] = (even[...] - odd[...]) * row_weight
        copies = [pltpu.make_async_copy(above, out_ref.at[:, half:], sems.at[0])]
        copies[0].start()
        below[...] = mirrored()
        copies.append(pltpu.make_async_copy(below, out_ref.at[:, :half], sems.at[1]))
        copies[1].start()
    for copy in copies:
        copy.wait()


def moved(me, move, size):
    return me ^ move if size & (size - 1) == 0 else lax.rem(me + size - move, size)


def moved_index(me, move, size):
    return me ^ move if size & (size - 1) == 0 else (me - move) % size


def fetched(block, group_move, band_move):
    groups, shards = lax.axis_size("grp"), lax.axis_size("freq")
    route = [
        (
            moved_index(group, group_move, groups) * shards + moved_index(band, band_move, shards),
            group * shards + band,
        )
        for group in range(groups)
        for band in range(shards)
    ]
    return lax.ppermute(block, ("grp", "freq"), route)


def exchange(column, ready):
    groups = lax.axis_size("grp")
    rows = column.shape[0]
    if groups != 4:
        near = [column] + [fetched(column, move, 0) for move in range(1, groups)]
        far = [fetched(column, move, 1) for move in range(groups)]
        return near, far, [(move, 0, move) for move in range(groups)], ready
    across = fetched(column, 2, 0)
    beside = fetched(column, 0, 1)
    across, beside, *ready = lax.optimization_barrier((across, beside, *ready))
    near = jnp.concatenate([column, across], axis=0)
    near = [near, fetched(near, 1, 0)]
    far = [beside, fetched(beside, 2, 0)]
    return near, far, [(0, 0, 0), (0, rows, 2), (1, 0, 1), (1, rows, 3)], ready


def across_cores(far):
    if lax.axis_size("grp") != 4:
        return far
    far = jnp.concatenate(far, axis=0)
    return [far, fetched(far, 1, 0)]


def per_device(spectra, station_mask, owners):
    stations, _, band_bins = spectra.shape
    groups = lax.axis_size("grp")
    shards = lax.axis_size("freq")
    rounds = owners.shape[1]
    pairs = stations * stations
    bin_total = band_bins * shards
    capacity = (2 * pairs + groups - 1) // groups
    slots = padded(capacity, SUBLANES)
    lag_band = LAGS // shards
    half_band = lag_band // 2
    chunks = band_bins // LANES
    rows = rounds * groups * slots

    scalar = pl.BlockSpec(memory_space=pltpu.SMEM)
    vector = pl.BlockSpec(memory_space=pltpu.VMEM)
    in_hbm = pl.BlockSpec(memory_space=pltpu.HBM)

    def call(kernel, name, scalars, arrays, out_shape, scratch, cost, others=()):
        arrays = [pltpu.with_memory_space_constraint(array, pltpu.VMEM) for array in arrays]
        others = [pltpu.with_memory_space_constraint(array, pltpu.HBM) for array in others]
        to_hbm = isinstance(out_shape, jax.ShapeDtypeStruct)
        return pl.pallas_call(
            kernel,
            out_shape=out_shape,
            in_specs=[scalar] * len(scalars) + [in_hbm] * len(others) + [vector] * len(arrays),
            out_specs=in_hbm if to_hbm else [vector] * len(out_shape),
            scratch_shapes=scratch,
            compiler_params=pltpu.CompilerParams(vmem_limit_bytes=24 * 1024 * 1024),
            cost_estimate=cost,
            name=name,
        )(*scalars, *others, *arrays)

    steps = shards // 2
    me = jnp.stack([lax.axis_index("grp"), lax.axis_index("freq")]).astype(jnp.int32)
    near_bands = me[1] ^ jnp.arange(0, shards, 2, dtype=jnp.int32)
    tiles = spectra.reshape(stations, 2, chunks, LANES).transpose(1, 2, 0, 3)
    tiles = tiles.reshape(2 * chunks * stations, LANES)
    column = [tiles] + [fetched(tiles, 0, move) for move in range(2, shards, 2)]

    table = pltpu.VMEM((steps * band_bins, lag_band), jnp.bfloat16)
    turn = pltpu.VMEM((steps, chunks, LANES), jnp.float32)
    base = pltpu.VMEM((64, half_band), jnp.float32)
    table_cost = pl.CostEstimate(
        flops=0, bytes_accessed=4 * bin_total * half_band, transcendentals=0
    )
    *near_table, extras = call(
        functools.partial(near_tables, bin_total),
        "near_tables",
        [near_bands, me],
        [],
        [table] * 2 + [turn] * 2 + [pltpu.VMEM((SUBLANES, LANES), jnp.float32)],
        [base] * 2
        + [
            pltpu.VMEM((1, rounds, 1, pairs), jnp.int32),
            pltpu.VMEM((1, stations), jnp.int32),
            pltpu.SemaphoreType.DMA((2,)),
        ],
        table_cost,
        [owners.transpose(0, 1, 3, 2), station_mask.reshape(1, stations)],
    )
    column = jnp.concatenate(column + [extras], axis=0)
    column, far_bands = lax.optimization_barrier((column, near_bands ^ 1))
    far_table = call(
        functools.partial(far_tables, bin_total),
        "far_tables",
        [far_bands, me],
        [],
        [table] * 2 + [turn] * 2,
        [base] * 2,
        table_cost,
    )
    near, far, layout, far_table = exchange(column, far_table)

    sizes = (groups, stations, rounds, slots, band_bins)
    depth = column.shape[0] - SUBLANES
    spectrum = pltpu.VMEM((groups, 2 * chunks, stations, LANES), jnp.float32)
    cross = pltpu.VMEM((rows, band_bins), jnp.bfloat16)
    scratch = ([spectrum] * 2 + [cross] * 4) * 2

    def cost(count):
        flops = 6 * rows * band_bins * lag_band * count
        return pl.CostEstimate(flops=flops, bytes_accessed=2 * 1024 * 1024, transcendentals=0)

    total = pltpu.VMEM((rows, half_band), jnp.float32)
    half_result = total if half_band % LANES == 0 else pltpu.VMEM((rows, lag_band), jnp.float32)
    index = pltpu.VMEM((rows, LANES), jnp.int32)
    table_at = [2, 3, 0, 1]
    first, second, weight, even, odd = call(
        functools.partial(near_kernel, sizes, layout, len(near), depth, range(steps // 2)),
        "near_first",
        [me],
        [near_table[place] for place in table_at] + near,
        [index] * 2 + [pltpu.VMEM((rows, LANES), jnp.float32)] + [total] * 2,
        scratch,
        cost(steps // 2),
    )
    *far, even = lax.optimization_barrier((*far, even))
    far = across_cores(far)
    even, odd = call(
        functools.partial(next_kernel, sizes, layout, len(near), range(steps // 2, steps)),
        "near_next",
        [me],
        [near_table[place] for place in table_at] + near + [first, second, even, odd],
        [total] * 2,
        scratch,
        cost(steps - steps // 2),
    )
    out = call(
        functools.partial(last_kernel, sizes, layout, len(far), range(steps)),
        "far_bands",
        [me],
        [far_table[place] for place in table_at] + far + [first, second, even, odd, weight],
        jax.ShapeDtypeStruct((rows, lag_band), jnp.float32),
        [total] * 2 + [half_result] * 2 + [pltpu.SemaphoreType.DMA((2,))] + scratch,
        cost(steps),
    )
    out = out.reshape(1, rounds, groups, slots, lag_band)
    return out[:, :, :, :capacity]


def solution(mesh):
    placed = (P("grp", None, "freq"), P("grp"), P("grp", None, None, None))
    return jax.shard_map(
        per_device,
        mesh=mesh,
        in_specs=placed,
        out_specs=P("grp", None, None, None, "freq"),
        check_vma=False,
    )
```

```python
import functools
import math

import jax
import jax.numpy as jnp
from jax import lax
from jax.experimental import pallas as pl
from jax.experimental.pallas import tpu as pltpu
from jax.sharding import PartitionSpec as P

LAGS = 4096
LANES = 128
SUBLANES = 8


def split_bf16(values, parts):
    pieces = []
    for _ in range(parts - 1):
        piece = values.astype(jnp.bfloat16)
        pieces.append(piece)
        values = values - piece.astype(jnp.float32)
    pieces.append(values.astype(jnp.bfloat16))
    return pieces


def iota(shape, axis):
    return lax.broadcasted_iota(jnp.int32, shape, axis)


def dot(left, right):
    return jnp.dot(left, right, preferred_element_type=jnp.float32)


def padded(count, multiple):
    return -(-count // multiple) * multiple


def pick_slots(extras, places, me, stations, rounds, slots):
    groups = len(extras)
    pairs = stations * stations
    listed = rounds * pairs
    rows = rounds * groups * slots
    place = iota((groups, groups), 1)
    held_by = jnp.zeros((groups, groups), jnp.int32)
    for position in range(groups):
        held_by = jnp.where(place == position, places[position], held_by)
    lane = iota((1, listed), 1)

    def by_group(row, shift):
        wanted = (iota((groups, groups), 0) + groups - shift) % groups
        held = jnp.concatenate([extra[row : row + 1, :] for extra in extras], axis=0)
        return dot((held_by == wanted).astype(jnp.bfloat16), held.astype(jnp.bfloat16))

    def of_station(values, number):
        spread = iota((LANES, listed), 0) == number
        return dot(values.astype(jnp.bfloat16), spread.astype(jnp.bfloat16))

    owner_ids = jnp.zeros((groups, listed), jnp.float32)
    partner_mask = jnp.zeros((groups, listed), jnp.float32)
    for index in range(rounds):
        of_round = lane // pairs == index
        owner_ids = jnp.where(of_round, by_group(index, 0), owner_ids)
        second = of_station(by_group(rounds, index + 1), lane % stations)
        partner_mask = jnp.where(of_round, second, partner_mask)
    own_mask = of_station(by_group(rounds, 0), lane % pairs // stations)
    pair_weight = own_mask * partner_mask
    mine = owner_ids == me.astype(jnp.float32)
    from_pair, to_pair = iota((listed, listed), 0), iota((listed, listed), 1)
    before = (from_pair < to_pair) & (from_pair // pairs == to_pair // pairs)
    rank = dot(mine.astype(jnp.bfloat16), before.astype(jnp.bfloat16))
    marked = jnp.where(mine, rank, -1.0).astype(jnp.bfloat16)
    of_group = (iota((rows, groups), 0) // slots) % groups == iota((rows, groups), 1)
    of_group = of_group.astype(jnp.bfloat16)
    row_id, lane_id = iota((rows, listed), 0), iota((rows, listed), 1)
    chosen = (dot(of_group, marked) == (row_id % slots).astype(jnp.float32)) & (
        row_id // (groups * slots) == lane_id // pairs
    )
    weighed = jnp.where(chosen, dot(of_group, pair_weight.astype(jnp.bfloat16)), 0.0)
    weight = dot(weighed.astype(jnp.bfloat16), jnp.ones((listed, LANES), jnp.bfloat16))
    chosen = chosen.astype(jnp.bfloat16)
    pair_id = iota((listed, LANES), 0) % pairs
    first = dot(chosen, (pair_id // stations).astype(jnp.bfloat16))
    second = dot(chosen, (pair_id % stations).astype(jnp.bfloat16))
    return first.astype(jnp.int32), second.astype(jnp.int32), weight


def make_tables(bands_ref, place, table_refs, turn_refs, base_refs, bin_total):
    near_cos, near_sin = base_refs
    fine, half_band = near_cos.shape
    steps, chunks, _ = turn_refs[0].shape
    band_bins = chunks * LANES

    def circle(turns):
        angles = (turns & (4 * bin_total - 1)).astype(jnp.float32) * (math.pi / (2 * bin_total))
        return jnp.cos(angles), jnp.sin(angles)

    def every(count, start, step):
        bins = start + iota((count, half_band), 0) * step
        return circle(bins * (2 * iota((count, half_band), 1) + 1))

    def added(cos, sin, other_cos, other_sin):
        return cos * other_cos - sin * other_sin, sin * other_cos + cos * other_sin

    low_cos, low_sin = every(SUBLANES, 0, 1)
    high_cos, high_sin = every(fine // SUBLANES, 0, SUBLANES)
    for index in range(fine // SUBLANES):
        rows, one = slice(index * SUBLANES, (index + 1) * SUBLANES), slice(index, index + 1)
        near_cos[rows, :], near_sin[rows, :] = added(
            high_cos[one], high_sin[one], low_cos, low_sin
        )

    centre = 2 * half_band * (2 * place + 1) - 1 - LAGS
    norm = 1.0 / math.sqrt(bin_total)
    for step in range(steps):
        start = bands_ref[step] * band_bins
        cos, sin = every(band_bins // fine, start, fine)
        for part in range(band_bins // fine):
            one = slice(part, part + 1)
            values = added(cos[one], sin[one], near_cos[...], near_sin[...])
            rows = slice(step * band_bins + part * fine, step * band_bins + (part + 1) * fine)
            for table, value in zip(table_refs, values):
                table[rows, :half_band], table[rows, half_band:] = split_bf16(value, 2)
        bins = start + iota((chunks, LANES), 0) * LANES + iota((chunks, LANES), 1)
        for turn, value in zip(turn_refs, circle(bins * centre)):
            turn[step] = value * norm


def near_tables(bin_total, bands_ref, me_ref, owners_hbm, mask_hbm, *refs):
    table_refs, turn_refs, extras = refs[:2], refs[2:4], refs[4]
    base_refs, (owners_ref, mask_ref, sems) = refs[5:7], refs[7:]
    copies = [
        pltpu.make_async_copy(owners_hbm, owners_ref, sems.at[0]),
        pltpu.make_async_copy(mask_hbm, mask_ref, sems.at[1]),
    ]
    for copy in copies:
        copy.start()
    make_tables(bands_ref, me_ref[1], table_refs, turn_refs, base_refs, bin_total)
    for copy in copies:
        copy.wait()
    extras[...] = jnp.zeros_like(extras)
    rounds, pairs = owners_ref.shape[1], owners_ref.shape[3]
    for index in range(rounds):
        lanes = slice(index * pairs, (index + 1) * pairs)
        extras[index : index + 1, lanes] = owners_ref[0, index].astype(jnp.float32)
    extras[rounds : rounds + 1, : mask_ref.shape[1]] = mask_ref[...].astype(jnp.float32)


def far_tables(bin_total, bands_ref, me_ref, *refs):
    make_tables(bands_ref, me_ref[1], refs[:2], refs[2:4], refs[4:], bin_total)


def add_bands(sizes, steps, places, turn_refs, table_refs, blocks, picks, sums, scratch):
    groups, stations, rounds, slots, band_bins = sizes
    chunks = band_bins // LANES
    depth = 2 * chunks * stations
    half = sums[0].shape[1]
    first, second = picks
    sets = [scratch[6 * index : 6 * (index + 1)] for index in range(2)]
    octets = [
        (group, (group + groups - 1 - index) % groups)
        for index in range(rounds)
        for group in range(groups)
        for _ in range(slots // SUBLANES)
    ]
    units = len(octets) // 2

    def prepare(index):
        (step, place_step), (held, turned) = steps[index], sets[index % 2][:2]
        for position, (ref, offset) in enumerate(blocks):
            group = places[position]
            for q in range(chunks):
                turn_cos, turn_sin = [turn[step, q : q + 1, :] for turn in turn_refs]
                start = offset + place_step * depth + q * stations
                real = ref[start : start + stations, :]
                start += chunks * stations
                imag = ref[start : start + stations, :]
                held[group, q] = real
                held[group, chunks + q] = imag
                turned[group, q] = real * turn_cos + imag * turn_sin
                turned[group, chunks + q] = imag * turn_cos - real * turn_sin

    def multiply(index, part, parts):
        held, turned, *cross = sets[index % 2]
        for unit in range(part * units // parts, (part + 1) * units // parts):
            rows = slice(2 * unit * SUBLANES, 2 * (unit + 1) * SUBLANES)
            for q in range(chunks):
                lanes = slice(q * LANES, (q + 1) * LANES)
                reals, imags = [], []
                for octet in (2 * unit, 2 * unit + 1):
                    group, partner = octets[octet]
                    lines = slice(octet * SUBLANES, (octet + 1) * SUBLANES)
                    index_a, index_b = first[lines, :], second[lines, :]
                    a_real = jnp.take_along_axis(held[group, q], index_a, axis=0)
                    a_imag = jnp.take_along_axis(held[group, chunks + q], index_a, axis=0)
                    b_real = jnp.take_along_axis(turned[partner, q], index_b, axis=0)
                    b_imag = jnp.take_along_axis(turned[partner, chunks + q], index_b, axis=0)
                    reals.append(a_real * b_real + a_imag * b_imag)
                    imags.append(a_imag * b_real - a_real * b_imag)
                for place, values in ((0, reals), (2, imags)):
                    high, low = split_bf16(jnp.concatenate(values, axis=0), 2)
                    cross[place][rows, lanes] = high
                    cross[place + 1][rows, lanes] = low

    def transform(index, which):
        step, (high, low) = steps[index][0], sets[index % 2][2 + 2 * which : 4 + 2 * which]
        bins = slice(step * band_bins, (step + 1) * band_bins)
        table, total = table_refs[which], sums[which]
        by_high = dot(high[...], table[bins, :])
        by_low = dot(low[...], table[bins, :half])
        total[...] += by_high[:, :half] + (by_high[:, half:] + by_low)

    prepare(0)
    multiply(0, 0, 1)
    for index in range(len(steps)):
        more = index + 1 < len(steps)
        if more:
            prepare(index + 1)
        for which in range(2):
            if more:
                multiply(index + 1, which, 2)
            transform(index, which)


def placed_blocks(array_refs, layout, me, groups):
    blocks = [(array_refs[index], offset) for index, offset, _ in layout]
    return blocks, [moved(me, move, groups) for _, _, move in layout]


def near_kernel(sizes, layout, array_count, depth, steps, me_ref, *refs):
    groups, stations, rounds, slots = sizes[:4]
    turn_refs, table_refs, refs = refs[:2], refs[2:4], refs[4:]
    array_refs, refs = refs[:array_count], refs[array_count:]
    (first, second, weight, even, odd), scratch = refs[:5], refs[5:]
    blocks, places = placed_blocks(array_refs, layout, me_ref[0], groups)
    extras = [ref[offset + depth : offset + depth + SUBLANES, :] for ref, offset in blocks]
    first[...], second[...], weight[...] = pick_slots(
        extras, places, me_ref[0], stations, rounds, slots
    )
    even[...] = jnp.zeros_like(even)
    odd[...] = jnp.zeros_like(odd)
    add_bands(
        sizes, steps, places, turn_refs, table_refs, blocks, (first, second), (even, odd), scratch
    )


def next_kernel(sizes, layout, array_count, steps, me_ref, *refs):
    turn_refs, table_refs, refs = refs[:2], refs[2:4], refs[4:]
    array_refs, refs = refs[:array_count], refs[array_count:]
    (first, second, even_in, odd_in, even, odd), scratch = refs[:6], refs[6:]
    even[...] = even_in[...]
    odd[...] = odd_in[...]
    blocks, places = placed_blocks(array_refs, layout, me_ref[0], sizes[0])
    add_bands(
        sizes, steps, places, turn_refs, table_refs, blocks, (first, second), (even, odd), scratch
    )


def last_kernel(sizes, layout, array_count, steps, me_ref, *refs):
    turn_refs, table_refs, refs = refs[:2], refs[2:4], refs[4:]
    array_refs, refs = refs[:array_count], refs[array_count:]
    first, second, even_in, odd_in, weight, out_ref, even, odd, above, below, sems = refs[:11]
    even[...] = even_in[...]
    odd[...] = odd_in[...]
    blocks, places = placed_blocks(array_refs, layout, me_ref[0], sizes[0])
    add_bands(
        sizes, steps, places, turn_refs, table_refs, blocks, (first, second), (even, odd), refs[11:]
    )
    half = even.shape[1]
    row_weight = weight[:, 0:1]
    mirror = (iota((half, half), 0) + iota((half, half), 1) == half - 1).astype(jnp.bfloat16)

    def mirrored():
        pieces = [dot(piece, mirror) for piece in split_bf16((even[...] + odd[...]) * row_weight, 3)]
        return pieces[0] + (pieces[1] + pieces[2])

    if half % LANES:
        above[:, half:] = (even[...] - odd[...]) * row_weight
        above[:, :half] = mirrored()
        copies = [pltpu.make_async_copy(above, out_ref, sems.at[0])]
        copies[0].start()
    else:
        above[...] = (even[...] - odd[...]) * row_weight
        copies = [pltpu.make_async_copy(above, out_ref.at[:, half:], sems.at[0])]
        copies[0].start()
        below[...] = mirrored()
        copies.append(pltpu.make_async_copy(below, out_ref.at[:, :half], sems.at[1]))
        copies[1].start()
    for copy in copies:
        copy.wait()


def moved(me, move, size):
    return me ^ move if size & (size - 1) == 0 else lax.rem(me + size - move, size)


def moved_index(me, move, size):
    return me ^ move if size & (size - 1) == 0 else (me - move) % size


def fetched(block, group_move, band_move):
    groups, shards = lax.axis_size("grp"), lax.axis_size("freq")
    route = [
        (
            moved_index(group, group_move, groups) * shards + moved_index(band, band_move, shards),
            group * shards + band,
        )
        for group in range(groups)
        for band in range(shards)
    ]
    return lax.ppermute(block, ("grp", "freq"), route)


def exchange(column, depth, parts, ready):
    groups = lax.axis_size("grp")
    if groups != 4:
        near = [column] + [fetched(column, move, 0) for move in range(1, groups)]
        layout = [(move, 0, move) for move in range(groups)]
        fars = [
            [fetched(column[first * depth : last * depth], move, 1) for move in range(groups)]
            for first, last in parts
        ]
        return near, layout, fars, ready
    across, *ready = lax.optimization_barrier((fetched(column, 2, 0), *ready))
    near = jnp.concatenate([column, across], axis=0)
    near = [near, fetched(near, 1, 0)]
    fars = []
    for first, last in parts:
        rows = slice(first * depth, last * depth)
        fars.append([fetched(jnp.concatenate([column[rows], across[rows]], axis=0), 0, 1)])
    return near, two_columns(column.shape[0]), fars, ready


def two_columns(rows):
    return [(0, 0, 0), (0, rows, 2), (1, 0, 1), (1, rows, 3)]


def across_cores(far):
    if lax.axis_size("grp") != 4:
        return far, [(move, 0, move) for move in range(len(far))]
    return [far[0], fetched(far[0], 1, 0)], two_columns(far[0].shape[0] // 2)


def per_device(spectra, station_mask, owners):
    stations, _, band_bins = spectra.shape
    groups = lax.axis_size("grp")
    shards = lax.axis_size("freq")
    rounds = owners.shape[1]
    pairs = stations * stations
    bin_total = band_bins * shards
    capacity = (2 * pairs + groups - 1) // groups
    slots = padded(capacity, SUBLANES)
    lag_band = LAGS // shards
    half_band = lag_band // 2
    chunks = band_bins // LANES
    rows = rounds * groups * slots

    scalar = pl.BlockSpec(memory_space=pltpu.SMEM)
    vector = pl.BlockSpec(memory_space=pltpu.VMEM)
    in_hbm = pl.BlockSpec(memory_space=pltpu.HBM)

    def call(kernel, name, scalars, arrays, out_shape, scratch, cost, others=()):
        arrays = [pltpu.with_memory_space_constraint(array, pltpu.VMEM) for array in arrays]
        others = [pltpu.with_memory_space_constraint(array, pltpu.HBM) for array in others]
        to_hbm = isinstance(out_shape, jax.ShapeDtypeStruct)
        return pl.pallas_call(
            kernel,
            out_shape=out_shape,
            in_specs=[scalar] * len(scalars) + [in_hbm] * len(others) + [vector] * len(arrays),
            out_specs=in_hbm if to_hbm else [vector] * len(out_shape),
            scratch_shapes=scratch,
            compiler_params=pltpu.CompilerParams(vmem_limit_bytes=24 * 1024 * 1024),
            cost_estimate=cost,
            name=name,
        )(*scalars, *others, *arrays)

    steps = shards // 2
    me = jnp.stack([lax.axis_index("grp"), lax.axis_index("freq")]).astype(jnp.int32)
    near_bands = me[1] ^ jnp.arange(0, shards, 2, dtype=jnp.int32)
    tiles = spectra.reshape(stations, 2, chunks, LANES).transpose(1, 2, 0, 3)
    tiles = tiles.reshape(2 * chunks * stations, LANES)
    column = [tiles] + [fetched(tiles, 0, move) for move in range(2, shards, 2)]

    table = pltpu.VMEM((steps * band_bins, lag_band), jnp.bfloat16)
    turn = pltpu.VMEM((steps, chunks, LANES), jnp.float32)
    base = pltpu.VMEM((64, half_band), jnp.float32)
    table_cost = pl.CostEstimate(
        flops=0, bytes_accessed=4 * bin_total * half_band, transcendentals=0
    )
    *near_table, extras = call(
        functools.partial(near_tables, bin_total),
        "near_tables",
        [near_bands, me],
        [],
        [table] * 2 + [turn] * 2 + [pltpu.VMEM((SUBLANES, LANES), jnp.float32)],
        [base] * 2
        + [
            pltpu.VMEM((1, rounds, 1, pairs), jnp.int32),
            pltpu.VMEM((1, stations), jnp.int32),
            pltpu.SemaphoreType.DMA((2,)),
        ],
        table_cost,
        [owners.transpose(0, 1, 3, 2), station_mask.reshape(1, stations)],
    )
    column = jnp.concatenate(column + [extras], axis=0)
    column, far_bands = lax.optimization_barrier((column, near_bands ^ 1))
    far_table = call(
        functools.partial(far_tables, bin_total),
        "far_tables",
        [far_bands, me],
        [],
        [table] * 2 + [turn] * 2,
        [base] * 2,
        table_cost,
    )
    depth = 2 * chunks * stations
    parts = [(0, steps // 2), (steps // 2, steps)]
    near, layout, fars, far_table = exchange(column, depth, parts, far_table)

    sizes = (groups, stations, rounds, slots, band_bins)
    spectrum = pltpu.VMEM((groups, 2 * chunks, stations, LANES), jnp.float32)
    cross = pltpu.VMEM((rows, band_bins), jnp.bfloat16)
    scratch = ([spectrum] * 2 + [cross] * 4) * 2

    def cost(count):
        flops = 6 * rows * band_bins * lag_band * count
        return pl.CostEstimate(flops=flops, bytes_accessed=2 * 1024 * 1024, transcendentals=0)

    total = pltpu.VMEM((rows, half_band), jnp.float32)
    half_result = total if half_band % LANES == 0 else pltpu.VMEM((rows, lag_band), jnp.float32)
    index = pltpu.VMEM((rows, LANES), jnp.int32)
    near_table = [near_table[place] for place in (2, 3, 0, 1)]
    far_table = [far_table[place] for place in (2, 3, 0, 1)]

    def more(name, layout, arrays, tables, first_step, last_step, place_step, sums):
        some = [(step, step - place_step) for step in range(first_step, last_step)]
        return call(
            functools.partial(next_kernel, sizes, layout, len(arrays), some),
            name,
            [me],
            [*tables, *arrays, first, second, *sums],
            [total] * 2,
            scratch,
            cost(len(some)),
        )

    split = steps - steps // 4
    first, second, weight, even, odd = call(
        functools.partial(
            near_kernel, sizes, layout, len(near), steps * depth, [(i, i) for i in range(split)]
        ),
        "near_first",
        [me],
        near_table + near,
        [index] * 2 + [pltpu.VMEM((rows, LANES), jnp.float32)] + [total] * 2,
        scratch,
        cost(split),
    )
    *far, even = lax.optimization_barrier((*fars[0], even))
    far, far_layout = across_cores(far)
    even, odd = more("near_next", layout, near, near_table, split, steps, 0, (even, odd))
    *last, even = lax.optimization_barrier((*fars[1], even))
    last, _ = across_cores(last)
    even, odd = more("far_first", far_layout, far, far_table, *parts[0], 0, (even, odd))
    some = [(step, step - parts[1][0]) for step in range(*parts[1])]
    out = call(
        functools.partial(last_kernel, sizes, far_layout, len(last), some),
        "far_next",
        [me],
        [*far_table, *last, first, second, even, odd, weight],
        jax.ShapeDtypeStruct((rows, lag_band), jnp.float32),
        [total] * 2 + [half_result] * 2 + [pltpu.SemaphoreType.DMA((2,))] + scratch,
        cost(len(some)),
    )
    out = out.reshape(1, rounds, groups, slots, lag_band)
    return out[:, :, :, :capacity]


def solution(mesh):
    placed = (P("grp", None, "freq"), P("grp"), P("grp", None, None, None))
    return jax.shard_map(
        per_device,
        mesh=mesh,
        in_specs=placed,
        out_specs=P("grp", None, None, None, "freq"),
        check_vma=False,
    )
```

```python
import functools
import math

import jax
import jax.numpy as jnp
from jax import lax
from jax.experimental import pallas as pl
from jax.experimental.pallas import tpu as pltpu
from jax.sharding import PartitionSpec as P

LAGS = 4096
LANES = 128
SUBLANES = 8
PARTS = 4


def split_bf16(values, parts):
    pieces = []
    for _ in range(parts - 1):
        piece = values.astype(jnp.bfloat16)
        pieces.append(piece)
        values = values - piece.astype(jnp.float32)
    pieces.append(values.astype(jnp.bfloat16))
    return pieces


def iota(shape, axis):
    return lax.broadcasted_iota(jnp.int32, shape, axis)


def dot(left, right):
    return jnp.dot(left, right, preferred_element_type=jnp.float32)


def padded(count, multiple):
    return -(-count // multiple) * multiple


def pick_slots(extras, places, me, stations, rounds, slots):
    groups = len(extras)
    pairs = stations * stations
    listed = rounds * pairs
    rows = rounds * groups * slots
    place = iota((groups, groups), 1)
    held_by = jnp.zeros((groups, groups), jnp.int32)
    for position in range(groups):
        held_by = jnp.where(place == position, places[position], held_by)
    lane = iota((1, listed), 1)

    def by_group(row, shift):
        wanted = (iota((groups, groups), 0) + groups - shift) % groups
        held = jnp.concatenate([extra[row : row + 1, :] for extra in extras], axis=0)
        return dot((held_by == wanted).astype(jnp.bfloat16), held.astype(jnp.bfloat16))

    def of_station(values, number):
        spread = iota((LANES, listed), 0) == number
        return dot(values.astype(jnp.bfloat16), spread.astype(jnp.bfloat16))

    owner_ids = jnp.zeros((groups, listed), jnp.float32)
    partner_mask = jnp.zeros((groups, listed), jnp.float32)
    for index in range(rounds):
        of_round = lane // pairs == index
        owner_ids = jnp.where(of_round, by_group(index, 0), owner_ids)
        second = of_station(by_group(rounds, index + 1), lane % stations)
        partner_mask = jnp.where(of_round, second, partner_mask)
    own_mask = of_station(by_group(rounds, 0), lane % pairs // stations)
    pair_weight = own_mask * partner_mask
    mine = owner_ids == me.astype(jnp.float32)
    from_pair, to_pair = iota((listed, listed), 0), iota((listed, listed), 1)
    before = (from_pair < to_pair) & (from_pair // pairs == to_pair // pairs)
    rank = dot(mine.astype(jnp.bfloat16), before.astype(jnp.bfloat16))
    marked = jnp.where(mine, rank, -1.0).astype(jnp.bfloat16)
    of_group = (iota((rows, groups), 0) // slots) % groups == iota((rows, groups), 1)
    of_group = of_group.astype(jnp.bfloat16)
    row_id, lane_id = iota((rows, listed), 0), iota((rows, listed), 1)
    chosen = (dot(of_group, marked) == (row_id % slots).astype(jnp.float32)) & (
        row_id // (groups * slots) == lane_id // pairs
    )
    weighed = jnp.where(chosen, dot(of_group, pair_weight.astype(jnp.bfloat16)), 0.0)
    weight = dot(weighed.astype(jnp.bfloat16), jnp.ones((listed, LANES), jnp.bfloat16))
    chosen = chosen.astype(jnp.bfloat16)
    pair_id = iota((listed, LANES), 0) % pairs
    first = dot(chosen, (pair_id // stations).astype(jnp.bfloat16))
    second = dot(chosen, (pair_id % stations).astype(jnp.bfloat16))
    return first.astype(jnp.int32), second.astype(jnp.int32), weight


def make_tables(bands_ref, place, table_refs, turn_refs, base_refs, bin_total):
    near_cos, near_sin = base_refs
    fine, half_band = near_cos.shape
    steps, chunks, _ = turn_refs[0].shape
    band_bins = chunks * LANES

    def circle(turns):
        angles = (turns & (4 * bin_total - 1)).astype(jnp.float32) * (math.pi / (2 * bin_total))
        return jnp.cos(angles), jnp.sin(angles)

    def every(count, start, step):
        bins = start + iota((count, half_band), 0) * step
        return circle(bins * (2 * iota((count, half_band), 1) + 1))

    def added(cos, sin, other_cos, other_sin):
        return cos * other_cos - sin * other_sin, sin * other_cos + cos * other_sin

    low_cos, low_sin = every(SUBLANES, 0, 1)
    high_cos, high_sin = every(fine // SUBLANES, 0, SUBLANES)
    for index in range(fine // SUBLANES):
        rows, one = slice(index * SUBLANES, (index + 1) * SUBLANES), slice(index, index + 1)
        near_cos[rows, :], near_sin[rows, :] = added(
            high_cos[one], high_sin[one], low_cos, low_sin
        )

    centre = 2 * half_band * (2 * place + 1) - 1 - LAGS
    norm = 1.0 / math.sqrt(bin_total)
    for step in range(steps):
        start = bands_ref[step] * band_bins
        cos, sin = every(band_bins // fine, start, fine)
        for part in range(band_bins // fine):
            one = slice(part, part + 1)
            values = added(cos[one], sin[one], near_cos[...], near_sin[...])
            rows = slice(step * band_bins + part * fine, step * band_bins + (part + 1) * fine)
            for table, value in zip(table_refs, values):
                table[rows, :half_band], table[rows, half_band:] = split_bf16(value, 2)
        bins = start + iota((chunks, LANES), 0) * LANES + iota((chunks, LANES), 1)
        for turn, value in zip(turn_refs, circle(bins * centre)):
            turn[step] = value * norm


def near_tables(bin_total, bands_ref, me_ref, owners_hbm, mask_hbm, *refs):
    table_refs, turn_refs, extras = refs[:2], refs[2:4], refs[4]
    base_refs, (owners_ref, mask_ref, sems) = refs[5:7], refs[7:]
    copies = [
        pltpu.make_async_copy(owners_hbm, owners_ref, sems.at[0]),
        pltpu.make_async_copy(mask_hbm, mask_ref, sems.at[1]),
    ]
    for copy in copies:
        copy.start()
    make_tables(bands_ref, me_ref[1], table_refs, turn_refs, base_refs, bin_total)
    for copy in copies:
        copy.wait()
    extras[...] = jnp.zeros_like(extras)
    rounds, pairs = owners_ref.shape[1], owners_ref.shape[3]
    for index in range(rounds):
        lanes = slice(index * pairs, (index + 1) * pairs)
        extras[index : index + 1, lanes] = owners_ref[0, index].astype(jnp.float32)
    extras[rounds : rounds + 1, : mask_ref.shape[1]] = mask_ref[...].astype(jnp.float32)


def far_tables(bin_total, bands_ref, me_ref, *refs):
    make_tables(bands_ref, me_ref[1], refs[:2], refs[2:4], refs[4:], bin_total)


def add_bands(sizes, steps, places, turn_refs, table_refs, blocks, picks, sums, scratch):
    groups, stations, rounds, slots, band_bins = sizes
    chunks = band_bins // LANES
    depth = 2 * chunks * stations
    half = sums[0].shape[1]
    first, second = picks
    sets = [scratch[6 * index : 6 * (index + 1)] for index in range(2)]
    part_groups = [range(part * groups // PARTS, (part + 1) * groups // PARTS) for part in range(PARTS)]
    bins_at_once = max(band_bins // 2, LANES)
    pieces = [(which, start) for which in range(2) for start in range(0, band_bins, bins_at_once)]

    def prepare(index):
        (step, place_step), (held, turned) = steps[index], sets[index % 2][:2]
        for position, (ref, offset) in enumerate(blocks):
            group = places[position]
            for q in range(chunks):
                turn_cos, turn_sin = [turn[step, q : q + 1, :] for turn in turn_refs]
                start = offset + place_step * depth + q * stations
                real = ref[start : start + stations, :]
                start += chunks * stations
                imag = ref[start : start + stations, :]
                held[group, q] = real
                held[group, chunks + q] = imag
                turned[group, q] = real * turn_cos + imag * turn_sin
                turned[group, chunks + q] = imag * turn_cos - real * turn_sin

    def multiply(index, part):
        held, turned, *cross = sets[index % 2]
        for group in part_groups[part]:
            sources = []
            for number in range(rounds):
                start = (number * groups + group) * slots
                lines = [slice(start + o, start + o + SUBLANES) for o in range(0, slots, SUBLANES)]
                partner = (group + groups - 1 - number) % groups
                sources.append((start, partner, [(first[line, :], second[line, :]) for line in lines]))
            for q in range(chunks):
                lanes = slice(q * LANES, (q + 1) * LANES)
                own_real, own_imag = held[group, q], held[group, chunks + q]
                for start, partner, indices in sources:
                    real, imag = turned[partner, q], turned[partner, chunks + q]
                    reals, imags = [], []
                    for index_a, index_b in indices:
                        a_real = jnp.take_along_axis(own_real, index_a, axis=0)
                        a_imag = jnp.take_along_axis(own_imag, index_a, axis=0)
                        b_real = jnp.take_along_axis(real, index_b, axis=0)
                        b_imag = jnp.take_along_axis(imag, index_b, axis=0)
                        reals.append(a_real * b_real + a_imag * b_imag)
                        imags.append(a_imag * b_real - a_real * b_imag)
                    rows = slice(start, start + slots)
                    for place, values in ((0, reals), (2, imags)):
                        high, low = split_bf16(jnp.concatenate(values, axis=0), 2)
                        cross[place][rows, lanes] = high
                        cross[place + 1][rows, lanes] = low

    def transform(index, which, start):
        step, (high, low) = steps[index][0], sets[index % 2][2 + 2 * which : 4 + 2 * which]
        lanes = slice(start, start + bins_at_once)
        bins = slice(step * band_bins + start, step * band_bins + start + bins_at_once)
        table, total = table_refs[which], sums[which]
        by_high = dot(high[:, lanes], table[bins, :])
        by_low = dot(low[:, lanes], table[bins, :half])
        total[...] += by_high[:, :half] + (by_high[:, half:] + by_low)

    prepare(0)
    for part in range(PARTS):
        multiply(0, part)
    for index in range(len(steps)):
        more = index + 1 < len(steps)
        if more:
            prepare(index + 1)
        for part in range(PARTS):
            if more:
                multiply(index + 1, part)
            if part < len(pieces):
                transform(index, *pieces[part])


def placed_blocks(array_refs, layout, me, groups):
    blocks = [(array_refs[index], offset) for index, offset, _ in layout]
    return blocks, [moved(me, move, groups) for _, _, move in layout]


def near_kernel(sizes, layout, array_count, depth, steps, me_ref, *refs):
    groups, stations, rounds, slots = sizes[:4]
    turn_refs, table_refs, refs = refs[:2], refs[2:4], refs[4:]
    array_refs, refs = refs[:array_count], refs[array_count:]
    (first, second, weight, even, odd), scratch = refs[:5], refs[5:]
    blocks, places = placed_blocks(array_refs, layout, me_ref[0], groups)
    extras = [ref[offset + depth : offset + depth + SUBLANES, :] for ref, offset in blocks]
    first[...], second[...], weight[...] = pick_slots(
        extras, places, me_ref[0], stations, rounds, slots
    )
    even[...] = jnp.zeros_like(even)
    odd[...] = jnp.zeros_like(odd)
    add_bands(
        sizes, steps, places, turn_refs, table_refs, blocks, (first, second), (even, odd), scratch
    )


def next_kernel(sizes, layout, array_count, steps, me_ref, *refs):
    turn_refs, table_refs, refs = refs[:2], refs[2:4], refs[4:]
    array_refs, refs = refs[:array_count], refs[array_count:]
    (first, second, even_in, odd_in, even, odd), scratch = refs[:6], refs[6:]
    even[...] = even_in[...]
    odd[...] = odd_in[...]
    blocks, places = placed_blocks(array_refs, layout, me_ref[0], sizes[0])
    add_bands(
        sizes, steps, places, turn_refs, table_refs, blocks, (first, second), (even, odd), scratch
    )


def last_kernel(sizes, layout, array_count, steps, me_ref, *refs):
    turn_refs, table_refs, refs = refs[:2], refs[2:4], refs[4:]
    array_refs, refs = refs[:array_count], refs[array_count:]
    first, second, even_in, odd_in, weight, out_ref, even, odd, above, below, sems = refs[:11]
    even[...] = even_in[...]
    odd[...] = odd_in[...]
    blocks, places = placed_blocks(array_refs, layout, me_ref[0], sizes[0])
    add_bands(
        sizes, steps, places, turn_refs, table_refs, blocks, (first, second), (even, odd), refs[11:]
    )
    half = even.shape[1]
    row_weight = weight[:, 0:1]
    mirror = (iota((half, half), 0) + iota((half, half), 1) == half - 1).astype(jnp.bfloat16)

    def mirrored():
        pieces = [dot(piece, mirror) for piece in split_bf16((even[...] + odd[...]) * row_weight, 3)]
        return pieces[0] + (pieces[1] + pieces[2])

    if half % LANES:
        above[:, half:] = (even[...] - odd[...]) * row_weight
        above[:, :half] = mirrored()
        copies = [pltpu.make_async_copy(above, out_ref, sems.at[0])]
        copies[0].start()
    else:
        above[...] = (even[...] - odd[...]) * row_weight
        copies = [pltpu.make_async_copy(above, out_ref.at[:, half:], sems.at[0])]
        copies[0].start()
        below[...] = mirrored()
        copies.append(pltpu.make_async_copy(below, out_ref.at[:, :half], sems.at[1]))
        copies[1].start()
    for copy in copies:
        copy.wait()


def moved(me, move, size):
    return me ^ move if size & (size - 1) == 0 else lax.rem(me + size - move, size)


def moved_index(me, move, size):
    return me ^ move if size & (size - 1) == 0 else (me - move) % size


def fetched(block, group_move, band_move):
    groups, shards = lax.axis_size("grp"), lax.axis_size("freq")
    route = [
        (
            moved_index(group, group_move, groups) * shards + moved_index(band, band_move, shards),
            group * shards + band,
        )
        for group in range(groups)
        for band in range(shards)
    ]
    return lax.ppermute(block, ("grp", "freq"), route)


def exchange(column, depth, parts, ready):
    groups = lax.axis_size("grp")
    if groups != 4:
        near = [column] + [fetched(column, move, 0) for move in range(1, groups)]
        layout = [(move, 0, move) for move in range(groups)]
        fars = [
            [fetched(column[first * depth : last * depth], move, 1) for move in range(groups)]
            for first, last in parts
        ]
        return near, layout, fars, ready
    across, *ready = lax.optimization_barrier((fetched(column, 2, 0), *ready))
    near = jnp.concatenate([column, across], axis=0)
    near = [near, fetched(near, 1, 0)]
    fars = []
    for first, last in parts:
        rows = slice(first * depth, last * depth)
        fars.append([fetched(jnp.concatenate([column[rows], across[rows]], axis=0), 0, 1)])
    return near, two_columns(column.shape[0]), fars, ready


def two_columns(rows):
    return [(0, 0, 0), (0, rows, 2), (1, 0, 1), (1, rows, 3)]


def across_cores(far):
    if lax.axis_size("grp") != 4:
        return far, [(move, 0, move) for move in range(len(far))]
    return [far[0], fetched(far[0], 1, 0)], two_columns(far[0].shape[0] // 2)


def per_device(spectra, station_mask, owners):
    stations, _, band_bins = spectra.shape
    groups = lax.axis_size("grp")
    shards = lax.axis_size("freq")
    rounds = owners.shape[1]
    pairs = stations * stations
    bin_total = band_bins * shards
    capacity = (2 * pairs + groups - 1) // groups
    slots = padded(capacity, 2 * SUBLANES)
    lag_band = LAGS // shards
    half_band = lag_band // 2
    chunks = band_bins // LANES
    rows = rounds * groups * slots

    scalar = pl.BlockSpec(memory_space=pltpu.SMEM)
    vector = pl.BlockSpec(memory_space=pltpu.VMEM)
    in_hbm = pl.BlockSpec(memory_space=pltpu.HBM)

    def call(kernel, name, scalars, arrays, out_shape, scratch, cost, others=()):
        arrays = [pltpu.with_memory_space_constraint(array, pltpu.VMEM) for array in arrays]
        others = [pltpu.with_memory_space_constraint(array, pltpu.HBM) for array in others]
        to_hbm = isinstance(out_shape, jax.ShapeDtypeStruct)
        return pl.pallas_call(
            kernel,
            out_shape=out_shape,
            in_specs=[scalar] * len(scalars) + [in_hbm] * len(others) + [vector] * len(arrays),
            out_specs=in_hbm if to_hbm else [vector] * len(out_shape),
            scratch_shapes=scratch,
            compiler_params=pltpu.CompilerParams(vmem_limit_bytes=24 * 1024 * 1024),
            cost_estimate=cost,
            name=name,
        )(*scalars, *others, *arrays)

    steps = shards // 2
    me = jnp.stack([lax.axis_index("grp"), lax.axis_index("freq")]).astype(jnp.int32)
    near_bands = me[1] ^ jnp.arange(0, shards, 2, dtype=jnp.int32)
    tiles = spectra.reshape(stations, 2, chunks, LANES).transpose(1, 2, 0, 3)
    tiles = tiles.reshape(2 * chunks * stations, LANES)
    column = [tiles] + [fetched(tiles, 0, move) for move in range(2, shards, 2)]

    table = pltpu.VMEM((steps * band_bins, lag_band), jnp.bfloat16)
    turn = pltpu.VMEM((steps, chunks, LANES), jnp.float32)
    base = pltpu.VMEM((64, half_band), jnp.float32)
    table_cost = pl.CostEstimate(
        flops=0, bytes_accessed=4 * bin_total * half_band, transcendentals=0
    )
    *near_table, extras = call(
        functools.partial(near_tables, bin_total),
        "near_tables",
        [near_bands, me],
        [],
        [table] * 2 + [turn] * 2 + [pltpu.VMEM((SUBLANES, LANES), jnp.float32)],
        [base] * 2
        + [
            pltpu.VMEM((1, rounds, 1, pairs), jnp.int32),
            pltpu.VMEM((1, stations), jnp.int32),
            pltpu.SemaphoreType.DMA((2,)),
        ],
        table_cost,
        [owners.transpose(0, 1, 3, 2), station_mask.reshape(1, stations)],
    )
    column = jnp.concatenate(column + [extras], axis=0)
    column, far_bands = lax.optimization_barrier((column, near_bands ^ 1))
    far_table = call(
        functools.partial(far_tables, bin_total),
        "far_tables",
        [far_bands, me],
        [],
        [table] * 2 + [turn] * 2,
        [base] * 2,
        table_cost,
    )
    depth = 2 * chunks * stations
    parts = [(0, steps // 2), (steps // 2, steps)]
    near, layout, fars, far_table = exchange(column, depth, parts, far_table)

    sizes = (groups, stations, rounds, slots, band_bins)
    spectrum = pltpu.VMEM((groups, 2 * chunks, stations, LANES), jnp.float32)
    cross = pltpu.VMEM((rows, band_bins), jnp.bfloat16)
    scratch = ([spectrum] * 2 + [cross] * 4) * 2

    def cost(count):
        flops = 6 * rows * band_bins * lag_band * count
        return pl.CostEstimate(flops=flops, bytes_accessed=2 * 1024 * 1024, transcendentals=0)

    total = pltpu.VMEM((rows, half_band), jnp.float32)
    half_result = total if half_band % LANES == 0 else pltpu.VMEM((rows, lag_band), jnp.float32)
    index = pltpu.VMEM((rows, LANES), jnp.int32)
    near_table = [near_table[place] for place in (2, 3, 0, 1)]
    far_table = [far_table[place] for place in (2, 3, 0, 1)]

    def more(name, layout, arrays, tables, first_step, last_step, place_step, sums):
        some = [(step, step - place_step) for step in range(first_step, last_step)]
        return call(
            functools.partial(next_kernel, sizes, layout, len(arrays), some),
            name,
            [me],
            [*tables, *arrays, first, second, *sums],
            [total] * 2,
            scratch,
            cost(len(some)),
        )

    split = steps - steps // 4
    first, second, weight, even, odd = call(
        functools.partial(
            near_kernel, sizes, layout, len(near), steps * depth, [(i, i) for i in range(split)]
        ),
        "near_first",
        [me],
        near_table + near,
        [index] * 2 + [pltpu.VMEM((rows, LANES), jnp.float32)] + [total] * 2,
        scratch,
        cost(split),
    )
    *far, even = lax.optimization_barrier((*fars[0], even))
    far, far_layout = across_cores(far)
    even, odd = more("near_next", layout, near, near_table, split, steps, 0, (even, odd))
    *last, even = lax.optimization_barrier((*fars[1], even))
    last, _ = across_cores(last)
    even, odd = more("far_first", far_layout, far, far_table, *parts[0], 0, (even, odd))
    some = [(step, step - parts[1][0]) for step in range(*parts[1])]
    out = call(
        functools.partial(last_kernel, sizes, far_layout, len(last), some),
        "far_next",
        [me],
        [*far_table, *last, first, second, even, odd, weight],
        jax.ShapeDtypeStruct((rows, lag_band), jnp.float32),
        [total] * 2 + [half_result] * 2 + [pltpu.SemaphoreType.DMA((2,))] + scratch,
        cost(len(some)),
    )
    out = out.reshape(1, rounds, groups, slots, lag_band)
    return out[:, :, :, :capacity]


def solution(mesh):
    placed = (P("grp", None, "freq"), P("grp"), P("grp", None, None, None))
    return jax.shard_map(
        per_device,
        mesh=mesh,
        in_specs=placed,
        out_specs=P("grp", None, None, None, "freq"),
        check_vma=False,
    )
```

```python
import functools
import math

import jax
import jax.numpy as jnp
from jax import lax
from jax.experimental import pallas as pl
from jax.experimental.pallas import tpu as pltpu
from jax.sharding import PartitionSpec as P

LAGS = 4096
LANES = 128
SUBLANES = 8
PARTS = 4


def split_bf16(values, parts):
    pieces = []
    for _ in range(parts - 1):
        piece = values.astype(jnp.bfloat16)
        pieces.append(piece)
        values = values - piece.astype(jnp.float32)
    pieces.append(values.astype(jnp.bfloat16))
    return pieces


def iota(shape, axis):
    return lax.broadcasted_iota(jnp.int32, shape, axis)


def dot(left, right):
    return jnp.dot(left, right, preferred_element_type=jnp.float32)


def padded(count, multiple):
    return -(-count // multiple) * multiple


def pick_slots(extras, places, me, stations, rounds, slots):
    groups = len(extras)
    pairs = stations * stations
    listed = rounds * pairs
    rows = rounds * groups * slots
    place = iota((groups, groups), 1)
    held_by = jnp.zeros((groups, groups), jnp.int32)
    for position in range(groups):
        held_by = jnp.where(place == position, places[position], held_by)
    lane = iota((1, listed), 1)

    def by_group(row, shift):
        wanted = (iota((groups, groups), 0) + groups - shift) % groups
        held = jnp.concatenate([extra[row : row + 1, :] for extra in extras], axis=0)
        return dot((held_by == wanted).astype(jnp.bfloat16), held.astype(jnp.bfloat16))

    def of_station(values, number):
        spread = iota((LANES, listed), 0) == number
        return dot(values.astype(jnp.bfloat16), spread.astype(jnp.bfloat16))

    owner_ids = jnp.zeros((groups, listed), jnp.float32)
    partner_mask = jnp.zeros((groups, listed), jnp.float32)
    for index in range(rounds):
        of_round = lane // pairs == index
        owner_ids = jnp.where(of_round, by_group(index, 0), owner_ids)
        second = of_station(by_group(rounds, index + 1), lane % stations)
        partner_mask = jnp.where(of_round, second, partner_mask)
    own_mask = of_station(by_group(rounds, 0), lane % pairs // stations)
    pair_weight = own_mask * partner_mask
    mine = owner_ids == me.astype(jnp.float32)
    from_pair, to_pair = iota((listed, listed), 0), iota((listed, listed), 1)
    before = (from_pair < to_pair) & (from_pair // pairs == to_pair // pairs)
    rank = dot(mine.astype(jnp.bfloat16), before.astype(jnp.bfloat16))
    marked = jnp.where(mine, rank, -1.0).astype(jnp.bfloat16)
    of_group = (iota((rows, groups), 0) // slots) % groups == iota((rows, groups), 1)
    of_group = of_group.astype(jnp.bfloat16)
    row_id, lane_id = iota((rows, listed), 0), iota((rows, listed), 1)
    chosen = (dot(of_group, marked) == (row_id % slots).astype(jnp.float32)) & (
        row_id // (groups * slots) == lane_id // pairs
    )
    weighed = jnp.where(chosen, dot(of_group, pair_weight.astype(jnp.bfloat16)), 0.0)
    weight = dot(weighed.astype(jnp.bfloat16), jnp.ones((listed, LANES), jnp.bfloat16))
    chosen = chosen.astype(jnp.bfloat16)
    pair_id = iota((listed, LANES), 0) % pairs
    first = dot(chosen, (pair_id // stations).astype(jnp.bfloat16))
    second = dot(chosen, (pair_id % stations).astype(jnp.bfloat16))
    return first.astype(jnp.int32), second.astype(jnp.int32), weight


def make_tables(bands_ref, place, table_refs, turn_refs, base_refs, bin_total):
    near_cos, near_sin = base_refs
    fine, half_band = near_cos.shape
    steps, chunks, _ = turn_refs[0].shape
    band_bins = chunks * LANES

    def circle(turns):
        angles = (turns & (4 * bin_total - 1)).astype(jnp.float32) * (math.pi / (2 * bin_total))
        return jnp.cos(angles), jnp.sin(angles)

    def every(count, start, step):
        bins = start + iota((count, half_band), 0) * step
        return circle(bins * (2 * iota((count, half_band), 1) + 1))

    def added(cos, sin, other_cos, other_sin):
        return cos * other_cos - sin * other_sin, sin * other_cos + cos * other_sin

    low_cos, low_sin = every(SUBLANES, 0, 1)
    high_cos, high_sin = every(fine // SUBLANES, 0, SUBLANES)
    for index in range(fine // SUBLANES):
        rows, one = slice(index * SUBLANES, (index + 1) * SUBLANES), slice(index, index + 1)
        near_cos[rows, :], near_sin[rows, :] = added(
            high_cos[one], high_sin[one], low_cos, low_sin
        )

    centre = 2 * half_band * (2 * place + 1) - 1 - LAGS
    norm = 1.0 / math.sqrt(bin_total)
    for step in range(steps):
        start = bands_ref[step] * band_bins
        cos, sin = every(band_bins // fine, start, fine)
        for part in range(band_bins // fine):
            one = slice(part, part + 1)
            values = added(cos[one], sin[one], near_cos[...], near_sin[...])
            rows = slice(step * band_bins + part * fine, step * band_bins + (part + 1) * fine)
            for table, value in zip(table_refs, values):
                table[rows, :half_band], table[rows, half_band:] = split_bf16(value, 2)
        bins = start + iota((chunks, LANES), 0) * LANES + iota((chunks, LANES), 1)
        for turn, value in zip(turn_refs, circle(bins * centre)):
            turn[step] = value * norm


def near_tables(bin_total, bands_ref, me_ref, owners_hbm, mask_hbm, *refs):
    table_refs, turn_refs, extras = refs[:2], refs[2:4], refs[4]
    base_refs, (owners_ref, mask_ref, sems) = refs[5:7], refs[7:]
    copies = [
        pltpu.make_async_copy(owners_hbm, owners_ref, sems.at[0]),
        pltpu.make_async_copy(mask_hbm, mask_ref, sems.at[1]),
    ]
    for copy in copies:
        copy.start()
    make_tables(bands_ref, me_ref[1], table_refs, turn_refs, base_refs, bin_total)
    for copy in copies:
        copy.wait()
    extras[...] = jnp.zeros_like(extras)
    rounds, pairs = owners_ref.shape[1], owners_ref.shape[3]
    for index in range(rounds):
        lanes = slice(index * pairs, (index + 1) * pairs)
        extras[index : index + 1, lanes] = owners_ref[0, index].astype(jnp.float32)
    extras[rounds : rounds + 1, : mask_ref.shape[1]] = mask_ref[...].astype(jnp.float32)


def far_tables(bin_total, bands_ref, me_ref, *refs):
    make_tables(bands_ref, me_ref[1], refs[:2], refs[2:4], refs[4:], bin_total)


def add_bands(sizes, steps, places, turn_refs, table_refs, blocks, picks, sums, scratch):
    groups, stations, rounds, slots, band_bins = sizes
    chunks = band_bins // LANES
    depth = 2 * chunks * stations
    half = sums[0].shape[1]
    first, second = picks
    sets = [scratch[6 * index : 6 * (index + 1)] for index in range(2)]
    part_groups = [range(part * groups // PARTS, (part + 1) * groups // PARTS) for part in range(PARTS)]
    bins_at_once = max(band_bins // 2, LANES)
    pieces = [(which, start) for which in range(2) for start in range(0, band_bins, bins_at_once)]

    def prepare(index):
        (step, place_step), (held, turned) = steps[index], sets[index % 2][:2]
        for position, (ref, offset) in enumerate(blocks):
            group = places[position]
            for q in range(chunks):
                turn_cos, turn_sin = [turn[step, q : q + 1, :] for turn in turn_refs]
                start = offset + place_step * depth + q * stations
                real = ref[start : start + stations, :]
                start += chunks * stations
                imag = ref[start : start + stations, :]
                held[group, q] = real
                held[group, chunks + q] = imag
                turned[group, q] = real * turn_cos + imag * turn_sin
                turned[group, chunks + q] = imag * turn_cos - real * turn_sin

    def multiply(index, part):
        held, turned, *cross = sets[index % 2]
        for group in part_groups[part]:
            sources = []
            for number in range(rounds):
                start = (number * groups + group) * slots
                lines = [slice(start + o, start + o + SUBLANES) for o in range(0, slots, SUBLANES)]
                partner = (group + groups - 1 - number) % groups
                sources.append((start, partner, [(first[line, :], second[line, :]) for line in lines]))
            for q in range(chunks):
                lanes = slice(q * LANES, (q + 1) * LANES)
                own_real, own_imag = held[group, q], held[group, chunks + q]
                for start, partner, indices in sources:
                    real, imag = turned[partner, q], turned[partner, chunks + q]
                    reals, imags = [], []
                    for index_a, index_b in indices:
                        a_real = jnp.take_along_axis(own_real, index_a, axis=0)
                        a_imag = jnp.take_along_axis(own_imag, index_a, axis=0)
                        b_real = jnp.take_along_axis(real, index_b, axis=0)
                        b_imag = jnp.take_along_axis(imag, index_b, axis=0)
                        reals.append(a_real * b_real + a_imag * b_imag)
                        imags.append(a_imag * b_real - a_real * b_imag)
                    rows = slice(start, start + slots)
                    for place, values in ((0, reals), (2, imags)):
                        high, low = split_bf16(jnp.concatenate(values, axis=0), 2)
                        cross[place][rows, lanes] = high
                        cross[place + 1][rows, lanes] = low

    def transform(index, which, start):
        step, (high, low) = steps[index][0], sets[index % 2][2 + 2 * which : 4 + 2 * which]
        lanes = slice(start, start + bins_at_once)
        bins = slice(step * band_bins + start, step * band_bins + start + bins_at_once)
        table, total = table_refs[which], sums[which]
        by_high = dot(high[:, lanes], table[bins, :])
        by_low = dot(low[:, lanes], table[bins, :half])
        total[...] += by_high[:, :half] + (by_high[:, half:] + by_low)

    prepare(0)
    for part in range(PARTS):
        multiply(0, part)
    for index in range(len(steps)):
        more = index + 1 < len(steps)
        if more:
            prepare(index + 1)
        for part in range(PARTS):
            if more:
                multiply(index + 1, part)
            if part < len(pieces):
                transform(index, *pieces[part])


def placed_blocks(array_refs, layout, me, groups):
    blocks = [(array_refs[index], offset) for index, offset, _ in layout]
    return blocks, [moved(me, move, groups) for _, _, move in layout]


def near_kernel(sizes, layout, array_count, depth, steps, me_ref, *refs):
    groups, stations, rounds, slots = sizes[:4]
    turn_refs, table_refs, refs = refs[:2], refs[2:4], refs[4:]
    array_refs, refs = refs[:array_count], refs[array_count:]
    (first, second, weight, even, odd), scratch = refs[:5], refs[5:]
    blocks, places = placed_blocks(array_refs, layout, me_ref[0], groups)
    extras = [ref[offset + depth : offset + depth + SUBLANES, :] for ref, offset in blocks]
    first[...], second[...], weight[...] = pick_slots(
        extras, places, me_ref[0], stations, rounds, slots
    )
    even[...] = jnp.zeros_like(even)
    odd[...] = jnp.zeros_like(odd)
    add_bands(
        sizes, steps, places, turn_refs, table_refs, blocks, (first, second), (even, odd), scratch
    )


def next_kernel(sizes, layout, array_count, steps, me_ref, *refs):
    turn_refs, table_refs, refs = refs[:2], refs[2:4], refs[4:]
    array_refs, refs = refs[:array_count], refs[array_count:]
    (first, second, even_in, odd_in, even, odd), scratch = refs[:6], refs[6:]
    even[...] = even_in[...]
    odd[...] = odd_in[...]
    blocks, places = placed_blocks(array_refs, layout, me_ref[0], sizes[0])
    add_bands(
        sizes, steps, places, turn_refs, table_refs, blocks, (first, second), (even, odd), scratch
    )


def last_kernel(sizes, layout, array_count, steps, me_ref, *refs):
    turn_refs, table_refs, refs = refs[:2], refs[2:4], refs[4:]
    array_refs, refs = refs[:array_count], refs[array_count:]
    first, second, even_in, odd_in, weight, out_ref, even, odd, above, below, sems = refs[:11]
    even[...] = even_in[...]
    odd[...] = odd_in[...]
    blocks, places = placed_blocks(array_refs, layout, me_ref[0], sizes[0])
    add_bands(
        sizes, steps, places, turn_refs, table_refs, blocks, (first, second), (even, odd), refs[11:]
    )
    half = even.shape[1]
    row_weight = weight[:, 0:1]
    mirror = (iota((half, half), 0) + iota((half, half), 1) == half - 1).astype(jnp.bfloat16)

    def mirrored():
        pieces = [dot(piece, mirror) for piece in split_bf16((even[...] + odd[...]) * row_weight, 3)]
        return pieces[0] + (pieces[1] + pieces[2])

    if half % LANES:
        above[:, half:] = (even[...] - odd[...]) * row_weight
        above[:, :half] = mirrored()
        copies = [pltpu.make_async_copy(above, out_ref, sems.at[0])]
        copies[0].start()
    else:
        above[...] = (even[...] - odd[...]) * row_weight
        copies = [pltpu.make_async_copy(above, out_ref.at[:, half:], sems.at[0])]
        copies[0].start()
        below[...] = mirrored()
        copies.append(pltpu.make_async_copy(below, out_ref.at[:, :half], sems.at[1]))
        copies[1].start()
    for copy in copies:
        copy.wait()


def moved(me, move, size):
    return me ^ move if size & (size - 1) == 0 else lax.rem(me + size - move, size)


def moved_index(me, move, size):
    return me ^ move if size & (size - 1) == 0 else (me - move) % size


def fetched(block, group_move, band_move):
    groups, shards = lax.axis_size("grp"), lax.axis_size("freq")
    route = [
        (
            moved_index(group, group_move, groups) * shards + moved_index(band, band_move, shards),
            group * shards + band,
        )
        for group in range(groups)
        for band in range(shards)
    ]
    return lax.ppermute(block, ("grp", "freq"), route)


def exchange(column, ready):
    groups = lax.axis_size("grp")
    if groups != 4:
        near = [column] + [fetched(column, move, 0) for move in range(1, groups)]
        layout = [(move, 0, move) for move in range(groups)]
        far = [fetched(column, move, 1) for move in range(groups)]
        return near, layout, far, ready
    across, beside = fetched(column, 2, 0), fetched(column, 0, 1)
    across, beside, *ready = lax.optimization_barrier((across, beside, *ready))
    near = jnp.concatenate([column, across], axis=0)
    near = [near, fetched(near, 1, 0)]
    return near, two_columns(column.shape[0]), [beside, fetched(across, 0, 1)], ready


def two_columns(rows):
    return [(0, 0, 0), (0, rows, 2), (1, 0, 1), (1, rows, 3)]


def across_cores(far):
    if lax.axis_size("grp") != 4:
        return far
    far = jnp.concatenate(far, axis=0)
    return [far, fetched(far, 1, 0)]


def per_device(spectra, station_mask, owners):
    stations, _, band_bins = spectra.shape
    groups = lax.axis_size("grp")
    shards = lax.axis_size("freq")
    rounds = owners.shape[1]
    pairs = stations * stations
    bin_total = band_bins * shards
    capacity = (2 * pairs + groups - 1) // groups
    slots = padded(capacity, 2 * SUBLANES)
    lag_band = LAGS // shards
    half_band = lag_band // 2
    chunks = band_bins // LANES
    rows = rounds * groups * slots

    scalar = pl.BlockSpec(memory_space=pltpu.SMEM)
    vector = pl.BlockSpec(memory_space=pltpu.VMEM)
    in_hbm = pl.BlockSpec(memory_space=pltpu.HBM)

    def call(kernel, name, scalars, arrays, out_shape, scratch, cost, others=()):
        arrays = [pltpu.with_memory_space_constraint(array, pltpu.VMEM) for array in arrays]
        others = [pltpu.with_memory_space_constraint(array, pltpu.HBM) for array in others]
        to_hbm = isinstance(out_shape, jax.ShapeDtypeStruct)
        return pl.pallas_call(
            kernel,
            out_shape=out_shape,
            in_specs=[scalar] * len(scalars) + [in_hbm] * len(others) + [vector] * len(arrays),
            out_specs=in_hbm if to_hbm else [vector] * len(out_shape),
            scratch_shapes=scratch,
            compiler_params=pltpu.CompilerParams(vmem_limit_bytes=24 * 1024 * 1024),
            cost_estimate=cost,
            name=name,
        )(*scalars, *others, *arrays)

    steps = shards // 2
    me = jnp.stack([lax.axis_index("grp"), lax.axis_index("freq")]).astype(jnp.int32)
    near_bands = me[1] ^ jnp.arange(0, shards, 2, dtype=jnp.int32)
    tiles = spectra.reshape(stations, 2, chunks, LANES).transpose(1, 2, 0, 3)
    tiles = tiles.reshape(2 * chunks * stations, LANES)
    column = [tiles] + [fetched(tiles, 0, move) for move in range(2, shards, 2)]

    table = pltpu.VMEM((steps * band_bins, lag_band), jnp.bfloat16)
    turn = pltpu.VMEM((steps, chunks, LANES), jnp.float32)
    base = pltpu.VMEM((64, half_band), jnp.float32)
    table_cost = pl.CostEstimate(
        flops=0, bytes_accessed=4 * bin_total * half_band, transcendentals=0
    )
    *near_table, extras = call(
        functools.partial(near_tables, bin_total),
        "near_tables",
        [near_bands, me],
        [],
        [table] * 2 + [turn] * 2 + [pltpu.VMEM((SUBLANES, LANES), jnp.float32)],
        [base] * 2
        + [
            pltpu.VMEM((1, rounds, 1, pairs), jnp.int32),
            pltpu.VMEM((1, stations), jnp.int32),
            pltpu.SemaphoreType.DMA((2,)),
        ],
        table_cost,
        [owners.transpose(0, 1, 3, 2), station_mask.reshape(1, stations)],
    )
    column = jnp.concatenate(column + [extras], axis=0)
    column, far_bands = lax.optimization_barrier((column, near_bands ^ 1))
    far_table = call(
        functools.partial(far_tables, bin_total),
        "far_tables",
        [far_bands, me],
        [],
        [table] * 2 + [turn] * 2,
        [base] * 2,
        table_cost,
    )
    depth = 2 * chunks * stations
    near, layout, far, far_table = exchange(column, far_table)

    sizes = (groups, stations, rounds, slots, band_bins)
    spectrum = pltpu.VMEM((groups, 2 * chunks, stations, LANES), jnp.float32)
    cross = pltpu.VMEM((rows, band_bins), jnp.bfloat16)
    scratch = ([spectrum] * 2 + [cross] * 4) * 2

    def cost(count):
        flops = 6 * rows * band_bins * lag_band * count
        return pl.CostEstimate(flops=flops, bytes_accessed=2 * 1024 * 1024, transcendentals=0)

    total = pltpu.VMEM((rows, half_band), jnp.float32)
    half_result = total if half_band % LANES == 0 else pltpu.VMEM((rows, lag_band), jnp.float32)
    index = pltpu.VMEM((rows, LANES), jnp.int32)
    near_table = [near_table[place] for place in (2, 3, 0, 1)]
    far_table = [far_table[place] for place in (2, 3, 0, 1)]

    split = steps - steps // 4
    first, second, weight, even, odd = call(
        functools.partial(
            near_kernel, sizes, layout, len(near), steps * depth, [(i, i) for i in range(split)]
        ),
        "near_first",
        [me],
        near_table + near,
        [index] * 2 + [pltpu.VMEM((rows, LANES), jnp.float32)] + [total] * 2,
        scratch,
        cost(split),
    )
    *far, even = lax.optimization_barrier((*far, even))
    far = across_cores(far)
    even, odd = call(
        functools.partial(
            next_kernel, sizes, layout, len(near), [(i, i) for i in range(split, steps)]
        ),
        "near_next",
        [me],
        [*near_table, *near, first, second, even, odd],
        [total] * 2,
        scratch,
        cost(steps - split),
    )
    out = call(
        functools.partial(last_kernel, sizes, layout, len(far), [(i, i) for i in range(steps)]),
        "far_bands",
        [me],
        [*far_table, *far, first, second, even, odd, weight],
        jax.ShapeDtypeStruct((rows, lag_band), jnp.float32),
        [total] * 2 + [half_result] * 2 + [pltpu.SemaphoreType.DMA((2,))] + scratch,
        cost(steps),
    )
    out = out.reshape(1, rounds, groups, slots, lag_band)
    return out[:, :, :, :capacity]


def solution(mesh):
    placed = (P("grp", None, "freq"), P("grp"), P("grp", None, None, None))
    return jax.shard_map(
        per_device,
        mesh=mesh,
        in_specs=placed,
        out_specs=P("grp", None, None, None, "freq"),
        check_vma=False,
    )
```

```python
import functools
import math

import jax
import jax.numpy as jnp
from jax import lax
from jax.experimental import pallas as pl
from jax.experimental.pallas import tpu as pltpu
from jax.sharding import PartitionSpec as P

LAGS = 4096
LANES = 128
SUBLANES = 8
PARTS = 4


def split_bf16(values, parts):
    pieces = []
    for _ in range(parts - 1):
        piece = values.astype(jnp.bfloat16)
        pieces.append(piece)
        values = values - piece.astype(jnp.float32)
    pieces.append(values.astype(jnp.bfloat16))
    return pieces


def iota(shape, axis):
    return lax.broadcasted_iota(jnp.int32, shape, axis)


def dot(left, right):
    return jnp.dot(left, right, preferred_element_type=jnp.float32)


def padded(count, multiple):
    return -(-count // multiple) * multiple


def pick_slots(extras, places, me, stations, rounds, slots):
    groups = len(extras)
    pairs = stations * stations
    listed = rounds * pairs
    rows = rounds * groups * slots
    place = iota((groups, groups), 1)
    held_by = jnp.zeros((groups, groups), jnp.int32)
    for position in range(groups):
        held_by = jnp.where(place == position, places[position], held_by)
    lane = iota((1, listed), 1)

    def by_group(row, shift):
        wanted = (iota((groups, groups), 0) + groups - shift) % groups
        held = jnp.concatenate([extra[row : row + 1, :] for extra in extras], axis=0)
        return dot((held_by == wanted).astype(jnp.bfloat16), held.astype(jnp.bfloat16))

    def of_station(values, number):
        spread = iota((LANES, listed), 0) == number
        return dot(values.astype(jnp.bfloat16), spread.astype(jnp.bfloat16))

    owner_ids = jnp.zeros((groups, listed), jnp.float32)
    partner_mask = jnp.zeros((groups, listed), jnp.float32)
    for index in range(rounds):
        of_round = lane // pairs == index
        owner_ids = jnp.where(of_round, by_group(index, 0), owner_ids)
        second = of_station(by_group(rounds, index + 1), lane % stations)
        partner_mask = jnp.where(of_round, second, partner_mask)
    own_mask = of_station(by_group(rounds, 0), lane % pairs // stations)
    pair_weight = own_mask * partner_mask
    mine = owner_ids == me.astype(jnp.float32)
    from_pair, to_pair = iota((listed, listed), 0), iota((listed, listed), 1)
    before = (from_pair < to_pair) & (from_pair // pairs == to_pair // pairs)
    rank = dot(mine.astype(jnp.bfloat16), before.astype(jnp.bfloat16))
    marked = jnp.where(mine, rank, -1.0).astype(jnp.bfloat16)
    of_group = (iota((rows, groups), 0) // slots) % groups == iota((rows, groups), 1)
    of_group = of_group.astype(jnp.bfloat16)
    row_id, lane_id = iota((rows, listed), 0), iota((rows, listed), 1)
    chosen = (dot(of_group, marked) == (row_id % slots).astype(jnp.float32)) & (
        row_id // (groups * slots) == lane_id // pairs
    )
    weighed = jnp.where(chosen, dot(of_group, pair_weight.astype(jnp.bfloat16)), 0.0)
    weight = dot(weighed.astype(jnp.bfloat16), jnp.ones((listed, LANES), jnp.bfloat16))
    chosen = chosen.astype(jnp.bfloat16)
    pair_id = iota((listed, LANES), 0) % pairs
    first = dot(chosen, (pair_id // stations).astype(jnp.bfloat16))
    second = dot(chosen, (pair_id % stations).astype(jnp.bfloat16))
    return first.astype(jnp.int32), second.astype(jnp.int32), weight


def make_tables(bands_ref, place, table_refs, turn_refs, base_refs, bin_total):
    near_cos, near_sin = base_refs
    fine, half_band = near_cos.shape
    steps, chunks, _ = turn_refs[0].shape
    band_bins = chunks * LANES

    def circle(turns):
        angles = (turns & (4 * bin_total - 1)).astype(jnp.float32) * (math.pi / (2 * bin_total))
        return jnp.cos(angles), jnp.sin(angles)

    def every(count, start, step):
        bins = start + iota((count, half_band), 0) * step
        return circle(bins * (2 * iota((count, half_band), 1) + 1))

    def added(cos, sin, other_cos, other_sin):
        return cos * other_cos - sin * other_sin, sin * other_cos + cos * other_sin

    low_cos, low_sin = every(SUBLANES, 0, 1)
    high_cos, high_sin = every(fine // SUBLANES, 0, SUBLANES)
    for index in range(fine // SUBLANES):
        rows, one = slice(index * SUBLANES, (index + 1) * SUBLANES), slice(index, index + 1)
        near_cos[rows, :], near_sin[rows, :] = added(
            high_cos[one], high_sin[one], low_cos, low_sin
        )

    centre = 2 * half_band * (2 * place + 1) - 1 - LAGS
    norm = 1.0 / math.sqrt(bin_total)
    for step in range(steps):
        start = bands_ref[step] * band_bins
        cos, sin = every(band_bins // fine, start, fine)
        for part in range(band_bins // fine):
            one = slice(part, part + 1)
            values = added(cos[one], sin[one], near_cos[...], near_sin[...])
            rows = slice(step * band_bins + part * fine, step * band_bins + (part + 1) * fine)
            for table, value in zip(table_refs, values):
                table[rows, :half_band], table[rows, half_band:] = split_bf16(value, 2)
        bins = start + iota((chunks, LANES), 0) * LANES + iota((chunks, LANES), 1)
        for turn, value in zip(turn_refs, circle(bins * centre)):
            turn[step] = value * norm


def near_tables(bin_total, bands_ref, me_ref, owners_hbm, mask_hbm, *refs):
    table_refs, turn_refs, extras = refs[:2], refs[2:4], refs[4]
    base_refs, (owners_ref, mask_ref, sems) = refs[5:7], refs[7:]
    copies = [
        pltpu.make_async_copy(owners_hbm, owners_ref, sems.at[0]),
        pltpu.make_async_copy(mask_hbm, mask_ref, sems.at[1]),
    ]
    for copy in copies:
        copy.start()
    make_tables(bands_ref, me_ref[1], table_refs, turn_refs, base_refs, bin_total)
    for copy in copies:
        copy.wait()
    extras[...] = jnp.zeros_like(extras)
    rounds, pairs = owners_ref.shape[1], owners_ref.shape[3]
    for index in range(rounds):
        lanes = slice(index * pairs, (index + 1) * pairs)
        extras[index : index + 1, lanes] = owners_ref[0, index].astype(jnp.float32)
    extras[rounds : rounds + 1, : mask_ref.shape[1]] = mask_ref[...].astype(jnp.float32)


def far_tables(bin_total, bands_ref, me_ref, *refs):
    make_tables(bands_ref, me_ref[1], refs[:2], refs[2:4], refs[4:], bin_total)


def add_bands(sizes, steps, places, turn_refs, table_refs, blocks, picks, sums, scratch):
    groups, stations, rounds, slots, band_bins = sizes
    chunks = band_bins // LANES
    depth = 2 * chunks * stations
    half = sums[0].shape[1]
    first, second = picks
    sets = [scratch[6 * index : 6 * (index + 1)] for index in range(2)]
    part_groups = [range(part * groups // PARTS, (part + 1) * groups // PARTS) for part in range(PARTS)]
    bins_at_once = max(band_bins // 2, LANES)
    pieces = [(which, start) for which in range(2) for start in range(0, band_bins, bins_at_once)]

    def prepare(index):
        step, (held, turned) = steps[index], sets[index % 2][:2]
        for position, (ref, offset) in enumerate(blocks):
            group = places[position]
            for q in range(chunks):
                turn_cos, turn_sin = [turn[step, q : q + 1, :] for turn in turn_refs]
                start = offset + step * depth + q * stations
                real = ref[start : start + stations, :]
                start += chunks * stations
                imag = ref[start : start + stations, :]
                held[group, q] = real
                held[group, chunks + q] = imag
                turned[group, q] = real * turn_cos + imag * turn_sin
                turned[group, chunks + q] = imag * turn_cos - real * turn_sin

    def multiply(index, part):
        held, turned, *cross = sets[index % 2]
        for group in part_groups[part]:
            sources = []
            for number in range(rounds):
                start = (number * groups + group) * slots
                lines = [slice(start + o, start + o + SUBLANES) for o in range(0, slots, SUBLANES)]
                partner = (group + groups - 1 - number) % groups
                sources.append((start, partner, [(first[line, :], second[line, :]) for line in lines]))
            for q in range(chunks):
                lanes = slice(q * LANES, (q + 1) * LANES)
                own_real, own_imag = held[group, q], held[group, chunks + q]
                for start, partner, indices in sources:
                    real, imag = turned[partner, q], turned[partner, chunks + q]
                    reals, imags = [], []
                    for index_a, index_b in indices:
                        a_real = jnp.take_along_axis(own_real, index_a, axis=0)
                        a_imag = jnp.take_along_axis(own_imag, index_a, axis=0)
                        b_real = jnp.take_along_axis(real, index_b, axis=0)
                        b_imag = jnp.take_along_axis(imag, index_b, axis=0)
                        reals.append(a_real * b_real + a_imag * b_imag)
                        imags.append(a_imag * b_real - a_real * b_imag)
                    rows = slice(start, start + slots)
                    for place, values in ((0, reals), (2, imags)):
                        high, low = split_bf16(jnp.concatenate(values, axis=0), 2)
                        cross[place][rows, lanes] = high
                        cross[place + 1][rows, lanes] = low

    def transform(index, which, start):
        step, (high, low) = steps[index], sets[index % 2][2 + 2 * which : 4 + 2 * which]
        lanes = slice(start, start + bins_at_once)
        bins = slice(step * band_bins + start, step * band_bins + start + bins_at_once)
        table, total = table_refs[which], sums[which]
        by_high = dot(high[:, lanes], table[bins, :])
        by_low = dot(low[:, lanes], table[bins, :half])
        total[...] += by_high[:, :half] + (by_high[:, half:] + by_low)

    prepare(0)
    for part in range(PARTS):
        multiply(0, part)
    for index in range(len(steps)):
        more = index + 1 < len(steps)
        if more:
            prepare(index + 1)
        for part in range(PARTS):
            if more:
                multiply(index + 1, part)
            if part < len(pieces):
                transform(index, *pieces[part])


def placed_blocks(array_refs, layout, me, groups):
    blocks = [(array_refs[index], offset) for index, offset, _ in layout]
    return blocks, [moved(me, move, groups) for _, _, move in layout]


def pick_kernel(sizes, layout, array_count, me_ref, *refs):
    groups, stations, rounds, slots, _ = sizes
    blocks, places = placed_blocks(refs[:array_count], layout, me_ref[0], groups)
    extras = [ref[offset : offset + SUBLANES, :] for ref, offset in blocks]
    first, second, weight = refs[array_count:]
    first[...], second[...], weight[...] = pick_slots(
        extras, places, me_ref[0], stations, rounds, slots
    )


def band_kernel(sizes, layout, array_count, steps, is_start, me_ref, *refs):
    turn_refs, table_refs, refs = refs[:2], refs[2:4], refs[4:]
    array_refs, refs = refs[:array_count], refs[array_count:]
    picks, refs = refs[:2], refs[2:]
    sums_in, refs = ((), refs) if is_start else (refs[:2], refs[2:])
    sums, scratch = refs[:2], refs[2:]
    for place, total in enumerate(sums):
        total[...] = jnp.zeros_like(total) if is_start else sums_in[place][...]
    blocks, places = placed_blocks(array_refs, layout, me_ref[0], sizes[0])
    add_bands(sizes, steps, places, turn_refs, table_refs, blocks, picks, sums, scratch)


def last_kernel(sizes, layout, array_count, steps, me_ref, *refs):
    turn_refs, table_refs, refs = refs[:2], refs[2:4], refs[4:]
    array_refs, refs = refs[:array_count], refs[array_count:]
    first, second, even_in, odd_in, weight, out_ref, even, odd, above, below, sems = refs[:11]
    even[...] = even_in[...]
    odd[...] = odd_in[...]
    blocks, places = placed_blocks(array_refs, layout, me_ref[0], sizes[0])
    add_bands(
        sizes, steps, places, turn_refs, table_refs, blocks, (first, second), (even, odd), refs[11:]
    )
    half = even.shape[1]
    row_weight = weight[:, 0:1]
    mirror = (iota((half, half), 0) + iota((half, half), 1) == half - 1).astype(jnp.bfloat16)

    def mirrored():
        pieces = [dot(piece, mirror) for piece in split_bf16((even[...] + odd[...]) * row_weight, 3)]
        return pieces[0] + (pieces[1] + pieces[2])

    if half % LANES:
        above[:, half:] = (even[...] - odd[...]) * row_weight
        above[:, :half] = mirrored()
        copies = [pltpu.make_async_copy(above, out_ref, sems.at[0])]
        copies[0].start()
    else:
        above[...] = (even[...] - odd[...]) * row_weight
        copies = [pltpu.make_async_copy(above, out_ref.at[:, half:], sems.at[0])]
        copies[0].start()
        below[...] = mirrored()
        copies.append(pltpu.make_async_copy(below, out_ref.at[:, :half], sems.at[1]))
        copies[1].start()
    for copy in copies:
        copy.wait()


def moved(me, move, size):
    return me ^ move if size & (size - 1) == 0 else lax.rem(me + size - move, size)


def moved_index(me, move, size):
    return me ^ move if size & (size - 1) == 0 else (me - move) % size


def fetched(block, group_move, band_move):
    groups, shards = lax.axis_size("grp"), lax.axis_size("freq")
    route = [
        (
            moved_index(group, group_move, groups) * shards + moved_index(band, band_move, shards),
            group * shards + band,
        )
        for group in range(groups)
        for band in range(shards)
    ]
    return lax.ppermute(block, ("grp", "freq"), route)


def across_x(block):
    return [block, fetched(block, 2, 0)] if lax.axis_size("grp") == 4 else [block]


def across_cores(blocks):
    groups = lax.axis_size("grp")
    if groups != 4:
        arrays = blocks + [fetched(blocks[0], move, 0) for move in range(1, groups)]
        return arrays, [(move, 0, move) for move in range(groups)]
    rows = blocks[0].shape[0]
    both = blocks[0] if len(blocks) == 1 else jnp.concatenate(blocks, axis=0)
    layout = [(core, part * rows, 2 * part + core) for core in range(2) for part in range(len(blocks))]
    return [both, fetched(both, 1, 0)], layout


def per_device(spectra, station_mask, owners):
    stations, _, band_bins = spectra.shape
    groups = lax.axis_size("grp")
    shards = lax.axis_size("freq")
    rounds = owners.shape[1]
    pairs = stations * stations
    bin_total = band_bins * shards
    capacity = (2 * pairs + groups - 1) // groups
    slots = padded(capacity, 2 * SUBLANES)
    lag_band = LAGS // shards
    half_band = lag_band // 2
    chunks = band_bins // LANES
    rows = rounds * groups * slots

    scalar = pl.BlockSpec(memory_space=pltpu.SMEM)
    vector = pl.BlockSpec(memory_space=pltpu.VMEM)
    in_hbm = pl.BlockSpec(memory_space=pltpu.HBM)

    def call(kernel, name, scalars, arrays, out_shape, scratch, cost, others=()):
        arrays = [pltpu.with_memory_space_constraint(array, pltpu.VMEM) for array in arrays]
        others = [pltpu.with_memory_space_constraint(array, pltpu.HBM) for array in others]
        to_hbm = isinstance(out_shape, jax.ShapeDtypeStruct)
        return pl.pallas_call(
            kernel,
            out_shape=out_shape,
            in_specs=[scalar] * len(scalars) + [in_hbm] * len(others) + [vector] * len(arrays),
            out_specs=in_hbm if to_hbm else [vector] * len(out_shape),
            scratch_shapes=scratch,
            compiler_params=pltpu.CompilerParams(vmem_limit_bytes=24 * 1024 * 1024),
            cost_estimate=cost,
            name=name,
        )(*scalars, *others, *arrays)

    steps = shards // 2
    me = jnp.stack([lax.axis_index("grp"), lax.axis_index("freq")]).astype(jnp.int32)
    near_bands = me[1] ^ jnp.arange(0, shards, 2, dtype=jnp.int32)
    tiles = spectra.reshape(stations, 2, chunks, LANES).transpose(1, 2, 0, 3)
    tiles = tiles.reshape(2 * chunks * stations, LANES)
    column = [tiles] + [fetched(tiles, 0, move) for move in range(2, shards, 2)]

    table = pltpu.VMEM((steps * band_bins, lag_band), jnp.bfloat16)
    turn = pltpu.VMEM((steps, chunks, LANES), jnp.float32)
    base = pltpu.VMEM((64, half_band), jnp.float32)
    table_cost = pl.CostEstimate(
        flops=0, bytes_accessed=4 * bin_total * half_band, transcendentals=0
    )
    *near_table, extras = call(
        functools.partial(near_tables, bin_total),
        "near_tables",
        [near_bands, me],
        [],
        [table] * 2 + [turn] * 2 + [pltpu.VMEM((SUBLANES, LANES), jnp.float32)],
        [base] * 2
        + [
            pltpu.VMEM((1, rounds, 1, pairs), jnp.int32),
            pltpu.VMEM((1, stations), jnp.int32),
            pltpu.SemaphoreType.DMA((2,)),
        ],
        table_cost,
        [owners.transpose(0, 1, 3, 2), station_mask.reshape(1, stations)],
    )
    ahead = across_x(extras)
    column = jnp.concatenate(column, axis=0)
    column, far_bands, *ahead = lax.optimization_barrier((column, near_bands ^ 1, *ahead))
    far_table = call(
        functools.partial(far_tables, bin_total),
        "far_tables",
        [far_bands, me],
        [],
        [table] * 2 + [turn] * 2,
        [base] * 2,
        table_cost,
    )
    sizes = (groups, stations, rounds, slots, band_bins)
    index = pltpu.VMEM((rows, LANES), jnp.int32)
    ahead, layout = across_cores(ahead)
    picks = call(
        functools.partial(pick_kernel, sizes, layout, len(ahead)),
        "picks",
        [me],
        ahead,
        [index] * 2 + [pltpu.VMEM((rows, LANES), jnp.float32)],
        [],
        table_cost,
    )
    across, beside = across_x(column), fetched(column, 0, 1)
    across, beside, far_table, picks = lax.optimization_barrier((across, beside, far_table, picks))
    near, layout = across_cores(across)
    split, middle = steps - steps // 4, steps // 2
    depth = column.shape[0] // steps
    fars, layout_near = [], layout
    beside, _ = across_cores([beside])
    for start, stop in ((0, middle), (middle, steps)):
        rows_of = slice(start * depth, stop * depth)
        fars.append([fetched(source[rows_of], 0, 1) for source in across[1:]])

    spectrum = pltpu.VMEM((groups, 2 * chunks, stations, LANES), jnp.float32)
    cross = pltpu.VMEM((rows, band_bins), jnp.bfloat16)
    scratch = ([spectrum] * 2 + [cross] * 4) * 2

    def cost(count):
        flops = 6 * rows * band_bins * lag_band * count
        return pl.CostEstimate(flops=flops, bytes_accessed=2 * 1024 * 1024, transcendentals=0)

    total = pltpu.VMEM((rows, half_band), jnp.float32)
    half_result = total if half_band % LANES == 0 else pltpu.VMEM((rows, lag_band), jnp.float32)
    near_table = [near_table[place] for place in (2, 3, 0, 1)]
    far_table = [far_table[place] for place in (2, 3, 0, 1)]

    def add(name, layout, arrays, tables, some, sums):
        return call(
            functools.partial(band_kernel, sizes, layout, len(arrays), some, not sums),
            name,
            [me],
            [*tables, *arrays, *picks[:2], *sums],
            [total] * 2,
            scratch,
            cost(len(some)),
        )

    def far_blocks(diagonal, start):
        arrays = list(beside)
        layout = [(move, 0, move) for move in range(len(arrays))]
        for block in diagonal:
            layout += [(len(arrays) + core, -start * depth, 2 + core) for core in range(2)]
            arrays += across_cores([block])[0]
        return layout, arrays

    every = list(range(steps))
    even, odd = add("near_first", layout_near, near, near_table, every[:split], ())
    *diagonal, even = lax.optimization_barrier((*fars[0], even))
    layout, far = far_blocks(diagonal, 0)
    even, odd = add("near_next", layout_near, near, near_table, every[split:], (even, odd))
    *diagonal, even = lax.optimization_barrier((*fars[1], even))
    layout_last, last = far_blocks(diagonal, middle)
    even, odd = add("far_first", layout, far, far_table, every[:middle], (even, odd))
    out = call(
        functools.partial(last_kernel, sizes, layout_last, len(last), every[middle:]),
        "far_next",
        [me],
        [*far_table, *last, *picks[:2], even, odd, picks[2]],
        jax.ShapeDtypeStruct((rows, lag_band), jnp.float32),
        [total] * 2 + [half_result] * 2 + [pltpu.SemaphoreType.DMA((2,))] + scratch,
        cost(steps - middle),
    )
    out = out.reshape(1, rounds, groups, slots, lag_band)
    return out[:, :, :, :capacity]


def solution(mesh):
    placed = (P("grp", None, "freq"), P("grp"), P("grp", None, None, None))
    return jax.shard_map(
        per_device,
        mesh=mesh,
        in_specs=placed,
        out_specs=P("grp", None, None, None, "freq"),
        check_vma=False,
    )
```

```python
import functools
import math

import jax
import jax.numpy as jnp
from jax import lax
from jax.experimental import pallas as pl
from jax.experimental.pallas import tpu as pltpu
from jax.sharding import PartitionSpec as P

LAGS = 4096
LANES = 128
SUBLANES = 8
PARTS = 4


def split_bf16(values, parts):
    pieces = []
    for _ in range(parts - 1):
        piece = values.astype(jnp.bfloat16)
        pieces.append(piece)
        values = values - piece.astype(jnp.float32)
    pieces.append(values.astype(jnp.bfloat16))
    return pieces


def iota(shape, axis):
    return lax.broadcasted_iota(jnp.int32, shape, axis)


def dot(left, right):
    return jnp.dot(left, right, preferred_element_type=jnp.float32)


def padded(count, multiple):
    return -(-count // multiple) * multiple


def pick_slots(extras, places, me, stations, rounds, slots):
    groups = len(extras)
    pairs = stations * stations
    listed = rounds * pairs
    rows = rounds * groups * slots
    place = iota((groups, groups), 1)
    held_by = jnp.zeros((groups, groups), jnp.int32)
    for position in range(groups):
        held_by = jnp.where(place == position, places[position], held_by)
    lane = iota((1, listed), 1)

    def by_group(row, shift):
        wanted = (iota((groups, groups), 0) + groups - shift) % groups
        held = jnp.concatenate([extra[row : row + 1, :] for extra in extras], axis=0)
        return dot((held_by == wanted).astype(jnp.bfloat16), held.astype(jnp.bfloat16))

    def of_station(values, number):
        spread = iota((LANES, listed), 0) == number
        return dot(values.astype(jnp.bfloat16), spread.astype(jnp.bfloat16))

    owner_ids = jnp.zeros((groups, listed), jnp.float32)
    partner_mask = jnp.zeros((groups, listed), jnp.float32)
    for index in range(rounds):
        of_round = lane // pairs == index
        owner_ids = jnp.where(of_round, by_group(index, 0), owner_ids)
        second = of_station(by_group(rounds, index + 1), lane % stations)
        partner_mask = jnp.where(of_round, second, partner_mask)
    own_mask = of_station(by_group(rounds, 0), lane % pairs // stations)
    pair_weight = own_mask * partner_mask
    mine = owner_ids == me.astype(jnp.float32)
    from_pair, to_pair = iota((listed, listed), 0), iota((listed, listed), 1)
    before = (from_pair < to_pair) & (from_pair // pairs == to_pair // pairs)
    rank = dot(mine.astype(jnp.bfloat16), before.astype(jnp.bfloat16))
    marked = jnp.where(mine, rank, -1.0).astype(jnp.bfloat16)
    of_group = (iota((rows, groups), 0) // slots) % groups == iota((rows, groups), 1)
    of_group = of_group.astype(jnp.bfloat16)
    row_id, lane_id = iota((rows, listed), 0), iota((rows, listed), 1)
    chosen = (dot(of_group, marked) == (row_id % slots).astype(jnp.float32)) & (
        row_id // (groups * slots) == lane_id // pairs
    )
    weighed = jnp.where(chosen, dot(of_group, pair_weight.astype(jnp.bfloat16)), 0.0)
    weight = dot(weighed.astype(jnp.bfloat16), jnp.ones((listed, LANES), jnp.bfloat16))
    chosen = chosen.astype(jnp.bfloat16)
    pair_id = iota((listed, LANES), 0) % pairs
    first = dot(chosen, (pair_id // stations).astype(jnp.bfloat16))
    second = dot(chosen, (pair_id % stations).astype(jnp.bfloat16))
    return first.astype(jnp.int32), second.astype(jnp.int32), weight


def make_tables(parity, table_refs, turn_refs, base_refs, bin_total):
    place = lax.axis_index("freq").astype(jnp.int32)
    near_cos, near_sin = base_refs
    fine, half_band = near_cos.shape
    steps, chunks, _ = turn_refs[0].shape
    band_bins = chunks * LANES

    def circle(turns):
        angles = (turns & (4 * bin_total - 1)).astype(jnp.float32) * (math.pi / (2 * bin_total))
        return jnp.cos(angles), jnp.sin(angles)

    def every(count, start, step):
        bins = start + iota((count, half_band), 0) * step
        return circle(bins * (2 * iota((count, half_band), 1) + 1))

    def added(cos, sin, other_cos, other_sin):
        return cos * other_cos - sin * other_sin, sin * other_cos + cos * other_sin

    low_cos, low_sin = every(SUBLANES, 0, 1)
    high_cos, high_sin = every(fine // SUBLANES, 0, SUBLANES)
    for index in range(fine // SUBLANES):
        rows, one = slice(index * SUBLANES, (index + 1) * SUBLANES), slice(index, index + 1)
        near_cos[rows, :], near_sin[rows, :] = added(
            high_cos[one], high_sin[one], low_cos, low_sin
        )

    centre = 2 * half_band * (2 * place + 1) - 1 - LAGS
    norm = 1.0 / math.sqrt(bin_total)
    for step in range(steps):
        start = (place ^ (2 * step + parity)) * band_bins
        cos, sin = every(band_bins // fine, start, fine)
        for part in range(band_bins // fine):
            one = slice(part, part + 1)
            values = added(cos[one], sin[one], near_cos[...], near_sin[...])
            rows = slice(step * band_bins + part * fine, step * band_bins + (part + 1) * fine)
            for table, value in zip(table_refs, values):
                table[rows, :half_band], table[rows, half_band:] = split_bf16(value, 2)
        bins = start + iota((chunks, LANES), 0) * LANES + iota((chunks, LANES), 1)
        for turn, value in zip(turn_refs, circle(bins * centre)):
            turn[step] = value * norm


def near_tables(bin_total, owners_hbm, mask_hbm, *refs):
    table_refs, turn_refs, extras = refs[:2], refs[2:4], refs[4]
    base_refs, (owners_ref, mask_ref, sems) = refs[5:7], refs[7:]
    copies = [
        pltpu.make_async_copy(owners_hbm, owners_ref, sems.at[0]),
        pltpu.make_async_copy(mask_hbm, mask_ref, sems.at[1]),
    ]
    for copy in copies:
        copy.start()
    make_tables(0, table_refs, turn_refs, base_refs, bin_total)
    for copy in copies:
        copy.wait()
    extras[...] = jnp.zeros_like(extras)
    rounds, pairs = owners_ref.shape[1], owners_ref.shape[3]
    for index in range(rounds):
        lanes = slice(index * pairs, (index + 1) * pairs)
        extras[index : index + 1, lanes] = owners_ref[0, index].astype(jnp.float32)
    extras[rounds : rounds + 1, : mask_ref.shape[1]] = mask_ref[...].astype(jnp.float32)


def far_tables(bin_total, _, *refs):
    make_tables(1, refs[:2], refs[2:4], refs[4:], bin_total)


def add_bands(sizes, steps, places, turn_refs, table_refs, blocks, picks, sums, scratch):
    groups, stations, rounds, slots, band_bins = sizes
    chunks = band_bins // LANES
    depth = 2 * chunks * stations
    half = sums[0].shape[1]
    first, second = picks
    sets = [scratch[6 * index : 6 * (index + 1)] for index in range(2)]
    part_groups = [range(part * groups // PARTS, (part + 1) * groups // PARTS) for part in range(PARTS)]
    bins_at_once = max(band_bins // 2, LANES)
    pieces = [(which, start) for which in range(2) for start in range(0, band_bins, bins_at_once)]

    def prepare(index):
        (step, place_step), (held, turned) = steps[index], sets[index % 2][:2]
        for position, (ref, offset) in enumerate(blocks):
            group = places[position]
            for q in range(chunks):
                turn_cos, turn_sin = [turn[step, q : q + 1, :] for turn in turn_refs]
                start = offset + place_step * depth + q * stations
                real = ref[start : start + stations, :]
                start += chunks * stations
                imag = ref[start : start + stations, :]
                held[group, q] = real
                held[group, chunks + q] = imag
                turned[group, q] = real * turn_cos + imag * turn_sin
                turned[group, chunks + q] = imag * turn_cos - real * turn_sin

    def multiply(index, part):
        held, turned, *cross = sets[index % 2]
        for group in part_groups[part]:
            sources = []
            for number in range(rounds):
                start = (number * groups + group) * slots
                lines = [slice(start + o, start + o + SUBLANES) for o in range(0, slots, SUBLANES)]
                partner = (group + groups - 1 - number) % groups
                sources.append((start, partner, [(first[line, :], second[line, :]) for line in lines]))
            for q in range(chunks):
                lanes = slice(q * LANES, (q + 1) * LANES)
                own_real, own_imag = held[group, q], held[group, chunks + q]
                for start, partner, indices in sources:
                    real, imag = turned[partner, q], turned[partner, chunks + q]
                    reals, imags = [], []
                    for index_a, index_b in indices:
                        a_real = jnp.take_along_axis(own_real, index_a, axis=0)
                        a_imag = jnp.take_along_axis(own_imag, index_a, axis=0)
                        b_real = jnp.take_along_axis(real, index_b, axis=0)
                        b_imag = jnp.take_along_axis(imag, index_b, axis=0)
                        reals.append(a_real * b_real + a_imag * b_imag)
                        imags.append(a_imag * b_real - a_real * b_imag)
                    rows = slice(start, start + slots)
                    for place, values in ((0, reals), (2, imags)):
                        high, low = split_bf16(jnp.concatenate(values, axis=0), 2)
                        cross[place][rows, lanes] = high
                        cross[place + 1][rows, lanes] = low

    def transform(index, which, start):
        step, (high, low) = steps[index][0], sets[index % 2][2 + 2 * which : 4 + 2 * which]
        lanes = slice(start, start + bins_at_once)
        bins = slice(step * band_bins + start, step * band_bins + start + bins_at_once)
        table, total = table_refs[which], sums[which]
        by_high = dot(high[:, lanes], table[bins, :])
        by_low = dot(low[:, lanes], table[bins, :half])
        total[...] += by_high[:, :half] + (by_high[:, half:] + by_low)

    prepare(0)
    for part in range(PARTS):
        multiply(0, part)
    for index in range(len(steps)):
        more = index + 1 < len(steps)
        if more:
            prepare(index + 1)
        for part in range(PARTS):
            if more:
                multiply(index + 1, part)
            if part < len(pieces):
                transform(index, *pieces[part])


def placed_blocks(array_refs, layout, groups):
    me = lax.axis_index("grp").astype(jnp.int32)
    blocks = [(array_refs[index], offset) for index, offset, _ in layout]
    return blocks, [moved(me, move, groups) for _, _, move in layout]


def near_kernel(sizes, layout, array_count, depth, steps, *refs):
    groups, stations, rounds, slots = sizes[:4]
    turn_refs, table_refs, refs = refs[:2], refs[2:4], refs[4:]
    array_refs, refs = refs[:array_count], refs[array_count:]
    (first, second, weight, even, odd), scratch = refs[:5], refs[5:]
    blocks, places = placed_blocks(array_refs, layout, groups)
    extras = [ref[offset + depth : offset + depth + SUBLANES, :] for ref, offset in blocks]
    first[...], second[...], weight[...] = pick_slots(
        extras, places, lax.axis_index("grp"), stations, rounds, slots
    )
    even[...] = jnp.zeros_like(even)
    odd[...] = jnp.zeros_like(odd)
    add_bands(
        sizes, steps, places, turn_refs, table_refs, blocks, (first, second), (even, odd), scratch
    )


def next_kernel(sizes, layout, array_count, steps, *refs):
    turn_refs, table_refs, refs = refs[:2], refs[2:4], refs[4:]
    array_refs, refs = refs[:array_count], refs[array_count:]
    (first, second, even_in, odd_in, even, odd), scratch = refs[:6], refs[6:]
    even[...] = even_in[...]
    odd[...] = odd_in[...]
    blocks, places = placed_blocks(array_refs, layout, sizes[0])
    add_bands(
        sizes, steps, places, turn_refs, table_refs, blocks, (first, second), (even, odd), scratch
    )


def last_kernel(sizes, layout, array_count, steps, *refs):
    turn_refs, table_refs, refs = refs[:2], refs[2:4], refs[4:]
    array_refs, refs = refs[:array_count], refs[array_count:]
    first, second, even_in, odd_in, weight, out_ref, even, odd, above, below, sems = refs[:11]
    even[...] = even_in[...]
    odd[...] = odd_in[...]
    blocks, places = placed_blocks(array_refs, layout, sizes[0])
    add_bands(
        sizes, steps, places, turn_refs, table_refs, blocks, (first, second), (even, odd), refs[11:]
    )
    half = even.shape[1]
    row_weight = weight[:, 0:1]
    mirror = (iota((half, half), 0) + iota((half, half), 1) == half - 1).astype(jnp.bfloat16)

    def mirrored():
        pieces = [dot(piece, mirror) for piece in split_bf16((even[...] + odd[...]) * row_weight, 3)]
        return pieces[0] + (pieces[1] + pieces[2])

    if half % LANES:
        above[:, half:] = (even[...] - odd[...]) * row_weight
        above[:, :half] = mirrored()
        copies = [pltpu.make_async_copy(above, out_ref, sems.at[0])]
        copies[0].start()
    else:
        above[...] = (even[...] - odd[...]) * row_weight
        copies = [pltpu.make_async_copy(above, out_ref.at[:, half:], sems.at[0])]
        copies[0].start()
        below[...] = mirrored()
        copies.append(pltpu.make_async_copy(below, out_ref.at[:, :half], sems.at[1]))
        copies[1].start()
    for copy in copies:
        copy.wait()


def moved(me, move, size):
    return me ^ move if size & (size - 1) == 0 else lax.rem(me + size - move, size)


def moved_index(me, move, size):
    return me ^ move if size & (size - 1) == 0 else (me - move) % size


def fetched(block, group_move, band_move):
    groups, shards = lax.axis_size("grp"), lax.axis_size("freq")
    route = [
        (
            moved_index(group, group_move, groups) * shards + moved_index(band, band_move, shards),
            group * shards + band,
        )
        for group in range(groups)
        for band in range(shards)
    ]
    return lax.ppermute(block, ("grp", "freq"), route)


def exchange(column, ready):
    groups = lax.axis_size("grp")
    if groups != 4:
        near = [column] + [fetched(column, move, 0) for move in range(1, groups)]
        layout = [(move, 0, move) for move in range(groups)]
        far = [fetched(column, move, 1) for move in range(groups)]
        return near, layout, far, ready
    across, beside = fetched(column, 2, 0), fetched(column, 0, 1)
    across, beside, *ready = lax.optimization_barrier((across, beside, *ready))
    near = jnp.concatenate([column, across], axis=0)
    near = [near, fetched(near, 1, 0)]
    return near, two_columns(column.shape[0]), [beside, fetched(across, 0, 1)], ready


def two_columns(rows):
    return [(0, 0, 0), (0, rows, 2), (1, 0, 1), (1, rows, 3)]


def across_cores(far):
    if lax.axis_size("grp") != 4:
        return far
    far = jnp.concatenate(far, axis=0)
    return [far, fetched(far, 1, 0)]


def per_device(spectra, station_mask, owners):
    stations, _, band_bins = spectra.shape
    groups = lax.axis_size("grp")
    shards = lax.axis_size("freq")
    rounds = owners.shape[1]
    pairs = stations * stations
    bin_total = band_bins * shards
    capacity = (2 * pairs + groups - 1) // groups
    slots = padded(capacity, 2 * SUBLANES)
    lag_band = LAGS // shards
    half_band = lag_band // 2
    chunks = band_bins // LANES
    rows = rounds * groups * slots

    vector = pl.BlockSpec(memory_space=pltpu.VMEM)
    in_hbm = pl.BlockSpec(memory_space=pltpu.HBM)

    def call(kernel, name, arrays, out_shape, scratch, cost, others=()):
        arrays = [pltpu.with_memory_space_constraint(array, pltpu.VMEM) for array in arrays]
        others = [pltpu.with_memory_space_constraint(array, pltpu.HBM) for array in others]
        to_hbm = isinstance(out_shape, jax.ShapeDtypeStruct)
        return pl.pallas_call(
            kernel,
            out_shape=out_shape,
            in_specs=[in_hbm] * len(others) + [vector] * len(arrays),
            out_specs=in_hbm if to_hbm else [vector] * len(out_shape),
            scratch_shapes=scratch,
            compiler_params=pltpu.CompilerParams(vmem_limit_bytes=24 * 1024 * 1024),
            cost_estimate=cost,
            name=name,
        )(*others, *arrays)

    steps = shards // 2
    tiles = spectra.reshape(stations, 2, chunks, LANES).transpose(1, 2, 0, 3)
    tiles = tiles.reshape(2 * chunks * stations, LANES)
    column = [tiles] + [fetched(tiles, 0, move) for move in range(2, shards, 2)]

    table = pltpu.VMEM((steps * band_bins, lag_band), jnp.bfloat16)
    turn = pltpu.VMEM((steps, chunks, LANES), jnp.float32)
    base = pltpu.VMEM((64, half_band), jnp.float32)
    table_cost = pl.CostEstimate(
        flops=0, bytes_accessed=4 * bin_total * half_band, transcendentals=0
    )
    *near_table, extras = call(
        functools.partial(near_tables, bin_total),
        "near_tables",
        [],
        [table] * 2 + [turn] * 2 + [pltpu.VMEM((SUBLANES, LANES), jnp.float32)],
        [base] * 2
        + [
            pltpu.VMEM((1, rounds, 1, pairs), jnp.int32),
            pltpu.VMEM((1, stations), jnp.int32),
            pltpu.SemaphoreType.DMA((2,)),
        ],
        table_cost,
        [owners.transpose(0, 1, 3, 2), station_mask.reshape(1, stations)],
    )
    column = jnp.concatenate(column + [extras], axis=0)
    far_table = call(
        functools.partial(far_tables, bin_total),
        "far_tables",
        [column],
        [table] * 2 + [turn] * 2,
        [base] * 2,
        table_cost,
    )
    depth = 2 * chunks * stations
    near, layout, far, far_table = exchange(column, far_table)

    sizes = (groups, stations, rounds, slots, band_bins)
    spectrum = pltpu.VMEM((groups, 2 * chunks, stations, LANES), jnp.float32)
    cross = pltpu.VMEM((rows, band_bins), jnp.bfloat16)
    scratch = ([spectrum] * 2 + [cross] * 4) * 2

    def cost(count):
        flops = 6 * rows * band_bins * lag_band * count
        return pl.CostEstimate(flops=flops, bytes_accessed=2 * 1024 * 1024, transcendentals=0)

    total = pltpu.VMEM((rows, half_band), jnp.float32)
    half_result = total if half_band % LANES == 0 else pltpu.VMEM((rows, lag_band), jnp.float32)
    index = pltpu.VMEM((rows, LANES), jnp.int32)
    near_table = [near_table[place] for place in (2, 3, 0, 1)]
    far_table = [far_table[place] for place in (2, 3, 0, 1)]

    split = steps - steps // 4
    first, second, weight, even, odd = call(
        functools.partial(
            near_kernel, sizes, layout, len(near), steps * depth, [(i, i) for i in range(split)]
        ),
        "near_first",
        near_table + near,
        [index] * 2 + [pltpu.VMEM((rows, LANES), jnp.float32)] + [total] * 2,
        scratch,
        cost(split),
    )
    *far, even = lax.optimization_barrier((*far, even))
    far = across_cores(far)
    even, odd = call(
        functools.partial(
            next_kernel, sizes, layout, len(near), [(i, i) for i in range(split, steps)]
        ),
        "near_next",
        [*near_table, *near, first, second, even, odd],
        [total] * 2,
        scratch,
        cost(steps - split),
    )
    out = call(
        functools.partial(last_kernel, sizes, layout, len(far), [(i, i) for i in range(steps)]),
        "far_bands",
        [*far_table, *far, first, second, even, odd, weight],
        jax.ShapeDtypeStruct((rows, lag_band), jnp.float32),
        [total] * 2 + [half_result] * 2 + [pltpu.SemaphoreType.DMA((2,))] + scratch,
        cost(steps),
    )
    out = out.reshape(1, rounds, groups, slots, lag_band)
    return out[:, :, :, :capacity]


def solution(mesh):
    placed = (P("grp", None, "freq"), P("grp"), P("grp", None, None, None))
    return jax.shard_map(
        per_device,
        mesh=mesh,
        in_specs=placed,
        out_specs=P("grp", None, None, None, "freq"),
        check_vma=False,
    )
```

```python
import functools
import math

import jax
import jax.numpy as jnp
from jax import lax
from jax.experimental import pallas as pl
from jax.experimental.pallas import tpu as pltpu
from jax.sharding import PartitionSpec as P

LAGS = 4096
LANES = 128
SUBLANES = 8
PARTS = 4


def split_bf16(values, parts):
    pieces = []
    for _ in range(parts - 1):
        piece = values.astype(jnp.bfloat16)
        pieces.append(piece)
        values = values - piece.astype(jnp.float32)
    pieces.append(values.astype(jnp.bfloat16))
    return pieces


def iota(shape, axis):
    return lax.broadcasted_iota(jnp.int32, shape, axis)


def dot(left, right):
    return jnp.dot(left, right, preferred_element_type=jnp.float32)


def padded(count, multiple):
    return -(-count // multiple) * multiple


def pick_slots(extras, places, me, stations, rounds, slots):
    groups = len(extras)
    pairs = stations * stations
    listed = rounds * pairs
    rows = rounds * groups * slots
    place = iota((groups, groups), 1)
    held_by = jnp.zeros((groups, groups), jnp.int32)
    for position in range(groups):
        held_by = jnp.where(place == position, places[position], held_by)
    lane = iota((1, listed), 1)

    def by_group(row, shift):
        wanted = (iota((groups, groups), 0) + groups - shift) % groups
        held = jnp.concatenate([extra[row : row + 1, :] for extra in extras], axis=0)
        return dot((held_by == wanted).astype(jnp.bfloat16), held.astype(jnp.bfloat16))

    def of_station(values, number):
        spread = iota((LANES, listed), 0) == number
        return dot(values.astype(jnp.bfloat16), spread.astype(jnp.bfloat16))

    owner_ids = jnp.zeros((groups, listed), jnp.float32)
    partner_mask = jnp.zeros((groups, listed), jnp.float32)
    for index in range(rounds):
        of_round = lane // pairs == index
        owner_ids = jnp.where(of_round, by_group(index, 0), owner_ids)
        second = of_station(by_group(rounds, index + 1), lane % stations)
        partner_mask = jnp.where(of_round, second, partner_mask)
    own_mask = of_station(by_group(rounds, 0), lane % pairs // stations)
    pair_weight = own_mask * partner_mask
    mine = owner_ids == me.astype(jnp.float32)
    from_pair, to_pair = iota((listed, listed), 0), iota((listed, listed), 1)
    before = (from_pair < to_pair) & (from_pair // pairs == to_pair // pairs)
    rank = dot(mine.astype(jnp.bfloat16), before.astype(jnp.bfloat16))
    marked = jnp.where(mine, rank, -1.0).astype(jnp.bfloat16)
    of_group = (iota((rows, groups), 0) // slots) % groups == iota((rows, groups), 1)
    of_group = of_group.astype(jnp.bfloat16)
    row_id, lane_id = iota((rows, listed), 0), iota((rows, listed), 1)
    chosen = (dot(of_group, marked) == (row_id % slots).astype(jnp.float32)) & (
        row_id // (groups * slots) == lane_id // pairs
    )
    weighed = jnp.where(chosen, dot(of_group, pair_weight.astype(jnp.bfloat16)), 0.0)
    weight = dot(weighed.astype(jnp.bfloat16), jnp.ones((listed, LANES), jnp.bfloat16))
    chosen = chosen.astype(jnp.bfloat16)
    pair_id = iota((listed, LANES), 0) % pairs
    first = dot(chosen, (pair_id // stations).astype(jnp.bfloat16))
    second = dot(chosen, (pair_id % stations).astype(jnp.bfloat16))
    return first.astype(jnp.int32), second.astype(jnp.int32), weight


def make_tables(parity, table_refs, turn_refs, base_refs, bin_total):
    place = lax.axis_index("freq").astype(jnp.int32)
    near_cos, near_sin = base_refs
    fine, half_band = near_cos.shape
    steps, chunks, _ = turn_refs[0].shape
    band_bins = chunks * LANES

    def circle(turns):
        angles = (turns & (4 * bin_total - 1)).astype(jnp.float32) * (math.pi / (2 * bin_total))
        return jnp.cos(angles), jnp.sin(angles)

    def every(count, start, step):
        bins = start + iota((count, half_band), 0) * step
        return circle(bins * (2 * iota((count, half_band), 1) + 1))

    def added(cos, sin, other_cos, other_sin):
        return cos * other_cos - sin * other_sin, sin * other_cos + cos * other_sin

    low_cos, low_sin = every(SUBLANES, 0, 1)
    high_cos, high_sin = every(fine // SUBLANES, 0, SUBLANES)
    for index in range(fine // SUBLANES):
        rows, one = slice(index * SUBLANES, (index + 1) * SUBLANES), slice(index, index + 1)
        near_cos[rows, :], near_sin[rows, :] = added(
            high_cos[one], high_sin[one], low_cos, low_sin
        )

    centre = 2 * half_band * (2 * place + 1) - 1 - LAGS
    norm = 1.0 / math.sqrt(bin_total)
    for step in range(steps):
        start = (place ^ (2 * step + parity)) * band_bins
        cos, sin = every(band_bins // fine, start, fine)
        for part in range(band_bins // fine):
            one = slice(part, part + 1)
            values = added(cos[one], sin[one], near_cos[...], near_sin[...])
            rows = slice(step * band_bins + part * fine, step * band_bins + (part + 1) * fine)
            for table, value in zip(table_refs, values):
                table[rows, :half_band], table[rows, half_band:] = split_bf16(value, 2)
        bins = start + iota((chunks, LANES), 0) * LANES + iota((chunks, LANES), 1)
        for turn, value in zip(turn_refs, circle(bins * centre)):
            turn[step] = value * norm


def near_tables(bin_total, owners_hbm, mask_hbm, *refs):
    table_refs, turn_refs, extras = refs[:2], refs[2:4], refs[4]
    base_refs, (owners_ref, mask_ref, sems) = refs[5:7], refs[7:]
    copies = [
        pltpu.make_async_copy(owners_hbm, owners_ref, sems.at[0]),
        pltpu.make_async_copy(mask_hbm, mask_ref, sems.at[1]),
    ]
    for copy in copies:
        copy.start()
    make_tables(0, table_refs, turn_refs, base_refs, bin_total)
    for copy in copies:
        copy.wait()
    extras[...] = jnp.zeros_like(extras)
    rounds, pairs = owners_ref.shape[1], owners_ref.shape[3]
    for index in range(rounds):
        lanes = slice(index * pairs, (index + 1) * pairs)
        extras[index : index + 1, lanes] = owners_ref[0, index].astype(jnp.float32)
    extras[rounds : rounds + 1, : mask_ref.shape[1]] = mask_ref[...].astype(jnp.float32)


def far_tables(bin_total, _, *refs):
    make_tables(1, refs[:2], refs[2:4], refs[4:], bin_total)


def add_bands(sizes, steps, places, turn_refs, table_refs, blocks, picks, sums, scratch):
    groups, stations, rounds, slots, band_bins = sizes
    chunks = band_bins // LANES
    depth = 2 * chunks * stations
    half = sums[0].shape[1]
    first, second = picks
    sets = [scratch[6 * index : 6 * (index + 1)] for index in range(2)]
    part_groups = [range(part * groups // PARTS, (part + 1) * groups // PARTS) for part in range(PARTS)]
    bins_at_once = max(band_bins // 2, LANES)
    pieces = [(which, start) for which in range(2) for start in range(0, band_bins, bins_at_once)]

    def prepare(index):
        (step, place_step), (held, turned) = steps[index], sets[index % 2][:2]
        for position, (ref, offset) in enumerate(blocks):
            group = places[position]
            for q in range(chunks):
                turn_cos, turn_sin = [turn[step, q : q + 1, :] for turn in turn_refs]
                start = offset + place_step * depth + q * stations
                real = ref[start : start + stations, :]
                start += chunks * stations
                imag = ref[start : start + stations, :]
                held[group, q] = real
                held[group, chunks + q] = imag
                turned[group, q] = real * turn_cos + imag * turn_sin
                turned[group, chunks + q] = imag * turn_cos - real * turn_sin

    def multiply(index, part):
        held, turned, *cross = sets[index % 2]
        for group in part_groups[part]:
            sources = []
            for number in range(rounds):
                start = (number * groups + group) * slots
                lines = [slice(start + o, start + o + SUBLANES) for o in range(0, slots, SUBLANES)]
                partner = (group + groups - 1 - number) % groups
                sources.append((start, partner, [(first[line, :], second[line, :]) for line in lines]))
            for q in range(chunks):
                lanes = slice(q * LANES, (q + 1) * LANES)
                own_real, own_imag = held[group, q], held[group, chunks + q]
                for start, partner, indices in sources:
                    real, imag = turned[partner, q], turned[partner, chunks + q]
                    reals, imags = [], []
                    for index_a, index_b in indices:
                        a_real = jnp.take_along_axis(own_real, index_a, axis=0)
                        a_imag = jnp.take_along_axis(own_imag, index_a, axis=0)
                        b_real = jnp.take_along_axis(real, index_b, axis=0)
                        b_imag = jnp.take_along_axis(imag, index_b, axis=0)
                        reals.append(a_real * b_real + a_imag * b_imag)
                        imags.append(a_imag * b_real - a_real * b_imag)
                    rows = slice(start, start + slots)
                    for place, values in ((0, reals), (2, imags)):
                        high, low = split_bf16(jnp.concatenate(values, axis=0), 2)
                        cross[place][rows, lanes] = high
                        cross[place + 1][rows, lanes] = low

    def transform(index, which, start):
        step, (high, low) = steps[index][0], sets[index % 2][2 + 2 * which : 4 + 2 * which]
        lanes = slice(start, start + bins_at_once)
        bins = slice(step * band_bins + start, step * band_bins + start + bins_at_once)
        table, total = table_refs[which], sums[which]
        by_high = dot(high[:, lanes], table[bins, :])
        by_low = dot(low[:, lanes], table[bins, :half])
        total[...] += by_high[:, :half] + (by_high[:, half:] + by_low)

    prepare(0)
    for part in range(PARTS):
        multiply(0, part)
    for index in range(len(steps)):
        more = index + 1 < len(steps)
        if more:
            prepare(index + 1)
        for part in range(PARTS):
            if more:
                multiply(index + 1, part)
            if part < len(pieces):
                transform(index, *pieces[part])


def placed_blocks(array_refs, layout, groups):
    me = lax.axis_index("grp").astype(jnp.int32)
    blocks = [(array_refs[index], offset) for index, offset, _ in layout]
    return blocks, [moved(me, move, groups) for _, _, move in layout]


def near_kernel(sizes, layout, array_count, depth, steps, *refs):
    groups, stations, rounds, slots = sizes[:4]
    turn_refs, table_refs, refs = refs[:2], refs[2:4], refs[4:]
    array_refs, refs = refs[:array_count], refs[array_count:]
    (first, second, weight, even, odd), scratch = refs[:5], refs[5:]
    blocks, places = placed_blocks(array_refs, layout, groups)
    extras = [ref[offset + depth : offset + depth + SUBLANES, :] for ref, offset in blocks]
    first[...], second[...], weight[...] = pick_slots(
        extras, places, lax.axis_index("grp"), stations, rounds, slots
    )
    even[...] = jnp.zeros_like(even)
    odd[...] = jnp.zeros_like(odd)
    add_bands(
        sizes, steps, places, turn_refs, table_refs, blocks, (first, second), (even, odd), scratch
    )


def next_kernel(sizes, layout, array_count, steps, *refs):
    turn_refs, table_refs, refs = refs[:2], refs[2:4], refs[4:]
    array_refs, refs = refs[:array_count], refs[array_count:]
    (first, second, even_in, odd_in, even, odd), scratch = refs[:6], refs[6:]
    even[...] = even_in[...]
    odd[...] = odd_in[...]
    blocks, places = placed_blocks(array_refs, layout, sizes[0])
    add_bands(
        sizes, steps, places, turn_refs, table_refs, blocks, (first, second), (even, odd), scratch
    )


def last_kernel(sizes, layout, array_count, steps, *refs):
    turn_refs, table_refs, refs = refs[:2], refs[2:4], refs[4:]
    array_refs, refs = refs[:array_count], refs[array_count:]
    first, second, even_in, odd_in, weight, out_ref, even, odd, above, below, sems = refs[:11]
    even[...] = even_in[...]
    odd[...] = odd_in[...]
    blocks, places = placed_blocks(array_refs, layout, sizes[0])
    add_bands(
        sizes, steps, places, turn_refs, table_refs, blocks, (first, second), (even, odd), refs[11:]
    )
    half = even.shape[1]
    row_weight = weight[:, 0:1]
    mirror = (iota((half, half), 0) + iota((half, half), 1) == half - 1).astype(jnp.bfloat16)

    def mirrored():
        pieces = [dot(piece, mirror) for piece in split_bf16((even[...] + odd[...]) * row_weight, 3)]
        return pieces[0] + (pieces[1] + pieces[2])

    if half % LANES:
        above[:, half:] = (even[...] - odd[...]) * row_weight
        above[:, :half] = mirrored()
        copies = [pltpu.make_async_copy(above, out_ref, sems.at[0])]
        copies[0].start()
    else:
        above[...] = (even[...] - odd[...]) * row_weight
        copies = [pltpu.make_async_copy(above, out_ref.at[:, half:], sems.at[0])]
        copies[0].start()
        below[...] = mirrored()
        copies.append(pltpu.make_async_copy(below, out_ref.at[:, :half], sems.at[1]))
        copies[1].start()
    for copy in copies:
        copy.wait()


def moved(me, move, size):
    return me ^ move if size & (size - 1) == 0 else lax.rem(me + size - move, size)


def moved_index(me, move, size):
    return me ^ move if size & (size - 1) == 0 else (me - move) % size


def fetched(block, group_move, band_move):
    groups, shards = lax.axis_size("grp"), lax.axis_size("freq")
    route = [
        (
            moved_index(group, group_move, groups) * shards + moved_index(band, band_move, shards),
            group * shards + band,
        )
        for group in range(groups)
        for band in range(shards)
    ]
    return lax.ppermute(block, ("grp", "freq"), route)


def exchange(column, ready):
    groups = lax.axis_size("grp")
    if groups != 4:
        near = [column] + [fetched(column, move, 0) for move in range(1, groups)]
        layout = [(move, 0, move) for move in range(groups)]
        far = [fetched(column, move, 1) for move in range(groups)]
        return near, layout, far, ready
    across, core = fetched(column, 2, 0), fetched(column, 1, 0)
    beside = fetched(longer(column), 0, 1)
    across, core, *ready = lax.optimization_barrier((across, core, *ready))
    near = [column, core, across, fetched(across, 1, 0)]
    diagonal = fetched(longer(across), 0, 1)
    far = [beside, fetched(beside, 1, 0), diagonal]
    return near, [(place, 0, place) for place in range(4)], far, ready


def longer(block):
    return jnp.concatenate([block, block[-SUBLANES:]], axis=0)


def across_cores(far):
    return far + [fetched(far[-1], 1, 0)] if lax.axis_size("grp") == 4 else far


def per_device(spectra, station_mask, owners):
    stations, _, band_bins = spectra.shape
    groups = lax.axis_size("grp")
    shards = lax.axis_size("freq")
    rounds = owners.shape[1]
    pairs = stations * stations
    bin_total = band_bins * shards
    capacity = (2 * pairs + groups - 1) // groups
    slots = padded(capacity, 2 * SUBLANES)
    lag_band = LAGS // shards
    half_band = lag_band // 2
    chunks = band_bins // LANES
    rows = rounds * groups * slots

    vector = pl.BlockSpec(memory_space=pltpu.VMEM)
    in_hbm = pl.BlockSpec(memory_space=pltpu.HBM)

    def call(kernel, name, arrays, out_shape, scratch, cost, others=()):
        arrays = [pltpu.with_memory_space_constraint(array, pltpu.VMEM) for array in arrays]
        others = [pltpu.with_memory_space_constraint(array, pltpu.HBM) for array in others]
        to_hbm = isinstance(out_shape, jax.ShapeDtypeStruct)
        return pl.pallas_call(
            kernel,
            out_shape=out_shape,
            in_specs=[in_hbm] * len(others) + [vector] * len(arrays),
            out_specs=in_hbm if to_hbm else [vector] * len(out_shape),
            scratch_shapes=scratch,
            compiler_params=pltpu.CompilerParams(vmem_limit_bytes=24 * 1024 * 1024),
            cost_estimate=cost,
            name=name,
        )(*others, *arrays)

    steps = shards // 2
    tiles = spectra.reshape(stations, 2, chunks, LANES).transpose(1, 2, 0, 3)
    tiles = tiles.reshape(2 * chunks * stations, LANES)
    column = [tiles] + [fetched(tiles, 0, move) for move in range(2, shards, 2)]

    table = pltpu.VMEM((steps * band_bins, lag_band), jnp.bfloat16)
    turn = pltpu.VMEM((steps, chunks, LANES), jnp.float32)
    base = pltpu.VMEM((64, half_band), jnp.float32)
    table_cost = pl.CostEstimate(
        flops=0, bytes_accessed=4 * bin_total * half_band, transcendentals=0
    )
    *near_table, extras = call(
        functools.partial(near_tables, bin_total),
        "near_tables",
        [],
        [table] * 2 + [turn] * 2 + [pltpu.VMEM((SUBLANES, LANES), jnp.float32)],
        [base] * 2
        + [
            pltpu.VMEM((1, rounds, 1, pairs), jnp.int32),
            pltpu.VMEM((1, stations), jnp.int32),
            pltpu.SemaphoreType.DMA((2,)),
        ],
        table_cost,
        [owners.transpose(0, 1, 3, 2), station_mask.reshape(1, stations)],
    )
    column = jnp.concatenate(column + [extras], axis=0)
    far_table = call(
        functools.partial(far_tables, bin_total),
        "far_tables",
        [column],
        [table] * 2 + [turn] * 2,
        [base] * 2,
        table_cost,
    )
    depth = 2 * chunks * stations
    near, layout, far, far_table = exchange(column, far_table)

    sizes = (groups, stations, rounds, slots, band_bins)
    spectrum = pltpu.VMEM((groups, 2 * chunks, stations, LANES), jnp.float32)
    cross = pltpu.VMEM((rows, band_bins), jnp.bfloat16)
    scratch = ([spectrum] * 2 + [cross] * 4) * 2

    def cost(count):
        flops = 6 * rows * band_bins * lag_band * count
        return pl.CostEstimate(flops=flops, bytes_accessed=2 * 1024 * 1024, transcendentals=0)

    total = pltpu.VMEM((rows, half_band), jnp.float32)
    half_result = total if half_band % LANES == 0 else pltpu.VMEM((rows, lag_band), jnp.float32)
    index = pltpu.VMEM((rows, LANES), jnp.int32)
    near_table = [near_table[place] for place in (2, 3, 0, 1)]
    far_table = [far_table[place] for place in (2, 3, 0, 1)]

    split = steps - steps // 4
    first, second, weight, even, odd = call(
        functools.partial(
            near_kernel, sizes, layout, len(near), steps * depth, [(i, i) for i in range(split)]
        ),
        "near_first",
        near_table + near,
        [index] * 2 + [pltpu.VMEM((rows, LANES), jnp.float32)] + [total] * 2,
        scratch,
        cost(split),
    )
    *far, even = lax.optimization_barrier((*far, even))
    far = across_cores(far)
    even, odd = call(
        functools.partial(
            next_kernel, sizes, layout, len(near), [(i, i) for i in range(split, steps)]
        ),
        "near_next",
        [*near_table, *near, first, second, even, odd],
        [total] * 2,
        scratch,
        cost(steps - split),
    )
    out = call(
        functools.partial(last_kernel, sizes, layout, len(far), [(i, i) for i in range(steps)]),
        "far_bands",
        [*far_table, *far, first, second, even, odd, weight],
        jax.ShapeDtypeStruct((rows, lag_band), jnp.float32),
        [total] * 2 + [half_result] * 2 + [pltpu.SemaphoreType.DMA((2,))] + scratch,
        cost(steps),
    )
    out = out.reshape(1, rounds, groups, slots, lag_band)
    return out[:, :, :, :capacity]


def solution(mesh):
    placed = (P("grp", None, "freq"), P("grp"), P("grp", None, None, None))
    return jax.shard_map(
        per_device,
        mesh=mesh,
        in_specs=placed,
        out_specs=P("grp", None, None, None, "freq"),
        check_vma=False,
    )
```

```python
import functools
import math

import jax
import jax.numpy as jnp
from jax import lax
from jax.experimental import pallas as pl
from jax.experimental.pallas import tpu as pltpu
from jax.sharding import PartitionSpec as P

LAGS = 4096
LANES = 128
SUBLANES = 8
PARTS = 4


def split_bf16(values, parts):
    pieces = []
    for _ in range(parts - 1):
        piece = values.astype(jnp.bfloat16)
        pieces.append(piece)
        values = values - piece.astype(jnp.float32)
    pieces.append(values.astype(jnp.bfloat16))
    return pieces


def iota(shape, axis):
    return lax.broadcasted_iota(jnp.int32, shape, axis)


def dot(left, right):
    return jnp.dot(left, right, preferred_element_type=jnp.float32)


def padded(count, multiple):
    return -(-count // multiple) * multiple


def pick_slots(extras, places, me, stations, rounds, slots):
    groups = len(extras)
    pairs = stations * stations
    listed = rounds * pairs
    rows = rounds * groups * slots
    place = iota((groups, groups), 1)
    held_by = jnp.zeros((groups, groups), jnp.int32)
    for position in range(groups):
        held_by = jnp.where(place == position, places[position], held_by)
    lane = iota((1, listed), 1)

    def by_group(row, shift):
        wanted = (iota((groups, groups), 0) + groups - shift) % groups
        held = jnp.concatenate([extra[row : row + 1, :] for extra in extras], axis=0)
        return dot((held_by == wanted).astype(jnp.bfloat16), held.astype(jnp.bfloat16))

    def of_station(values, number):
        spread = iota((LANES, listed), 0) == number
        return dot(values.astype(jnp.bfloat16), spread.astype(jnp.bfloat16))

    owner_ids = jnp.zeros((groups, listed), jnp.float32)
    partner_mask = jnp.zeros((groups, listed), jnp.float32)
    for index in range(rounds):
        of_round = lane // pairs == index
        owner_ids = jnp.where(of_round, by_group(index, 0), owner_ids)
        second = of_station(by_group(rounds, index + 1), lane % stations)
        partner_mask = jnp.where(of_round, second, partner_mask)
    own_mask = of_station(by_group(rounds, 0), lane % pairs // stations)
    pair_weight = own_mask * partner_mask
    mine = owner_ids == me.astype(jnp.float32)
    from_pair, to_pair = iota((listed, listed), 0), iota((listed, listed), 1)
    before = (from_pair < to_pair) & (from_pair // pairs == to_pair // pairs)
    rank = dot(mine.astype(jnp.bfloat16), before.astype(jnp.bfloat16))
    marked = jnp.where(mine, rank, -1.0).astype(jnp.bfloat16)
    of_group = (iota((rows, groups), 0) // slots) % groups == iota((rows, groups), 1)
    of_group = of_group.astype(jnp.bfloat16)
    row_id, lane_id = iota((rows, listed), 0), iota((rows, listed), 1)
    chosen = (dot(of_group, marked) == (row_id % slots).astype(jnp.float32)) & (
        row_id // (groups * slots) == lane_id // pairs
    )
    weighed = jnp.where(chosen, dot(of_group, pair_weight.astype(jnp.bfloat16)), 0.0)
    weight = dot(weighed.astype(jnp.bfloat16), jnp.ones((listed, LANES), jnp.bfloat16))
    chosen = chosen.astype(jnp.bfloat16)
    pair_id = iota((listed, LANES), 0) % pairs
    first = dot(chosen, (pair_id // stations).astype(jnp.bfloat16))
    second = dot(chosen, (pair_id % stations).astype(jnp.bfloat16))
    return first.astype(jnp.int32), second.astype(jnp.int32), weight


def make_tables(parity, table_refs, turn_refs, base_refs, bin_total):
    place = lax.axis_index("freq").astype(jnp.int32)
    near_cos, near_sin = base_refs
    fine, half_band = near_cos.shape
    steps, chunks, _ = turn_refs[0].shape
    band_bins = chunks * LANES

    def circle(turns):
        angles = (turns & (4 * bin_total - 1)).astype(jnp.float32) * (math.pi / (2 * bin_total))
        return jnp.cos(angles), jnp.sin(angles)

    def every(count, start, step):
        bins = start + iota((count, half_band), 0) * step
        return circle(bins * (2 * iota((count, half_band), 1) + 1))

    def added(cos, sin, other_cos, other_sin):
        return cos * other_cos - sin * other_sin, sin * other_cos + cos * other_sin

    low_cos, low_sin = every(SUBLANES, 0, 1)
    high_cos, high_sin = every(fine // SUBLANES, 0, SUBLANES)
    for index in range(fine // SUBLANES):
        rows, one = slice(index * SUBLANES, (index + 1) * SUBLANES), slice(index, index + 1)
        near_cos[rows, :], near_sin[rows, :] = added(
            high_cos[one], high_sin[one], low_cos, low_sin
        )

    centre = 2 * half_band * (2 * place + 1) - 1 - LAGS
    norm = 1.0 / math.sqrt(bin_total)
    for step in range(steps):
        start = (place ^ (2 * step + parity)) * band_bins
        cos, sin = every(band_bins // fine, start, fine)
        for part in range(band_bins // fine):
            one = slice(part, part + 1)
            values = added(cos[one], sin[one], near_cos[...], near_sin[...])
            rows = slice(step * band_bins + part * fine, step * band_bins + (part + 1) * fine)
            for table, value in zip(table_refs, values):
                table[rows, :half_band], table[rows, half_band:] = split_bf16(value, 2)
        bins = start + iota((chunks, LANES), 0) * LANES + iota((chunks, LANES), 1)
        for turn, value in zip(turn_refs, circle(bins * centre)):
            turn[step] = value * norm


def table_kernel(bin_total, owners_hbm, mask_hbm, *refs):
    near_refs, far_refs, extras = refs[:4], refs[4:8], refs[8]
    base_refs, (owners_ref, mask_ref, sems) = refs[9:11], refs[11:]
    copies = [
        pltpu.make_async_copy(owners_hbm, owners_ref, sems.at[0]),
        pltpu.make_async_copy(mask_hbm, mask_ref, sems.at[1]),
    ]
    for copy in copies:
        copy.start()
    make_tables(0, near_refs[:2], near_refs[2:], base_refs, bin_total)
    make_tables(1, far_refs[:2], far_refs[2:], base_refs, bin_total)
    for copy in copies:
        copy.wait()
    extras[...] = jnp.zeros_like(extras)
    rounds, pairs = owners_ref.shape[1], owners_ref.shape[3]
    for index in range(rounds):
        lanes = slice(index * pairs, (index + 1) * pairs)
        extras[index : index + 1, lanes] = owners_ref[0, index].astype(jnp.float32)
    extras[rounds : rounds + 1, : mask_ref.shape[1]] = mask_ref[...].astype(jnp.float32)


def add_bands(sizes, steps, places, turn_refs, table_refs, blocks, picks, sums, scratch):
    groups, stations, rounds, slots, band_bins = sizes
    chunks = band_bins // LANES
    depth = 2 * chunks * stations
    half = sums[0].shape[1]
    first, second = picks
    sets = [scratch[6 * index : 6 * (index + 1)] for index in range(2)]
    part_groups = [range(part * groups // PARTS, (part + 1) * groups // PARTS) for part in range(PARTS)]
    bins_at_once = max(band_bins // 2, LANES)
    pieces = [(which, start) for which in range(2) for start in range(0, band_bins, bins_at_once)]

    def prepare(index):
        (step, place_step), (held, turned) = steps[index], sets[index % 2][:2]
        for position, (ref, offset) in enumerate(blocks):
            group = places[position]
            for q in range(chunks):
                turn_cos, turn_sin = [turn[step, q : q + 1, :] for turn in turn_refs]
                start = offset + place_step * depth + q * stations
                real = ref[start : start + stations, :]
                start += chunks * stations
                imag = ref[start : start + stations, :]
                held[group, q] = real
                held[group, chunks + q] = imag
                turned[group, q] = real * turn_cos + imag * turn_sin
                turned[group, chunks + q] = imag * turn_cos - real * turn_sin

    def multiply(index, part):
        held, turned, *cross = sets[index % 2]
        for group in part_groups[part]:
            sources = []
            for number in range(rounds):
                start = (number * groups + group) * slots
                lines = [slice(start + o, start + o + SUBLANES) for o in range(0, slots, SUBLANES)]
                partner = (group + groups - 1 - number) % groups
                sources.append((start, partner, [(first[line, :], second[line, :]) for line in lines]))
            for q in range(chunks):
                lanes = slice(q * LANES, (q + 1) * LANES)
                own_real, own_imag = held[group, q], held[group, chunks + q]
                for start, partner, indices in sources:
                    real, imag = turned[partner, q], turned[partner, chunks + q]
                    reals, imags = [], []
                    for index_a, index_b in indices:
                        a_real = jnp.take_along_axis(own_real, index_a, axis=0)
                        a_imag = jnp.take_along_axis(own_imag, index_a, axis=0)
                        b_real = jnp.take_along_axis(real, index_b, axis=0)
                        b_imag = jnp.take_along_axis(imag, index_b, axis=0)
                        reals.append(a_real * b_real + a_imag * b_imag)
                        imags.append(a_imag * b_real - a_real * b_imag)
                    rows = slice(start, start + slots)
                    for place, values in ((0, reals), (2, imags)):
                        high, low = split_bf16(jnp.concatenate(values, axis=0), 2)
                        cross[place][rows, lanes] = high
                        cross[place + 1][rows, lanes] = low

    def transform(index, which, start):
        step, (high, low) = steps[index][0], sets[index % 2][2 + 2 * which : 4 + 2 * which]
        lanes = slice(start, start + bins_at_once)
        bins = slice(step * band_bins + start, step * band_bins + start + bins_at_once)
        table, total = table_refs[which], sums[which]
        by_high = dot(high[:, lanes], table[bins, :])
        by_low = dot(low[:, lanes], table[bins, :half])
        total[...] += by_high[:, :half] + (by_high[:, half:] + by_low)

    prepare(0)
    for part in range(PARTS):
        multiply(0, part)
    for index in range(len(steps)):
        more = index + 1 < len(steps)
        if more:
            prepare(index + 1)
        for part in range(PARTS):
            if more:
                multiply(index + 1, part)
            if part < len(pieces):
                transform(index, *pieces[part])


def placed_blocks(array_refs, layout, groups):
    me = lax.axis_index("grp").astype(jnp.int32)
    blocks = [(array_refs[index], offset) for index, offset, _ in layout]
    return blocks, [moved(me, move, groups) for _, _, move in layout]


def near_kernel(sizes, layout, array_count, depth, steps, *refs):
    groups, stations, rounds, slots = sizes[:4]
    turn_refs, table_refs, refs = refs[:2], refs[2:4], refs[4:]
    array_refs, refs = refs[:array_count], refs[array_count:]
    (first, second, weight, even, odd), scratch = refs[:5], refs[5:]
    blocks, places = placed_blocks(array_refs, layout, groups)
    extras = [ref[offset + depth : offset + depth + SUBLANES, :] for ref, offset in blocks]
    first[...], second[...], weight[...] = pick_slots(
        extras, places, lax.axis_index("grp"), stations, rounds, slots
    )
    even[...] = jnp.zeros_like(even)
    odd[...] = jnp.zeros_like(odd)
    add_bands(
        sizes, steps, places, turn_refs, table_refs, blocks, (first, second), (even, odd), scratch
    )


def next_kernel(sizes, layout, array_count, steps, *refs):
    turn_refs, table_refs, refs = refs[:2], refs[2:4], refs[4:]
    array_refs, refs = refs[:array_count], refs[array_count:]
    (first, second, even_in, odd_in, even, odd), scratch = refs[:6], refs[6:]
    even[...] = even_in[...]
    odd[...] = odd_in[...]
    blocks, places = placed_blocks(array_refs, layout, sizes[0])
    add_bands(
        sizes, steps, places, turn_refs, table_refs, blocks, (first, second), (even, odd), scratch
    )


def last_kernel(sizes, layout, array_count, steps, *refs):
    turn_refs, table_refs, refs = refs[:2], refs[2:4], refs[4:]
    array_refs, refs = refs[:array_count], refs[array_count:]
    first, second, even_in, odd_in, weight, out_ref, even, odd, above, below, sems = refs[:11]
    even[...] = even_in[...]
    odd[...] = odd_in[...]
    blocks, places = placed_blocks(array_refs, layout, sizes[0])
    add_bands(
        sizes, steps, places, turn_refs, table_refs, blocks, (first, second), (even, odd), refs[11:]
    )
    half = even.shape[1]
    row_weight = weight[:, 0:1]
    mirror = (iota((half, half), 0) + iota((half, half), 1) == half - 1).astype(jnp.bfloat16)

    def mirrored():
        pieces = [dot(piece, mirror) for piece in split_bf16((even[...] + odd[...]) * row_weight, 3)]
        return pieces[0] + (pieces[1] + pieces[2])

    if half % LANES:
        above[:, half:] = (even[...] - odd[...]) * row_weight
        above[:, :half] = mirrored()
        copies = [pltpu.make_async_copy(above, out_ref, sems.at[0])]
        copies[0].start()
    else:
        above[...] = (even[...] - odd[...]) * row_weight
        copies = [pltpu.make_async_copy(above, out_ref.at[:, half:], sems.at[0])]
        copies[0].start()
        below[...] = mirrored()
        copies.append(pltpu.make_async_copy(below, out_ref.at[:, :half], sems.at[1]))
        copies[1].start()
    for copy in copies:
        copy.wait()


def moved(me, move, size):
    return me ^ move if size & (size - 1) == 0 else lax.rem(me + size - move, size)


def moved_index(me, move, size):
    return me ^ move if size & (size - 1) == 0 else (me - move) % size


def fetched(block, group_move, band_move):
    groups, shards = lax.axis_size("grp"), lax.axis_size("freq")
    route = [
        (
            moved_index(group, group_move, groups) * shards + moved_index(band, band_move, shards),
            group * shards + band,
        )
        for group in range(groups)
        for band in range(shards)
    ]
    return lax.ppermute(block, ("grp", "freq"), route)


def exchange(column, parts):
    groups = lax.axis_size("grp")
    if groups != 4:
        near = [column] + [fetched(column, move, 0) for move in range(1, groups)]
        layout = [(move, 0, move) for move in range(groups)]
        far = [fetched(column, move, 1) for move in range(groups)]
        return near, layout, far, [[] for _ in parts]
    across, core = fetched(column, 2, 0), fetched(column, 1, 0)
    beside = fetched(longer(column), 0, 1)
    across, core = lax.optimization_barrier((across, core))
    near = [column, core, across, fetched(across, 1, 0)]
    diagonals = [[fetched(longer(across[start:stop]), 0, 1)] for start, stop in parts]
    far = [beside, fetched(beside, 1, 0)]
    return near, [(place, 0, place) for place in range(4)], far, diagonals


def longer(block):
    return jnp.concatenate([block, block[-SUBLANES:]], axis=0)


def across_cores(far, diagonal, first_row):
    arrays = far + [block for own in diagonal for block in (own, fetched(own, 1, 0))]
    layout = [
        (place, 0 if place < len(far) else -first_row, place) for place in range(len(arrays))
    ]
    return arrays, layout


def per_device(spectra, station_mask, owners):
    stations, _, band_bins = spectra.shape
    groups = lax.axis_size("grp")
    shards = lax.axis_size("freq")
    rounds = owners.shape[1]
    pairs = stations * stations
    bin_total = band_bins * shards
    capacity = (2 * pairs + groups - 1) // groups
    slots = padded(capacity, 2 * SUBLANES)
    lag_band = LAGS // shards
    half_band = lag_band // 2
    chunks = band_bins // LANES
    rows = rounds * groups * slots

    vector = pl.BlockSpec(memory_space=pltpu.VMEM)
    in_hbm = pl.BlockSpec(memory_space=pltpu.HBM)

    def call(kernel, name, arrays, out_shape, scratch, cost, others=()):
        arrays = [pltpu.with_memory_space_constraint(array, pltpu.VMEM) for array in arrays]
        others = [pltpu.with_memory_space_constraint(array, pltpu.HBM) for array in others]
        to_hbm = isinstance(out_shape, jax.ShapeDtypeStruct)
        return pl.pallas_call(
            kernel,
            out_shape=out_shape,
            in_specs=[in_hbm] * len(others) + [vector] * len(arrays),
            out_specs=in_hbm if to_hbm else [vector] * len(out_shape),
            scratch_shapes=scratch,
            compiler_params=pltpu.CompilerParams(vmem_limit_bytes=24 * 1024 * 1024),
            cost_estimate=cost,
            name=name,
        )(*others, *arrays)

    steps = shards // 2
    tiles = spectra.reshape(stations, 2, chunks, LANES).transpose(1, 2, 0, 3)
    tiles = tiles.reshape(2 * chunks * stations, LANES)
    column = [tiles] + [fetched(tiles, 0, move) for move in range(2, shards, 2)]

    table = pltpu.VMEM((steps * band_bins, lag_band), jnp.bfloat16)
    turn = pltpu.VMEM((steps, chunks, LANES), jnp.float32)
    base = pltpu.VMEM((64, half_band), jnp.float32)
    table_cost = pl.CostEstimate(
        flops=0, bytes_accessed=4 * bin_total * half_band, transcendentals=0
    )
    *band_tables, extras = call(
        functools.partial(table_kernel, bin_total),
        "tables",
        [],
        ([table] * 2 + [turn] * 2) * 2 + [pltpu.VMEM((SUBLANES, LANES), jnp.float32)],
        [base] * 2
        + [
            pltpu.VMEM((1, rounds, 1, pairs), jnp.int32),
            pltpu.VMEM((1, stations), jnp.int32),
            pltpu.SemaphoreType.DMA((2,)),
        ],
        table_cost,
        [owners.transpose(0, 1, 3, 2), station_mask.reshape(1, stations)],
    )
    column = jnp.concatenate(column + [extras], axis=0)
    depth = 2 * chunks * stations
    split, middle = steps - steps // 4, steps // 2
    parts = [(0, middle * depth), (middle * depth, steps * depth)]
    near, layout, far, diagonals = exchange(column, parts)

    sizes = (groups, stations, rounds, slots, band_bins)
    spectrum = pltpu.VMEM((groups, 2 * chunks, stations, LANES), jnp.float32)
    cross = pltpu.VMEM((rows, band_bins), jnp.bfloat16)
    scratch = ([spectrum] * 2 + [cross] * 4) * 2

    def cost(count):
        flops = 6 * rows * band_bins * lag_band * count
        return pl.CostEstimate(flops=flops, bytes_accessed=2 * 1024 * 1024, transcendentals=0)

    total = pltpu.VMEM((rows, half_band), jnp.float32)
    half_result = total if half_band % LANES == 0 else pltpu.VMEM((rows, lag_band), jnp.float32)
    index = pltpu.VMEM((rows, LANES), jnp.int32)
    near_table = [band_tables[place] for place in (2, 3, 0, 1)]
    far_table = [band_tables[place] for place in (6, 7, 4, 5)]

    first, second, weight, even, odd = call(
        functools.partial(
            near_kernel, sizes, layout, len(near), steps * depth, [(i, i) for i in range(split)]
        ),
        "near_first",
        near_table + near,
        [index] * 2 + [pltpu.VMEM((rows, LANES), jnp.float32)] + [total] * 2,
        scratch,
        cost(split),
    )
    def add(name, layout, arrays, tables, some, sums):
        return call(
            functools.partial(next_kernel, sizes, layout, len(arrays), [(i, i) for i in some]),
            name,
            [*tables, *arrays, first, second, *sums],
            [total] * 2,
            scratch,
            cost(len(some)),
        )

    *diagonal, even = lax.optimization_barrier((*diagonals[0], even))
    far_first, layout_first = across_cores(far, diagonal, parts[0][0])
    even, odd = add("near_next", layout, near, near_table, range(split, steps), (even, odd))
    *diagonal, even = lax.optimization_barrier((*diagonals[1], even))
    far_next, layout_next = across_cores(far, diagonal, parts[1][0])
    even, odd = add("far_first", layout_first, far_first, far_table, range(middle), (even, odd))
    some = [(i, i) for i in range(middle, steps)]
    out = call(
        functools.partial(last_kernel, sizes, layout_next, len(far_next), some),
        "far_next",
        [*far_table, *far_next, first, second, even, odd, weight],
        jax.ShapeDtypeStruct((rows, lag_band), jnp.float32),
        [total] * 2 + [half_result] * 2 + [pltpu.SemaphoreType.DMA((2,))] + scratch,
        cost(len(some)),
    )
    out = out.reshape(1, rounds, groups, slots, lag_band)
    return out[:, :, :, :capacity]


def solution(mesh):
    placed = (P("grp", None, "freq"), P("grp"), P("grp", None, None, None))
    return jax.shard_map(
        per_device,
        mesh=mesh,
        in_specs=placed,
        out_specs=P("grp", None, None, None, "freq"),
        check_vma=False,
    )
```

```python
import functools
import math

import jax
import jax.numpy as jnp
from jax import lax
from jax.experimental import pallas as pl
from jax.experimental.pallas import tpu as pltpu
from jax.sharding import PartitionSpec as P

LAGS = 4096
LANES = 128
SUBLANES = 8
PARTS = 4


def split_bf16(values, parts):
    pieces = []
    for _ in range(parts - 1):
        piece = values.astype(jnp.bfloat16)
        pieces.append(piece)
        values = values - piece.astype(jnp.float32)
    pieces.append(values.astype(jnp.bfloat16))
    return pieces


def iota(shape, axis):
    return lax.broadcasted_iota(jnp.int32, shape, axis)


def dot(left, right):
    return jnp.dot(left, right, preferred_element_type=jnp.float32)


def padded(count, multiple):
    return -(-count // multiple) * multiple


def pick_slots(extras, places, me, stations, rounds, slots):
    groups = len(extras)
    pairs = stations * stations
    listed = rounds * pairs
    rows = rounds * groups * slots
    place = iota((groups, groups), 1)
    held_by = jnp.zeros((groups, groups), jnp.int32)
    for position in range(groups):
        held_by = jnp.where(place == position, places[position], held_by)
    lane = iota((1, listed), 1)

    def by_group(row, shift):
        wanted = (iota((groups, groups), 0) + groups - shift) % groups
        held = jnp.concatenate([extra[row : row + 1, :] for extra in extras], axis=0)
        return dot((held_by == wanted).astype(jnp.bfloat16), held.astype(jnp.bfloat16))

    def of_station(values, number):
        spread = iota((LANES, listed), 0) == number
        return dot(values.astype(jnp.bfloat16), spread.astype(jnp.bfloat16))

    owner_ids = jnp.zeros((groups, listed), jnp.float32)
    partner_mask = jnp.zeros((groups, listed), jnp.float32)
    for index in range(rounds):
        of_round = lane // pairs == index
        owner_ids = jnp.where(of_round, by_group(index, 0), owner_ids)
        second = of_station(by_group(rounds, index + 1), lane % stations)
        partner_mask = jnp.where(of_round, second, partner_mask)
    own_mask = of_station(by_group(rounds, 0), lane % pairs // stations)
    pair_weight = own_mask * partner_mask
    mine = owner_ids == me.astype(jnp.float32)
    from_pair, to_pair = iota((listed, listed), 0), iota((listed, listed), 1)
    before = (from_pair < to_pair) & (from_pair // pairs == to_pair // pairs)
    rank = dot(mine.astype(jnp.bfloat16), before.astype(jnp.bfloat16))
    marked = jnp.where(mine, rank, -1.0).astype(jnp.bfloat16)
    of_group = (iota((rows, groups), 0) // slots) % groups == iota((rows, groups), 1)
    of_group = of_group.astype(jnp.bfloat16)
    row_id, lane_id = iota((rows, listed), 0), iota((rows, listed), 1)
    chosen = (dot(of_group, marked) == (row_id % slots).astype(jnp.float32)) & (
        row_id // (groups * slots) == lane_id // pairs
    )
    weighed = jnp.where(chosen, dot(of_group, pair_weight.astype(jnp.bfloat16)), 0.0)
    weight = dot(weighed.astype(jnp.bfloat16), jnp.ones((listed, LANES), jnp.bfloat16))
    chosen = chosen.astype(jnp.bfloat16)
    pair_id = iota((listed, LANES), 0) % pairs
    first = dot(chosen, (pair_id // stations).astype(jnp.bfloat16))
    second = dot(chosen, (pair_id % stations).astype(jnp.bfloat16))
    return first.astype(jnp.int32), second.astype(jnp.int32), weight


def band_moves(shards):
    return [0] + list(range(shards - 2, 0, -2))


def make_tables(parity, table_refs, turn_refs, base_refs, bin_total):
    place = lax.axis_index("freq").astype(jnp.int32)
    near_cos, near_sin = base_refs
    fine, half_band = near_cos.shape
    steps, chunks, _ = turn_refs[0].shape
    band_bins = chunks * LANES
    moves = band_moves(bin_total // band_bins)

    def circle(turns):
        angles = (turns & (4 * bin_total - 1)).astype(jnp.float32) * (math.pi / (2 * bin_total))
        return jnp.cos(angles), jnp.sin(angles)

    def every(count, start, step):
        bins = start + iota((count, half_band), 0) * step
        return circle(bins * (2 * iota((count, half_band), 1) + 1))

    def added(cos, sin, other_cos, other_sin):
        return cos * other_cos - sin * other_sin, sin * other_cos + cos * other_sin

    low_cos, low_sin = every(SUBLANES, 0, 1)
    high_cos, high_sin = every(fine // SUBLANES, 0, SUBLANES)
    for index in range(fine // SUBLANES):
        rows, one = slice(index * SUBLANES, (index + 1) * SUBLANES), slice(index, index + 1)
        near_cos[rows, :], near_sin[rows, :] = added(
            high_cos[one], high_sin[one], low_cos, low_sin
        )

    centre = 2 * half_band * (2 * place + 1) - 1 - LAGS
    norm = 1.0 / math.sqrt(bin_total)
    for step in range(steps):
        start = (place ^ (moves[step] + parity)) * band_bins
        cos, sin = every(band_bins // fine, start, fine)
        for part in range(band_bins // fine):
            one = slice(part, part + 1)
            values = added(cos[one], sin[one], near_cos[...], near_sin[...])
            rows = slice(step * band_bins + part * fine, step * band_bins + (part + 1) * fine)
            for table, value in zip(table_refs, values):
                table[rows, :half_band], table[rows, half_band:] = split_bf16(value, 2)
        bins = start + iota((chunks, LANES), 0) * LANES + iota((chunks, LANES), 1)
        for turn, value in zip(turn_refs, circle(bins * centre)):
            turn[step] = value * norm


def table_kernel(bin_total, owners_hbm, mask_hbm, *refs):
    near_refs, far_refs, extras = refs[:4], refs[4:8], refs[8]
    base_refs, (owners_ref, mask_ref, sems) = refs[9:11], refs[11:]
    copies = [
        pltpu.make_async_copy(owners_hbm, owners_ref, sems.at[0]),
        pltpu.make_async_copy(mask_hbm, mask_ref, sems.at[1]),
    ]
    for copy in copies:
        copy.start()
    make_tables(0, near_refs[:2], near_refs[2:], base_refs, bin_total)
    make_tables(1, far_refs[:2], far_refs[2:], base_refs, bin_total)
    for copy in copies:
        copy.wait()
    extras[...] = jnp.zeros_like(extras)
    rounds, pairs = owners_ref.shape[1], owners_ref.shape[3]
    for index in range(rounds):
        lanes = slice(index * pairs, (index + 1) * pairs)
        extras[index : index + 1, lanes] = owners_ref[0, index].astype(jnp.float32)
    extras[rounds : rounds + 1, : mask_ref.shape[1]] = mask_ref[...].astype(jnp.float32)


def add_bands(sizes, steps, places, turn_refs, table_refs, blocks, picks, sums, scratch):
    groups, stations, rounds, slots, band_bins = sizes
    chunks = band_bins // LANES
    depth = 2 * chunks * stations
    half = sums[0].shape[1]
    first, second = picks
    sets = [scratch[6 * index : 6 * (index + 1)] for index in range(2)]
    part_groups = [range(part * groups // PARTS, (part + 1) * groups // PARTS) for part in range(PARTS)]
    bins_at_once = max(band_bins // 2, LANES)
    pieces = [(which, start) for which in range(2) for start in range(0, band_bins, bins_at_once)]

    def prepare(index):
        (step, place_step), (held, turned) = steps[index], sets[index % 2][:2]
        for position, (ref, offset) in enumerate(blocks):
            group = places[position]
            for q in range(chunks):
                turn_cos, turn_sin = [turn[step, q : q + 1, :] for turn in turn_refs]
                start = offset + place_step * depth + q * stations
                real = ref[start : start + stations, :]
                start += chunks * stations
                imag = ref[start : start + stations, :]
                held[group, q] = real
                held[group, chunks + q] = imag
                turned[group, q] = real * turn_cos + imag * turn_sin
                turned[group, chunks + q] = imag * turn_cos - real * turn_sin

    def multiply(index, part):
        held, turned, *cross = sets[index % 2]
        for group in part_groups[part]:
            sources = []
            for number in range(rounds):
                start = (number * groups + group) * slots
                lines = [slice(start + o, start + o + SUBLANES) for o in range(0, slots, SUBLANES)]
                partner = (group + groups - 1 - number) % groups
                sources.append((start, partner, [(first[line, :], second[line, :]) for line in lines]))
            for q in range(chunks):
                lanes = slice(q * LANES, (q + 1) * LANES)
                own_real, own_imag = held[group, q], held[group, chunks + q]
                for start, partner, indices in sources:
                    real, imag = turned[partner, q], turned[partner, chunks + q]
                    reals, imags = [], []
                    for index_a, index_b in indices:
                        a_real = jnp.take_along_axis(own_real, index_a, axis=0)
                        a_imag = jnp.take_along_axis(own_imag, index_a, axis=0)
                        b_real = jnp.take_along_axis(real, index_b, axis=0)
                        b_imag = jnp.take_along_axis(imag, index_b, axis=0)
                        reals.append(a_real * b_real + a_imag * b_imag)
                        imags.append(a_imag * b_real - a_real * b_imag)
                    rows = slice(start, start + slots)
                    for place, values in ((0, reals), (2, imags)):
                        high, low = split_bf16(jnp.concatenate(values, axis=0), 2)
                        cross[place][rows, lanes] = high
                        cross[place + 1][rows, lanes] = low

    def transform(index, which, start):
        step, (high, low) = steps[index][0], sets[index % 2][2 + 2 * which : 4 + 2 * which]
        lanes = slice(start, start + bins_at_once)
        bins = slice(step * band_bins + start, step * band_bins + start + bins_at_once)
        table, total = table_refs[which], sums[which]
        cross, exact = high[:, lanes], table[bins, :half]
        total[...] += dot(
            jnp.concatenate([cross, cross, low[:, lanes]], axis=1),
            jnp.concatenate([exact, table[bins, half:], exact], axis=0),
        )

    prepare(0)
    for part in range(PARTS):
        multiply(0, part)
    for index in range(len(steps)):
        more = index + 1 < len(steps)
        if more:
            prepare(index + 1)
        for part in range(PARTS):
            if more:
                multiply(index + 1, part)
            if part < len(pieces):
                transform(index, *pieces[part])


def placed_blocks(array_refs, layout, groups):
    me = lax.axis_index("grp").astype(jnp.int32)
    blocks = [(array_refs[index], offset) for index, offset, _ in layout]
    return blocks, [moved(me, move, groups) for _, _, move in layout]


def near_kernel(sizes, layout, array_count, depth, steps, *refs):
    groups, stations, rounds, slots = sizes[:4]
    turn_refs, table_refs, refs = refs[:2], refs[2:4], refs[4:]
    array_refs, refs = refs[:array_count], refs[array_count:]
    (first, second, weight, even, odd), scratch = refs[:5], refs[5:]
    blocks, places = placed_blocks(array_refs, layout, groups)
    extras = [ref[offset + depth : offset + depth + SUBLANES, :] for ref, offset in blocks]
    first[...], second[...], weight[...] = pick_slots(
        extras, places, lax.axis_index("grp"), stations, rounds, slots
    )
    even[...] = jnp.zeros_like(even)
    odd[...] = jnp.zeros_like(odd)
    add_bands(
        sizes, steps, places, turn_refs, table_refs, blocks, (first, second), (even, odd), scratch
    )


def next_kernel(sizes, layout, array_count, steps, *refs):
    turn_refs, table_refs, refs = refs[:2], refs[2:4], refs[4:]
    array_refs, refs = refs[:array_count], refs[array_count:]
    (first, second, even_in, odd_in, even, odd), scratch = refs[:6], refs[6:]
    even[...] = even_in[...]
    odd[...] = odd_in[...]
    blocks, places = placed_blocks(array_refs, layout, sizes[0])
    add_bands(
        sizes, steps, places, turn_refs, table_refs, blocks, (first, second), (even, odd), scratch
    )


def last_kernel(sizes, layout, array_count, steps, *refs):
    turn_refs, table_refs, refs = refs[:2], refs[2:4], refs[4:]
    array_refs, refs = refs[:array_count], refs[array_count:]
    first, second, even_in, odd_in, weight, out_ref, even, odd, result, sems = refs[:10]
    even[...] = even_in[...]
    odd[...] = odd_in[...]
    blocks, places = placed_blocks(array_refs, layout, sizes[0])
    add_bands(
        sizes, steps, places, turn_refs, table_refs, blocks, (first, second), (even, odd), refs[10:]
    )
    half = even.shape[1]
    mirror = (iota((half, half), 0) + iota((half, half), 1) == half - 1).astype(jnp.bfloat16)
    copies = []
    block = even.shape[0] // PARTS
    for part in range(PARTS):
        lines = slice(part * block, (part + 1) * block)
        row_weight = weight[lines, 0:1]
        high, low = split_bf16((even[lines, :] + odd[lines, :]) * row_weight, 2)
        result[lines, :half] = dot(high, mirror) + dot(low, mirror)
        result[lines, half:] = (even[lines, :] - odd[lines, :]) * row_weight
        copies.append(pltpu.make_async_copy(result.at[lines], out_ref.at[lines], sems.at[part]))
        copies[part].start()
    for copy in copies:
        copy.wait()


def moved(me, move, size):
    return me ^ move if size & (size - 1) == 0 else lax.rem(me + size - move, size)


def moved_index(me, move, size):
    return me ^ move if size & (size - 1) == 0 else (me - move) % size


def fetched(block, group_move, band_move):
    groups, shards = lax.axis_size("grp"), lax.axis_size("freq")
    route = [
        (
            moved_index(group, group_move, groups) * shards + moved_index(band, band_move, shards),
            group * shards + band,
        )
        for group in range(groups)
        for band in range(shards)
    ]
    return lax.ppermute(block, ("grp", "freq"), route)


def exchange(column, parts):
    groups = lax.axis_size("grp")
    if groups != 4:
        near = [column] + [fetched(column, move, 0) for move in range(1, groups)]
        layout = [(move, 0, move) for move in range(groups)]
        far = [fetched(column, move, 1) for move in range(groups)]
        return near, layout, far, [[] for _ in parts]
    across, core = fetched(column, 2, 0), fetched(column, 1, 0)
    beside = fetched(longer(column), 0, 1)
    across, core = lax.optimization_barrier((across, core))
    near = [column, core, across, fetched(across, 1, 0)]
    diagonals = [[fetched(longer(across[start:stop]), 0, 1)] for start, stop in parts]
    far = [beside, fetched(beside, 1, 0)]
    return near, [(place, 0, place) for place in range(4)], far, diagonals


def longer(block):
    return jnp.concatenate([block, block[-SUBLANES:]], axis=0)


def across_cores(far, diagonal, first_row):
    arrays = far + [block for own in diagonal for block in (own, fetched(own, 1, 0))]
    layout = [
        (place, 0 if place < len(far) else -first_row, place) for place in range(len(arrays))
    ]
    return arrays, layout


def per_device(spectra, station_mask, owners):
    stations, _, band_bins = spectra.shape
    groups = lax.axis_size("grp")
    shards = lax.axis_size("freq")
    rounds = owners.shape[1]
    pairs = stations * stations
    bin_total = band_bins * shards
    capacity = (2 * pairs + groups - 1) // groups
    slots = padded(capacity, 2 * SUBLANES)
    lag_band = LAGS // shards
    half_band = lag_band // 2
    chunks = band_bins // LANES
    rows = rounds * groups * slots

    vector = pl.BlockSpec(memory_space=pltpu.VMEM)
    in_hbm = pl.BlockSpec(memory_space=pltpu.HBM)

    def call(kernel, name, arrays, out_shape, scratch, cost, others=()):
        arrays = [pltpu.with_memory_space_constraint(array, pltpu.VMEM) for array in arrays]
        others = [pltpu.with_memory_space_constraint(array, pltpu.HBM) for array in others]
        to_hbm = isinstance(out_shape, jax.ShapeDtypeStruct)
        return pl.pallas_call(
            kernel,
            out_shape=out_shape,
            in_specs=[in_hbm] * len(others) + [vector] * len(arrays),
            out_specs=in_hbm if to_hbm else [vector] * len(out_shape),
            scratch_shapes=scratch,
            compiler_params=pltpu.CompilerParams(vmem_limit_bytes=24 * 1024 * 1024),
            cost_estimate=cost,
            name=name,
        )(*others, *arrays)

    steps = shards // 2
    tiles = spectra.reshape(stations, 2, chunks, LANES).transpose(1, 2, 0, 3)
    tiles = tiles.reshape(2 * chunks * stations, LANES)
    column = [fetched(tiles, 0, move) if move else tiles for move in band_moves(shards)]

    table = pltpu.VMEM((steps * band_bins, lag_band), jnp.bfloat16)
    turn = pltpu.VMEM((steps, chunks, LANES), jnp.float32)
    base = pltpu.VMEM((64, half_band), jnp.float32)
    table_cost = pl.CostEstimate(
        flops=0, bytes_accessed=4 * bin_total * half_band, transcendentals=0
    )
    *band_tables, extras = call(
        functools.partial(table_kernel, bin_total),
        "tables",
        [],
        ([table] * 2 + [turn] * 2) * 2 + [pltpu.VMEM((SUBLANES, LANES), jnp.float32)],
        [base] * 2
        + [
            pltpu.VMEM((1, rounds, 1, pairs), jnp.int32),
            pltpu.VMEM((1, stations), jnp.int32),
            pltpu.SemaphoreType.DMA((2,)),
        ],
        table_cost,
        [owners.transpose(0, 1, 3, 2), station_mask.reshape(1, stations)],
    )
    column = jnp.concatenate(column + [extras], axis=0)
    depth = 2 * chunks * stations
    split, middle = steps - steps // 4, steps // 2
    parts = [(0, middle * depth), (middle * depth, steps * depth)]
    near, layout, far, diagonals = exchange(column, parts)

    sizes = (groups, stations, rounds, slots, band_bins)
    spectrum = pltpu.VMEM((groups, 2 * chunks, stations, LANES), jnp.float32)
    cross = pltpu.VMEM((rows, band_bins), jnp.bfloat16)
    scratch = ([spectrum] * 2 + [cross] * 4) * 2

    def cost(count):
        flops = 6 * rows * band_bins * lag_band * count
        return pl.CostEstimate(flops=flops, bytes_accessed=2 * 1024 * 1024, transcendentals=0)

    total = pltpu.VMEM((rows, half_band), jnp.float32)
    index = pltpu.VMEM((rows, LANES), jnp.int32)
    near_table = [band_tables[place] for place in (2, 3, 0, 1)]
    far_table = [band_tables[place] for place in (6, 7, 4, 5)]

    first, second, weight, even, odd = call(
        functools.partial(
            near_kernel, sizes, layout, len(near), steps * depth, [(i, i) for i in range(split)]
        ),
        "near_first",
        near_table + near,
        [index] * 2 + [pltpu.VMEM((rows, LANES), jnp.float32)] + [total] * 2,
        scratch,
        cost(split),
    )
    def add(name, layout, arrays, tables, some, sums):
        return call(
            functools.partial(next_kernel, sizes, layout, len(arrays), [(i, i) for i in some]),
            name,
            [*tables, *arrays, first, second, *sums],
            [total] * 2,
            scratch,
            cost(len(some)),
        )

    *diagonal, even = lax.optimization_barrier((*diagonals[0], even))
    far_first, layout_first = across_cores(far, diagonal, parts[0][0])
    even, odd = add("near_next", layout, near, near_table, range(split, steps), (even, odd))
    *diagonal, even = lax.optimization_barrier((*diagonals[1], even))
    far_next, layout_next = across_cores(far, diagonal, parts[1][0])
    even, odd = add("far_first", layout_first, far_first, far_table, range(middle), (even, odd))
    some = [(i, i) for i in range(middle, steps)]
    out = call(
        functools.partial(last_kernel, sizes, layout_next, len(far_next), some),
        "far_next",
        [*far_table, *far_next, first, second, even, odd, weight],
        jax.ShapeDtypeStruct((rows, lag_band), jnp.float32),
        [total] * 2 + [pltpu.VMEM((rows, lag_band), jnp.float32), pltpu.SemaphoreType.DMA((PARTS,))] + scratch,
        cost(len(some)),
    )
    out = out.reshape(1, rounds, groups, slots, lag_band)
    return out[:, :, :, :capacity]


def solution(mesh):
    placed = (P("grp", None, "freq"), P("grp"), P("grp", None, None, None))
    return jax.shard_map(
        per_device,
        mesh=mesh,
        in_specs=placed,
        out_specs=P("grp", None, None, None, "freq"),
        check_vma=False,
    )
```

```python
import functools
import math

import jax
import jax.numpy as jnp
from jax import lax
from jax.experimental import pallas as pl
from jax.experimental.pallas import tpu as pltpu
from jax.sharding import PartitionSpec as P

LAGS = 4096
LANES = 128
SUBLANES = 8
PARTS = 4


def split_bf16(values, parts):
    pieces = []
    for _ in range(parts - 1):
        piece = values.astype(jnp.bfloat16)
        pieces.append(piece)
        values = values - piece.astype(jnp.float32)
    pieces.append(values.astype(jnp.bfloat16))
    return pieces


def iota(shape, axis):
    return lax.broadcasted_iota(jnp.int32, shape, axis)


def dot(left, right):
    return jnp.dot(left, right, preferred_element_type=jnp.float32)


def padded(count, multiple):
    return -(-count // multiple) * multiple


def pick_slots(extras, places, me, stations, rounds, slots):
    groups = len(extras)
    pairs = stations * stations
    listed = rounds * pairs
    rows = rounds * groups * slots
    place = iota((groups, groups), 1)
    held_by = jnp.zeros((groups, groups), jnp.int32)
    for position in range(groups):
        held_by = jnp.where(place == position, places[position], held_by)
    lane = iota((1, listed), 1)

    def by_group(row, shift):
        wanted = (iota((groups, groups), 0) + groups - shift) % groups
        held = jnp.concatenate([extra[row : row + 1, :] for extra in extras], axis=0)
        return dot((held_by == wanted).astype(jnp.bfloat16), held.astype(jnp.bfloat16))

    def of_station(values, number):
        spread = iota((LANES, listed), 0) == number
        return dot(values.astype(jnp.bfloat16), spread.astype(jnp.bfloat16))

    owner_ids = jnp.zeros((groups, listed), jnp.float32)
    partner_mask = jnp.zeros((groups, listed), jnp.float32)
    for index in range(rounds):
        of_round = lane // pairs == index
        owner_ids = jnp.where(of_round, by_group(index, 0), owner_ids)
        second = of_station(by_group(rounds, index + 1), lane % stations)
        partner_mask = jnp.where(of_round, second, partner_mask)
    own_mask = of_station(by_group(rounds, 0), lane % pairs // stations)
    pair_weight = own_mask * partner_mask
    mine = owner_ids == me.astype(jnp.float32)
    from_pair, to_pair = iota((listed, listed), 0), iota((listed, listed), 1)
    before = (from_pair < to_pair) & (from_pair // pairs == to_pair // pairs)
    rank = dot(mine.astype(jnp.bfloat16), before.astype(jnp.bfloat16))
    marked = jnp.where(mine, rank, -1.0).astype(jnp.bfloat16)
    of_group = (iota((rows, groups), 0) // slots) % groups == iota((rows, groups), 1)
    of_group = of_group.astype(jnp.bfloat16)
    row_id, lane_id = iota((rows, listed), 0), iota((rows, listed), 1)
    chosen = (dot(of_group, marked) == (row_id % slots).astype(jnp.float32)) & (
        row_id // (groups * slots) == lane_id // pairs
    )
    weighed = jnp.where(chosen, dot(of_group, pair_weight.astype(jnp.bfloat16)), 0.0)
    weight = dot(weighed.astype(jnp.bfloat16), jnp.ones((listed, LANES), jnp.bfloat16))
    chosen = chosen.astype(jnp.bfloat16)
    pair_id = iota((listed, LANES), 0) % pairs
    first = dot(chosen, (pair_id // stations).astype(jnp.bfloat16))
    second = dot(chosen, (pair_id % stations).astype(jnp.bfloat16))
    columns = 2 * groups * stations
    row_id, column = iota((rows, columns), 0), iota((rows, columns), 1)
    partner = ((row_id // slots) % groups + groups - 1 - row_id // (groups * slots)) % groups
    wanted = partner * stations + second[:, 0:1].astype(jnp.int32)
    picks_second = (column % (groups * stations) == wanted).astype(jnp.bfloat16)
    return first.astype(jnp.int32), picks_second, weight


def band_moves(shards):
    return [0] + list(range(shards - 2, 0, -2))


def make_tables(parity, table_refs, turn_refs, base_refs, bin_total):
    place = lax.axis_index("freq").astype(jnp.int32)
    near_cos, near_sin = base_refs
    fine, half_band = near_cos.shape
    steps, chunks, _ = turn_refs[0].shape
    band_bins = chunks * LANES
    moves = band_moves(bin_total // band_bins)

    def circle(turns):
        angles = (turns & (4 * bin_total - 1)).astype(jnp.float32) * (math.pi / (2 * bin_total))
        return jnp.cos(angles), jnp.sin(angles)

    def every(count, start, step):
        bins = start + iota((count, half_band), 0) * step
        return circle(bins * (2 * iota((count, half_band), 1) + 1))

    def added(cos, sin, other_cos, other_sin):
        return cos * other_cos - sin * other_sin, sin * other_cos + cos * other_sin

    low_cos, low_sin = every(SUBLANES, 0, 1)
    high_cos, high_sin = every(fine // SUBLANES, 0, SUBLANES)
    for index in range(fine // SUBLANES):
        rows, one = slice(index * SUBLANES, (index + 1) * SUBLANES), slice(index, index + 1)
        near_cos[rows, :], near_sin[rows, :] = added(
            high_cos[one], high_sin[one], low_cos, low_sin
        )

    centre = 2 * half_band * (2 * place + 1) - 1 - LAGS
    norm = 1.0 / math.sqrt(bin_total)
    for step in range(steps):
        start = (place ^ (moves[step] + parity)) * band_bins
        cos, sin = every(band_bins // fine, start, fine)
        for part in range(band_bins // fine):
            one = slice(part, part + 1)
            values = added(cos[one], sin[one], near_cos[...], near_sin[...])
            rows = slice(step * band_bins + part * fine, step * band_bins + (part + 1) * fine)
            for table, value in zip(table_refs, values):
                table[rows, :half_band], table[rows, half_band:] = split_bf16(value, 2)
        bins = start + iota((chunks, LANES), 0) * LANES + iota((chunks, LANES), 1)
        for turn, value in zip(turn_refs, circle(bins * centre)):
            turn[step] = value * norm


def table_kernel(bin_total, owners_hbm, mask_hbm, *refs):
    near_refs, far_refs, extras = refs[:4], refs[4:8], refs[8]
    base_refs, (owners_ref, mask_ref, sems) = refs[9:11], refs[11:]
    copies = [
        pltpu.make_async_copy(owners_hbm, owners_ref, sems.at[0]),
        pltpu.make_async_copy(mask_hbm, mask_ref, sems.at[1]),
    ]
    for copy in copies:
        copy.start()
    make_tables(0, near_refs[:2], near_refs[2:], base_refs, bin_total)
    make_tables(1, far_refs[:2], far_refs[2:], base_refs, bin_total)
    for copy in copies:
        copy.wait()
    extras[...] = jnp.zeros_like(extras)
    rounds, pairs = owners_ref.shape[1], owners_ref.shape[3]
    for index in range(rounds):
        lanes = slice(index * pairs, (index + 1) * pairs)
        extras[index : index + 1, lanes] = owners_ref[0, index].astype(jnp.float32)
    extras[rounds : rounds + 1, : mask_ref.shape[1]] = mask_ref[...].astype(jnp.float32)


def add_bands(sizes, steps, places, turn_refs, table_refs, blocks, picks, sums, scratch):
    groups, stations, rounds, slots, band_bins = sizes
    chunks = band_bins // LANES
    depth = 2 * chunks * stations
    half = sums[0].shape[1]
    first, second = picks
    sets = [scratch[7 * index : 7 * (index + 1)] for index in range(2)]
    part_groups = [range(part * groups // PARTS, (part + 1) * groups // PARTS) for part in range(PARTS)]
    bins_at_once = max(band_bins // 2, LANES)
    pieces = [(which, start) for which in range(2) for start in range(0, band_bins, bins_at_once)]

    def prepare(index):
        (step, place_step), (held, turned, second_of) = steps[index], sets[index % 2][:3]
        for position, (ref, offset) in enumerate(blocks):
            group = places[position]
            for q in range(chunks):
                turn_cos, turn_sin = [turn[step, q : q + 1, :] for turn in turn_refs]
                start = offset + place_step * depth + q * stations
                real = ref[start : start + stations, :]
                start += chunks * stations
                imag = ref[start : start + stations, :]
                held[group, q] = real
                held[group, chunks + q] = imag
                turned[group, q] = real * turn_cos + imag * turn_sin
                turned[group, chunks + q] = imag * turn_cos - real * turn_sin
        parts = [
            jnp.concatenate(split_bf16(turned[:, q].reshape(groups * stations, LANES), 2), axis=0)
            for q in range(2 * chunks)
        ]
        second_of[...] = dot(second[...], jnp.concatenate(parts, axis=1))

    def multiply(index, part):
        held, _, second_of, *cross = sets[index % 2]
        for group in part_groups[part]:
            sources = []
            for number in range(rounds):
                start = (number * groups + group) * slots
                lines = [slice(start + o, start + o + SUBLANES) for o in range(0, slots, SUBLANES)]
                sources.append((start, [(line, first[line, :]) for line in lines]))
            for q in range(chunks):
                lanes = slice(q * LANES, (q + 1) * LANES)
                imag_lanes = slice((chunks + q) * LANES, (chunks + q + 1) * LANES)
                own_real, own_imag = held[group, q], held[group, chunks + q]
                for start, indices in sources:
                    reals, imags = [], []
                    for line, index_a in indices:
                        a_real = jnp.take_along_axis(own_real, index_a, axis=0)
                        a_imag = jnp.take_along_axis(own_imag, index_a, axis=0)
                        b_real, b_imag = second_of[line, lanes], second_of[line, imag_lanes]
                        reals.append(a_real * b_real + a_imag * b_imag)
                        imags.append(a_imag * b_real - a_real * b_imag)
                    rows = slice(start, start + slots)
                    for place, values in ((0, reals), (2, imags)):
                        high, low = split_bf16(jnp.concatenate(values, axis=0), 2)
                        cross[place][rows, lanes] = high
                        cross[place + 1][rows, lanes] = low

    def transform(index, which, start):
        step, (high, low) = steps[index][0], sets[index % 2][3 + 2 * which : 5 + 2 * which]
        lanes = slice(start, start + bins_at_once)
        bins = slice(step * band_bins + start, step * band_bins + start + bins_at_once)
        table, total = table_refs[which], sums[which]
        cross, exact = high[:, lanes], table[bins, :half]
        total[...] += dot(
            jnp.concatenate([cross, cross, low[:, lanes]], axis=1),
            jnp.concatenate([exact, table[bins, half:], exact], axis=0),
        )

    prepare(0)
    for part in range(PARTS):
        multiply(0, part)
    for index in range(len(steps)):
        more = index + 1 < len(steps)
        if more:
            prepare(index + 1)
        for part in range(PARTS):
            if more:
                multiply(index + 1, part)
            if part < len(pieces):
                transform(index, *pieces[part])


def placed_blocks(array_refs, layout, groups):
    me = lax.axis_index("grp").astype(jnp.int32)
    blocks = [(array_refs[index], offset) for index, offset, _ in layout]
    return blocks, [moved(me, move, groups) for _, _, move in layout]


def near_kernel(sizes, layout, array_count, depth, steps, *refs):
    groups, stations, rounds, slots = sizes[:4]
    turn_refs, table_refs, refs = refs[:2], refs[2:4], refs[4:]
    array_refs, refs = refs[:array_count], refs[array_count:]
    (first, second, weight, even, odd), scratch = refs[:5], refs[5:]
    blocks, places = placed_blocks(array_refs, layout, groups)
    extras = [ref[offset + depth : offset + depth + SUBLANES, :] for ref, offset in blocks]
    first[...], second[...], weight[...] = pick_slots(
        extras, places, lax.axis_index("grp"), stations, rounds, slots
    )
    even[...] = jnp.zeros_like(even)
    odd[...] = jnp.zeros_like(odd)
    add_bands(
        sizes, steps, places, turn_refs, table_refs, blocks, (first, second), (even, odd), scratch
    )


def next_kernel(sizes, layout, array_count, steps, *refs):
    turn_refs, table_refs, refs = refs[:2], refs[2:4], refs[4:]
    array_refs, refs = refs[:array_count], refs[array_count:]
    (first, second, even_in, odd_in, even, odd), scratch = refs[:6], refs[6:]
    even[...] = even_in[...]
    odd[...] = odd_in[...]
    blocks, places = placed_blocks(array_refs, layout, sizes[0])
    add_bands(
        sizes, steps, places, turn_refs, table_refs, blocks, (first, second), (even, odd), scratch
    )


def last_kernel(sizes, layout, array_count, steps, *refs):
    turn_refs, table_refs, refs = refs[:2], refs[2:4], refs[4:]
    array_refs, refs = refs[:array_count], refs[array_count:]
    first, second, even_in, odd_in, weight, out_ref, even, odd, result, sems = refs[:10]
    even[...] = even_in[...]
    odd[...] = odd_in[...]
    blocks, places = placed_blocks(array_refs, layout, sizes[0])
    add_bands(
        sizes, steps, places, turn_refs, table_refs, blocks, (first, second), (even, odd), refs[10:]
    )
    half = even.shape[1]
    mirror = (iota((half, half), 0) + iota((half, half), 1) == half - 1).astype(jnp.bfloat16)
    copies = []
    block = even.shape[0] // PARTS
    for part in range(PARTS):
        lines = slice(part * block, (part + 1) * block)
        row_weight = weight[lines, 0:1]
        high, low = split_bf16((even[lines, :] + odd[lines, :]) * row_weight, 2)
        result[lines, :half] = dot(high, mirror) + dot(low, mirror)
        result[lines, half:] = (even[lines, :] - odd[lines, :]) * row_weight
        copies.append(pltpu.make_async_copy(result.at[lines], out_ref.at[lines], sems.at[part]))
        copies[part].start()
    for copy in copies:
        copy.wait()


def moved(me, move, size):
    return me ^ move if size & (size - 1) == 0 else lax.rem(me + size - move, size)


def moved_index(me, move, size):
    return me ^ move if size & (size - 1) == 0 else (me - move) % size


def fetched(block, group_move, band_move):
    groups, shards = lax.axis_size("grp"), lax.axis_size("freq")
    route = [
        (
            moved_index(group, group_move, groups) * shards + moved_index(band, band_move, shards),
            group * shards + band,
        )
        for group in range(groups)
        for band in range(shards)
    ]
    return lax.ppermute(block, ("grp", "freq"), route)


def exchange(column, parts):
    groups = lax.axis_size("grp")
    if groups != 4:
        near = [column] + [fetched(column, move, 0) for move in range(1, groups)]
        layout = [(move, 0, move) for move in range(groups)]
        far = [fetched(column, move, 1) for move in range(groups)]
        return near, layout, far, [[] for _ in parts]
    across, core = fetched(column, 2, 0), fetched(column, 1, 0)
    beside = fetched(longer(column), 0, 1)
    across, core = lax.optimization_barrier((across, core))
    near = [column, core, across, fetched(across, 1, 0)]
    diagonals = [[fetched(longer(across[start:stop]), 0, 1)] for start, stop in parts]
    far = [beside, fetched(beside, 1, 0)]
    return near, [(place, 0, place) for place in range(4)], far, diagonals


def longer(block):
    return jnp.concatenate([block, block[-SUBLANES:]], axis=0)


def across_cores(far, diagonal, first_row):
    arrays = far + [block for own in diagonal for block in (own, fetched(own, 1, 0))]
    layout = [
        (place, 0 if place < len(far) else -first_row, place) for place in range(len(arrays))
    ]
    return arrays, layout


def per_device(spectra, station_mask, owners):
    stations, _, band_bins = spectra.shape
    groups = lax.axis_size("grp")
    shards = lax.axis_size("freq")
    rounds = owners.shape[1]
    pairs = stations * stations
    bin_total = band_bins * shards
    capacity = (2 * pairs + groups - 1) // groups
    slots = padded(capacity, 2 * SUBLANES)
    lag_band = LAGS // shards
    half_band = lag_band // 2
    chunks = band_bins // LANES
    rows = rounds * groups * slots

    vector = pl.BlockSpec(memory_space=pltpu.VMEM)
    in_hbm = pl.BlockSpec(memory_space=pltpu.HBM)

    def call(kernel, name, arrays, out_shape, scratch, cost, others=()):
        arrays = [pltpu.with_memory_space_constraint(array, pltpu.VMEM) for array in arrays]
        others = [pltpu.with_memory_space_constraint(array, pltpu.HBM) for array in others]
        to_hbm = isinstance(out_shape, jax.ShapeDtypeStruct)
        return pl.pallas_call(
            kernel,
            out_shape=out_shape,
            in_specs=[in_hbm] * len(others) + [vector] * len(arrays),
            out_specs=in_hbm if to_hbm else [vector] * len(out_shape),
            scratch_shapes=scratch,
            compiler_params=pltpu.CompilerParams(vmem_limit_bytes=24 * 1024 * 1024),
            cost_estimate=cost,
            name=name,
        )(*others, *arrays)

    steps = shards // 2
    tiles = spectra.reshape(stations, 2, chunks, LANES).transpose(1, 2, 0, 3)
    tiles = tiles.reshape(2 * chunks * stations, LANES)
    column = [fetched(tiles, 0, move) if move else tiles for move in band_moves(shards)]

    table = pltpu.VMEM((steps * band_bins, lag_band), jnp.bfloat16)
    turn = pltpu.VMEM((steps, chunks, LANES), jnp.float32)
    base = pltpu.VMEM((64, half_band), jnp.float32)
    table_cost = pl.CostEstimate(
        flops=0, bytes_accessed=4 * bin_total * half_band, transcendentals=0
    )
    *band_tables, extras = call(
        functools.partial(table_kernel, bin_total),
        "tables",
        [],
        ([table] * 2 + [turn] * 2) * 2 + [pltpu.VMEM((SUBLANES, LANES), jnp.float32)],
        [base] * 2
        + [
            pltpu.VMEM((1, rounds, 1, pairs), jnp.int32),
            pltpu.VMEM((1, stations), jnp.int32),
            pltpu.SemaphoreType.DMA((2,)),
        ],
        table_cost,
        [owners.transpose(0, 1, 3, 2), station_mask.reshape(1, stations)],
    )
    column = jnp.concatenate(column + [extras], axis=0)
    depth = 2 * chunks * stations
    split, middle = steps - steps // 4, steps // 2
    parts = [(0, middle * depth), (middle * depth, steps * depth)]
    near, layout, far, diagonals = exchange(column, parts)

    sizes = (groups, stations, rounds, slots, band_bins)
    spectrum = pltpu.VMEM((groups, 2 * chunks, stations, LANES), jnp.float32)
    cross = pltpu.VMEM((rows, band_bins), jnp.bfloat16)
    second_of = pltpu.VMEM((rows, 2 * band_bins), jnp.float32)
    scratch = ([spectrum] * 2 + [second_of] + [cross] * 4) * 2

    def cost(count):
        flops = 6 * rows * band_bins * lag_band * count
        return pl.CostEstimate(flops=flops, bytes_accessed=2 * 1024 * 1024, transcendentals=0)

    total = pltpu.VMEM((rows, half_band), jnp.float32)
    near_table = [band_tables[place] for place in (2, 3, 0, 1)]
    far_table = [band_tables[place] for place in (6, 7, 4, 5)]

    first, second, weight, even, odd = call(
        functools.partial(
            near_kernel, sizes, layout, len(near), steps * depth, [(i, i) for i in range(split)]
        ),
        "near_first",
        near_table + near,
        [
            pltpu.VMEM((rows, LANES), jnp.int32),
            pltpu.VMEM((rows, 2 * groups * stations), jnp.bfloat16),
            pltpu.VMEM((rows, LANES), jnp.float32),
        ]
        + [total] * 2,
        scratch,
        cost(split),
    )
    def add(name, layout, arrays, tables, some, sums):
        return call(
            functools.partial(next_kernel, sizes, layout, len(arrays), [(i, i) for i in some]),
            name,
            [*tables, *arrays, first, second, *sums],
            [total] * 2,
            scratch,
            cost(len(some)),
        )

    *diagonal, even = lax.optimization_barrier((*diagonals[0], even))
    far_first, layout_first = across_cores(far, diagonal, parts[0][0])
    even, odd = add("near_next", layout, near, near_table, range(split, steps), (even, odd))
    *diagonal, even = lax.optimization_barrier((*diagonals[1], even))
    far_next, layout_next = across_cores(far, diagonal, parts[1][0])
    even, odd = add("far_first", layout_first, far_first, far_table, range(middle), (even, odd))
    some = [(i, i) for i in range(middle, steps)]
    out = call(
        functools.partial(last_kernel, sizes, layout_next, len(far_next), some),
        "far_next",
        [*far_table, *far_next, first, second, even, odd, weight],
        jax.ShapeDtypeStruct((rows, lag_band), jnp.float32),
        [total] * 2 + [pltpu.VMEM((rows, lag_band), jnp.float32), pltpu.SemaphoreType.DMA((PARTS,))] + scratch,
        cost(len(some)),
    )
    out = out.reshape(1, rounds, groups, slots, lag_band)
    return out[:, :, :, :capacity]


def solution(mesh):
    placed = (P("grp", None, "freq"), P("grp"), P("grp", None, None, None))
    return jax.shard_map(
        per_device,
        mesh=mesh,
        in_specs=placed,
        out_specs=P("grp", None, None, None, "freq"),
        check_vma=False,
    )
```

```python
import functools
import math

import jax
import jax.numpy as jnp
from jax import lax
from jax.experimental import pallas as pl
from jax.experimental.pallas import tpu as pltpu
from jax.sharding import PartitionSpec as P

LAGS = 4096
LANES = 128
SUBLANES = 8
PARTS = 4


def split_bf16(values, parts):
    pieces = []
    for _ in range(parts - 1):
        piece = values.astype(jnp.bfloat16)
        pieces.append(piece)
        values = values - piece.astype(jnp.float32)
    pieces.append(values.astype(jnp.bfloat16))
    return pieces


def iota(shape, axis):
    return lax.broadcasted_iota(jnp.int32, shape, axis)


def dot(left, right):
    return jnp.dot(left, right, preferred_element_type=jnp.float32)


def padded(count, multiple):
    return -(-count // multiple) * multiple


def pick_slots(extras, places, me, stations, rounds, slots):
    groups = len(extras)
    pairs = stations * stations
    listed = rounds * pairs
    rows = rounds * groups * slots
    place = iota((groups, groups), 1)
    held_by = jnp.zeros((groups, groups), jnp.int32)
    for position in range(groups):
        held_by = jnp.where(place == position, places[position], held_by)
    lane = iota((1, listed), 1)

    def by_group(row, shift):
        wanted = (iota((groups, groups), 0) + groups - shift) % groups
        held = jnp.concatenate([extra[row : row + 1, :] for extra in extras], axis=0)
        return dot((held_by == wanted).astype(jnp.bfloat16), held.astype(jnp.bfloat16))

    def of_station(values, number):
        spread = iota((LANES, listed), 0) == number
        return dot(values.astype(jnp.bfloat16), spread.astype(jnp.bfloat16))

    owner_ids = jnp.zeros((groups, listed), jnp.float32)
    partner_mask = jnp.zeros((groups, listed), jnp.float32)
    for index in range(rounds):
        of_round = lane // pairs == index
        owner_ids = jnp.where(of_round, by_group(index, 0), owner_ids)
        second = of_station(by_group(rounds, index + 1), lane % stations)
        partner_mask = jnp.where(of_round, second, partner_mask)
    own_mask = of_station(by_group(rounds, 0), lane % pairs // stations)
    pair_weight = own_mask * partner_mask
    mine = owner_ids == me.astype(jnp.float32)
    from_pair, to_pair = iota((listed, listed), 0), iota((listed, listed), 1)
    before = (from_pair < to_pair) & (from_pair // pairs == to_pair // pairs)
    rank = dot(mine.astype(jnp.bfloat16), before.astype(jnp.bfloat16))
    marked = jnp.where(mine, rank, -1.0).astype(jnp.bfloat16)
    of_group = (iota((rows, groups), 0) // slots) % groups == iota((rows, groups), 1)
    of_group = of_group.astype(jnp.bfloat16)
    row_id, lane_id = iota((rows, listed), 0), iota((rows, listed), 1)
    chosen = (dot(of_group, marked) == (row_id % slots).astype(jnp.float32)) & (
        row_id // (groups * slots) == lane_id // pairs
    )
    weighed = jnp.where(chosen, dot(of_group, pair_weight.astype(jnp.bfloat16)), 0.0)
    weight = dot(weighed.astype(jnp.bfloat16), jnp.ones((listed, LANES), jnp.bfloat16))
    chosen = chosen.astype(jnp.bfloat16)
    pair_id = iota((listed, LANES), 0) % pairs
    first = dot(chosen, (pair_id // stations).astype(jnp.bfloat16))
    second = dot(chosen, (pair_id % stations).astype(jnp.bfloat16))
    return first.astype(jnp.int32), second.astype(jnp.int32), weight


def band_moves(shards):
    return [0] + list(range(shards - 2, 0, -2))


def make_tables(parity, table_refs, turn_refs, base_refs, bin_total):
    place = lax.axis_index("freq").astype(jnp.int32)
    near_cos, near_sin = base_refs
    fine, half_band = near_cos.shape
    steps, chunks, _ = turn_refs[0].shape
    band_bins = chunks * LANES
    moves = band_moves(bin_total // band_bins)

    def circle(turns):
        angles = (turns & (4 * bin_total - 1)).astype(jnp.float32) * (math.pi / (2 * bin_total))
        return jnp.cos(angles), jnp.sin(angles)

    def every(count, start, step):
        bins = start + iota((count, half_band), 0) * step
        return circle(bins * (2 * iota((count, half_band), 1) + 1))

    def added(cos, sin, other_cos, other_sin):
        return cos * other_cos - sin * other_sin, sin * other_cos + cos * other_sin

    low_cos, low_sin = every(SUBLANES, 0, 1)
    high_cos, high_sin = every(fine // SUBLANES, 0, SUBLANES)
    for index in range(fine // SUBLANES):
        rows, one = slice(index * SUBLANES, (index + 1) * SUBLANES), slice(index, index + 1)
        near_cos[rows, :], near_sin[rows, :] = added(
            high_cos[one], high_sin[one], low_cos, low_sin
        )

    centre = 2 * half_band * (2 * place + 1) - 1 - LAGS
    norm = 1.0 / math.sqrt(bin_total)
    for step in range(steps):
        start = (place ^ (moves[step] + parity)) * band_bins
        cos, sin = every(band_bins // fine, start, fine)
        for part in range(band_bins // fine):
            one = slice(part, part + 1)
            values = added(cos[one], sin[one], near_cos[...], near_sin[...])
            rows = slice(step * band_bins + part * fine, step * band_bins + (part + 1) * fine)
            for table, value in zip(table_refs, values):
                table[rows, :half_band], table[rows, half_band:] = split_bf16(value, 2)
        bins = start + iota((chunks, LANES), 0) * LANES + iota((chunks, LANES), 1)
        for turn, value in zip(turn_refs, circle(bins * centre)):
            turn[step] = value * norm


def table_kernel(bin_total, owners_hbm, mask_hbm, *refs):
    near_refs, far_refs, extras = refs[:4], refs[4:8], refs[8]
    base_refs, (owners_ref, mask_ref, sems) = refs[9:11], refs[11:]
    copies = [
        pltpu.make_async_copy(owners_hbm, owners_ref, sems.at[0]),
        pltpu.make_async_copy(mask_hbm, mask_ref, sems.at[1]),
    ]
    for copy in copies:
        copy.start()
    make_tables(0, near_refs[:2], near_refs[2:], base_refs, bin_total)
    make_tables(1, far_refs[:2], far_refs[2:], base_refs, bin_total)
    for copy in copies:
        copy.wait()
    extras[...] = jnp.zeros_like(extras)
    rounds, pairs = owners_ref.shape[1], owners_ref.shape[3]
    for index in range(rounds):
        lanes = slice(index * pairs, (index + 1) * pairs)
        extras[index : index + 1, lanes] = owners_ref[0, index].astype(jnp.float32)
    extras[rounds : rounds + 1, : mask_ref.shape[1]] = mask_ref[...].astype(jnp.float32)


def add_bands(sizes, steps, places, turn_refs, table_refs, blocks, picks, sums, scratch):
    groups, stations, rounds, slots, band_bins = sizes
    chunks = band_bins // LANES
    depth = 2 * chunks * stations
    half = sums[0].shape[1]
    first, second = picks
    sets = [scratch[6 * index : 6 * (index + 1)] for index in range(2)]
    part_groups = [range(part * groups // PARTS, (part + 1) * groups // PARTS) for part in range(PARTS)]
    bins_at_once = max(band_bins // 2, LANES)
    pieces = [(which, start) for which in range(2) for start in range(0, band_bins, bins_at_once)]

    def prepare(index):
        (step, place_step), (held, turned) = steps[index], sets[index % 2][:2]
        for position, (ref, offset) in enumerate(blocks):
            group = places[position]
            for q in range(chunks):
                turn_cos, turn_sin = [turn[step, q : q + 1, :] for turn in turn_refs]
                start = offset + place_step * depth + q * stations
                real = ref[start : start + stations, :]
                start += chunks * stations
                imag = ref[start : start + stations, :]
                held[group, q] = real
                held[group, chunks + q] = imag
                turned[group, q] = real * turn_cos + imag * turn_sin
                turned[group, chunks + q] = imag * turn_cos - real * turn_sin

    def multiply(index, part):
        held, turned, *cross = sets[index % 2]
        for group in part_groups[part]:
            sources = []
            for number in range(rounds):
                start = (number * groups + group) * slots
                lines = [slice(start + o, start + o + SUBLANES) for o in range(0, slots, SUBLANES)]
                partner = (group + groups - 1 - number) % groups
                sources.append((start, partner, [(first[line, :], second[line, :]) for line in lines]))
            for q in range(chunks):
                lanes = slice(q * LANES, (q + 1) * LANES)
                own_real, own_imag = held[group, q], held[group, chunks + q]
                for start, partner, indices in sources:
                    real, imag = turned[partner, q], turned[partner, chunks + q]
                    reals, imags = [], []
                    for index_a, index_b in indices:
                        a_real = jnp.take_along_axis(own_real, index_a, axis=0)
                        a_imag = jnp.take_along_axis(own_imag, index_a, axis=0)
                        b_real = jnp.take_along_axis(real, index_b, axis=0)
                        b_imag = jnp.take_along_axis(imag, index_b, axis=0)
                        reals.append(a_real * b_real + a_imag * b_imag)
                        imags.append(a_imag * b_real - a_real * b_imag)
                    rows = slice(start, start + slots)
                    for place, values in ((0, reals), (2, imags)):
                        high, low = split_bf16(jnp.concatenate(values, axis=0), 2)
                        cross[place][rows, lanes] = high
                        cross[place + 1][rows, lanes] = low

    def transform(index, which, start):
        step, (high, low) = steps[index][0], sets[index % 2][2 + 2 * which : 4 + 2 * which]
        lanes = slice(start, start + bins_at_once)
        bins = slice(step * band_bins + start, step * band_bins + start + bins_at_once)
        table, total = table_refs[which], sums[which]
        cross, exact = high[:, lanes], table[bins, :half]
        total[...] += dot(
            jnp.concatenate([cross, cross, low[:, lanes]], axis=1),
            jnp.concatenate([exact, table[bins, half:], exact], axis=0),
        )

    prepare(0)
    for part in range(PARTS):
        multiply(0, part)
    for index in range(len(steps)):
        more = index + 1 < len(steps)
        if more:
            prepare(index + 1)
        for part in range(PARTS):
            if more:
                multiply(index + 1, part)
            if part < len(pieces):
                transform(index, *pieces[part])


def placed_blocks(array_refs, layout, groups):
    me = lax.axis_index("grp").astype(jnp.int32)
    blocks = [(array_refs[index], offset) for index, offset, _ in layout]
    return blocks, [moved(me, move, groups) for _, _, move in layout]


def near_kernel(sizes, layout, array_count, depth, steps, *refs):
    groups, stations, rounds, slots = sizes[:4]
    turn_refs, table_refs, refs = refs[:2], refs[2:4], refs[4:]
    array_refs, refs = refs[:array_count], refs[array_count:]
    (first, second, weight, even, odd), scratch = refs[:5], refs[5:]
    blocks, places = placed_blocks(array_refs, layout, groups)
    extras = [ref[offset + depth : offset + depth + SUBLANES, :] for ref, offset in blocks]
    first[...], second[...], weight[...] = pick_slots(
        extras, places, lax.axis_index("grp"), stations, rounds, slots
    )
    even[...] = jnp.zeros_like(even)
    odd[...] = jnp.zeros_like(odd)
    add_bands(
        sizes, steps, places, turn_refs, table_refs, blocks, (first, second), (even, odd), scratch
    )


def next_kernel(sizes, layout, array_count, steps, *refs):
    turn_refs, table_refs, refs = refs[:2], refs[2:4], refs[4:]
    array_refs, refs = refs[:array_count], refs[array_count:]
    (first, second, even_in, odd_in, even, odd), scratch = refs[:6], refs[6:]
    even[...] = even_in[...]
    odd[...] = odd_in[...]
    blocks, places = placed_blocks(array_refs, layout, sizes[0])
    add_bands(
        sizes, steps, places, turn_refs, table_refs, blocks, (first, second), (even, odd), scratch
    )


def last_kernel(sizes, layout, array_count, steps, *refs):
    turn_refs, table_refs, refs = refs[:2], refs[2:4], refs[4:]
    array_refs, refs = refs[:array_count], refs[array_count:]
    first, second, even_in, odd_in, weight, out_ref, even, odd, result, sems = refs[:10]
    even[...] = even_in[...]
    odd[...] = odd_in[...]
    blocks, places = placed_blocks(array_refs, layout, sizes[0])
    add_bands(
        sizes, steps, places, turn_refs, table_refs, blocks, (first, second), (even, odd), refs[10:]
    )
    half = even.shape[1]
    mirror = (iota((half, half), 0) + iota((half, half), 1) == half - 1).astype(jnp.bfloat16)
    copies = []
    block = even.shape[0] // PARTS
    for part in range(PARTS):
        lines = slice(part * block, (part + 1) * block)
        row_weight = weight[lines, 0:1]
        high, low = split_bf16((even[lines, :] + odd[lines, :]) * row_weight, 2)
        result[lines, :half] = dot(high, mirror) + dot(low, mirror)
        result[lines, half:] = (even[lines, :] - odd[lines, :]) * row_weight
        copies.append(pltpu.make_async_copy(result.at[lines], out_ref.at[lines], sems.at[part]))
        copies[part].start()
    for copy in copies:
        copy.wait()


def moved(me, move, size):
    return me ^ move if size & (size - 1) == 0 else lax.rem(me + size - move, size)


def moved_index(me, move, size):
    return me ^ move if size & (size - 1) == 0 else (me - move) % size


def fetched(block, group_move, band_move):
    groups, shards = lax.axis_size("grp"), lax.axis_size("freq")
    route = [
        (
            moved_index(group, group_move, groups) * shards + moved_index(band, band_move, shards),
            group * shards + band,
        )
        for group in range(groups)
        for band in range(shards)
    ]
    return lax.ppermute(block, ("grp", "freq"), route)


def exchange(column, parts):
    groups = lax.axis_size("grp")
    if groups != 4:
        near = [column] + [fetched(column, move, 0) for move in range(1, groups)]
        layout = [(move, 0, move) for move in range(groups)]
        far = [fetched(column, move, 1) for move in range(groups)]
        return near, layout, far, [[] for _ in parts]
    across, core = fetched(column, 2, 0), fetched(column, 1, 0)
    beside = fetched(longer(column), 0, 1)
    across, core = lax.optimization_barrier((across, core))
    near = [column, core, across, fetched(across, 1, 0)]
    diagonals = [[fetched(longer(across[start:stop]), 0, 1)] for start, stop in parts]
    far = [beside, fetched(beside, 1, 0)]
    return near, [(place, 0, place) for place in range(4)], far, diagonals


def longer(block):
    return jnp.concatenate([block, block[-SUBLANES:]], axis=0)


def across_cores(far, diagonal, first_row):
    arrays = far + [block for own in diagonal for block in (own, fetched(own, 1, 0))]
    layout = [
        (place, 0 if place < len(far) else -first_row, place) for place in range(len(arrays))
    ]
    return arrays, layout


def per_device(spectra, station_mask, owners):
    stations, _, band_bins = spectra.shape
    groups = lax.axis_size("grp")
    shards = lax.axis_size("freq")
    rounds = owners.shape[1]
    pairs = stations * stations
    bin_total = band_bins * shards
    capacity = (2 * pairs + groups - 1) // groups
    slots = padded(capacity, 2 * SUBLANES)
    lag_band = LAGS // shards
    half_band = lag_band // 2
    chunks = band_bins // LANES
    rows = rounds * groups * slots

    vector = pl.BlockSpec(memory_space=pltpu.VMEM)
    in_hbm = pl.BlockSpec(memory_space=pltpu.HBM)

    def call(kernel, name, arrays, out_shape, scratch, cost, others=()):
        arrays = [pltpu.with_memory_space_constraint(array, pltpu.VMEM) for array in arrays]
        others = [pltpu.with_memory_space_constraint(array, pltpu.HBM) for array in others]
        to_hbm = isinstance(out_shape, jax.ShapeDtypeStruct)
        return pl.pallas_call(
            kernel,
            out_shape=out_shape,
            in_specs=[in_hbm] * len(others) + [vector] * len(arrays),
            out_specs=in_hbm if to_hbm else [vector] * len(out_shape),
            scratch_shapes=scratch,
            compiler_params=pltpu.CompilerParams(vmem_limit_bytes=24 * 1024 * 1024),
            cost_estimate=cost,
            name=name,
        )(*others, *arrays)

    steps = shards // 2
    tiles = spectra.reshape(stations, 2, chunks, LANES).transpose(1, 2, 0, 3)
    tiles = tiles.reshape(2 * chunks * stations, LANES)
    column = [fetched(tiles, 0, move) if move else tiles for move in band_moves(shards)]

    table = pltpu.VMEM((steps * band_bins, lag_band), jnp.bfloat16)
    turn = pltpu.VMEM((steps, chunks, LANES), jnp.float32)
    base = pltpu.VMEM((64, half_band), jnp.float32)
    table_cost = pl.CostEstimate(
        flops=0, bytes_accessed=4 * bin_total * half_band, transcendentals=0
    )
    *band_tables, extras = call(
        functools.partial(table_kernel, bin_total),
        "tables",
        [],
        ([table] * 2 + [turn] * 2) * 2 + [pltpu.VMEM((SUBLANES, LANES), jnp.float32)],
        [base] * 2
        + [
            pltpu.VMEM((1, rounds, 1, pairs), jnp.int32),
            pltpu.VMEM((1, stations), jnp.int32),
            pltpu.SemaphoreType.DMA((2,)),
        ],
        table_cost,
        [owners.transpose(0, 1, 3, 2), station_mask.reshape(1, stations)],
    )
    column = jnp.concatenate(column + [extras], axis=0)
    depth = 2 * chunks * stations
    split = middle = steps // 2
    parts = [(0, middle * depth), (middle * depth, steps * depth)]
    near, layout, far, diagonals = exchange(column, parts)

    sizes = (groups, stations, rounds, slots, band_bins)
    spectrum = pltpu.VMEM((groups, 2 * chunks, stations, LANES), jnp.float32)
    cross = pltpu.VMEM((rows, band_bins), jnp.bfloat16)
    scratch = ([spectrum] * 2 + [cross] * 4) * 2

    def cost(count):
        flops = 6 * rows * band_bins * lag_band * count
        return pl.CostEstimate(flops=flops, bytes_accessed=2 * 1024 * 1024, transcendentals=0)

    total = pltpu.VMEM((rows, half_band), jnp.float32)
    index = pltpu.VMEM((rows, LANES), jnp.int32)
    near_table = [band_tables[place] for place in (2, 3, 0, 1)]
    far_table = [band_tables[place] for place in (6, 7, 4, 5)]

    first, second, weight, even, odd = call(
        functools.partial(
            near_kernel, sizes, layout, len(near), steps * depth, [(i, i) for i in range(split)]
        ),
        "near_first",
        near_table + near,
        [index] * 2 + [pltpu.VMEM((rows, LANES), jnp.float32)] + [total] * 2,
        scratch,
        cost(split),
    )
    def add(name, layout, arrays, tables, some, sums):
        return call(
            functools.partial(next_kernel, sizes, layout, len(arrays), [(i, i) for i in some]),
            name,
            [*tables, *arrays, first, second, *sums],
            [total] * 2,
            scratch,
            cost(len(some)),
        )

    *diagonal, even = lax.optimization_barrier((*diagonals[0], even))
    far_first, layout_first = across_cores(far, diagonal, parts[0][0])
    even, odd = add("near_next", layout, near, near_table, range(split, steps), (even, odd))
    *diagonal, even = lax.optimization_barrier((*diagonals[1], even))
    far_next, layout_next = across_cores(far, diagonal, parts[1][0])
    even, odd = add("far_first", layout_first, far_first, far_table, range(middle), (even, odd))
    some = [(i, i) for i in range(middle, steps)]
    out = call(
        functools.partial(last_kernel, sizes, layout_next, len(far_next), some),
        "far_next",
        [*far_table, *far_next, first, second, even, odd, weight],
        jax.ShapeDtypeStruct((rows, lag_band), jnp.float32),
        [total] * 2 + [pltpu.VMEM((rows, lag_band), jnp.float32), pltpu.SemaphoreType.DMA((PARTS,))] + scratch,
        cost(len(some)),
    )
    out = out.reshape(1, rounds, groups, slots, lag_band)
    return out[:, :, :, :capacity]


def solution(mesh):
    placed = (P("grp", None, "freq"), P("grp"), P("grp", None, None, None))
    return jax.shard_map(
        per_device,
        mesh=mesh,
        in_specs=placed,
        out_specs=P("grp", None, None, None, "freq"),
        check_vma=False,
    )
```

```python
import functools
import math

import jax
import jax.numpy as jnp
from jax import lax
from jax.experimental import pallas as pl
from jax.experimental.pallas import tpu as pltpu
from jax.sharding import PartitionSpec as P

LAGS = 4096
LANES = 128
SUBLANES = 8
PARTS = 4


def split_bf16(values, parts):
    pieces = []
    for _ in range(parts - 1):
        piece = values.astype(jnp.bfloat16)
        pieces.append(piece)
        values = values - piece.astype(jnp.float32)
    pieces.append(values.astype(jnp.bfloat16))
    return pieces


def iota(shape, axis):
    return lax.broadcasted_iota(jnp.int32, shape, axis)


def dot(left, right):
    return jnp.dot(left, right, preferred_element_type=jnp.float32)


def padded(count, multiple):
    return -(-count // multiple) * multiple


def pick_slots(extras, places, me, stations, rounds, slots):
    groups = len(extras)
    pairs = stations * stations
    listed = rounds * pairs
    rows = rounds * groups * slots
    place = iota((groups, groups), 1)
    held_by = jnp.zeros((groups, groups), jnp.int32)
    for position in range(groups):
        held_by = jnp.where(place == position, places[position], held_by)
    lane = iota((1, listed), 1)

    def by_group(row, shift):
        wanted = (iota((groups, groups), 0) + groups - shift) % groups
        held = jnp.concatenate([extra[row : row + 1, :] for extra in extras], axis=0)
        return dot((held_by == wanted).astype(jnp.bfloat16), held.astype(jnp.bfloat16))

    def of_station(values, number):
        spread = iota((LANES, listed), 0) == number
        return dot(values.astype(jnp.bfloat16), spread.astype(jnp.bfloat16))

    owner_ids = jnp.zeros((groups, listed), jnp.float32)
    partner_mask = jnp.zeros((groups, listed), jnp.float32)
    for index in range(rounds):
        of_round = lane // pairs == index
        owner_ids = jnp.where(of_round, by_group(index, 0), owner_ids)
        second = of_station(by_group(rounds, index + 1), lane % stations)
        partner_mask = jnp.where(of_round, second, partner_mask)
    own_mask = of_station(by_group(rounds, 0), lane % pairs // stations)
    pair_weight = own_mask * partner_mask
    mine = owner_ids == me.astype(jnp.float32)
    from_pair, to_pair = iota((listed, listed), 0), iota((listed, listed), 1)
    before = (from_pair < to_pair) & (from_pair // pairs == to_pair // pairs)
    rank = dot(mine.astype(jnp.bfloat16), before.astype(jnp.bfloat16))
    marked = jnp.where(mine, rank, -1.0).astype(jnp.bfloat16)
    of_group = (iota((rows, groups), 0) // slots) % groups == iota((rows, groups), 1)
    of_group = of_group.astype(jnp.bfloat16)
    row_id, lane_id = iota((rows, listed), 0), iota((rows, listed), 1)
    chosen = (dot(of_group, marked) == (row_id % slots).astype(jnp.float32)) & (
        row_id // (groups * slots) == lane_id // pairs
    )
    weighed = jnp.where(chosen, dot(of_group, pair_weight.astype(jnp.bfloat16)), 0.0)
    weight = dot(weighed.astype(jnp.bfloat16), jnp.ones((listed, LANES), jnp.bfloat16))
    chosen = chosen.astype(jnp.bfloat16)
    pair_id = iota((listed, LANES), 0) % pairs
    first = dot(chosen, (pair_id // stations).astype(jnp.bfloat16))
    second = dot(chosen, (pair_id % stations).astype(jnp.bfloat16))
    return first.astype(jnp.int32), second.astype(jnp.int32), weight


def band_moves(shards):
    return [0] + list(range(shards - 2, 0, -2))


def make_tables(parity, table_refs, turn_refs, base_refs, bin_total):
    place = lax.axis_index("freq").astype(jnp.int32)
    near_cos, near_sin = base_refs
    fine, half_band = near_cos.shape
    steps, chunks, _ = turn_refs[0].shape
    band_bins = chunks * LANES
    moves = band_moves(bin_total // band_bins)

    def circle(turns):
        angles = (turns & (4 * bin_total - 1)).astype(jnp.float32) * (math.pi / (2 * bin_total))
        return jnp.cos(angles), jnp.sin(angles)

    def every(count, start, step):
        bins = start + iota((count, half_band), 0) * step
        return circle(bins * (2 * iota((count, half_band), 1) + 1))

    def added(cos, sin, other_cos, other_sin):
        return cos * other_cos - sin * other_sin, sin * other_cos + cos * other_sin

    low_cos, low_sin = every(SUBLANES, 0, 1)
    high_cos, high_sin = every(fine // SUBLANES, 0, SUBLANES)
    for index in range(fine // SUBLANES):
        rows, one = slice(index * SUBLANES, (index + 1) * SUBLANES), slice(index, index + 1)
        near_cos[rows, :], near_sin[rows, :] = added(
            high_cos[one], high_sin[one], low_cos, low_sin
        )

    centre = 2 * half_band * (2 * place + 1) - 1 - LAGS
    norm = 1.0 / math.sqrt(bin_total)
    for step in range(steps):
        start = (place ^ (moves[step] + parity)) * band_bins
        cos, sin = every(band_bins // fine, start, fine)
        for part in range(band_bins // fine):
            one = slice(part, part + 1)
            values = added(cos[one], sin[one], near_cos[...], near_sin[...])
            rows = slice(step * band_bins + part * fine, step * band_bins + (part + 1) * fine)
            for table, value in zip(table_refs, values):
                table[rows, :half_band], table[rows, half_band:] = split_bf16(value, 2)
        bins = start + iota((chunks, LANES), 0) * LANES + iota((chunks, LANES), 1)
        for turn, value in zip(turn_refs, circle(bins * centre)):
            turn[step] = value * norm


def table_kernel(bin_total, owners_hbm, mask_hbm, *refs):
    near_refs, far_refs, extras = refs[:4], refs[4:8], refs[8]
    base_refs, (owners_ref, mask_ref, sems) = refs[9:11], refs[11:]
    copies = [
        pltpu.make_async_copy(owners_hbm, owners_ref, sems.at[0]),
        pltpu.make_async_copy(mask_hbm, mask_ref, sems.at[1]),
    ]
    for copy in copies:
        copy.start()
    make_tables(0, near_refs[:2], near_refs[2:], base_refs, bin_total)
    make_tables(1, far_refs[:2], far_refs[2:], base_refs, bin_total)
    for copy in copies:
        copy.wait()
    extras[...] = jnp.zeros_like(extras)
    rounds, pairs = owners_ref.shape[1], owners_ref.shape[3]
    for index in range(rounds):
        lanes = slice(index * pairs, (index + 1) * pairs)
        extras[index : index + 1, lanes] = owners_ref[0, index].astype(jnp.float32)
    extras[rounds : rounds + 1, : mask_ref.shape[1]] = mask_ref[...].astype(jnp.float32)


def add_bands(sizes, steps, places, turn_refs, table_refs, blocks, picks, sums, scratch):
    groups, stations, rounds, slots, band_bins = sizes
    chunks = band_bins // LANES
    depth = 2 * chunks * stations
    half = sums[0].shape[1]
    first, second = picks
    sets = [scratch[6 * index : 6 * (index + 1)] for index in range(2)]
    part_groups = [range(part * groups // PARTS, (part + 1) * groups // PARTS) for part in range(PARTS)]
    bins_at_once = max(band_bins // 2, LANES)
    pieces = [(which, start) for which in range(2) for start in range(0, band_bins, bins_at_once)]

    def prepare(index):
        (step, place_step), (held, turned) = steps[index], sets[index % 2][:2]
        for position, (ref, offset) in enumerate(blocks):
            group = places[position]
            for q in range(chunks):
                turn_cos, turn_sin = [turn[step, q : q + 1, :] for turn in turn_refs]
                start = offset + place_step * depth + q * stations
                real = ref[start : start + stations, :]
                start += chunks * stations
                imag = ref[start : start + stations, :]
                held[group, q] = real
                held[group, chunks + q] = imag
                turned[group, q] = real * turn_cos + imag * turn_sin
                turned[group, chunks + q] = imag * turn_cos - real * turn_sin

    def multiply(index, part):
        held, turned, *cross = sets[index % 2]
        for group in part_groups[part]:
            sources = []
            for number in range(rounds):
                start = (number * groups + group) * slots
                lines = [slice(start + o, start + o + SUBLANES) for o in range(0, slots, SUBLANES)]
                partner = (group + groups - 1 - number) % groups
                sources.append((start, partner, [(first[line, :], second[line, :]) for line in lines]))
            for q in range(chunks):
                lanes = slice(q * LANES, (q + 1) * LANES)
                own_real, own_imag = held[group, q], held[group, chunks + q]
                for start, partner, indices in sources:
                    real, imag = turned[partner, q], turned[partner, chunks + q]
                    reals, imags = [], []
                    for index_a, index_b in indices:
                        a_real = jnp.take_along_axis(own_real, index_a, axis=0)
                        a_imag = jnp.take_along_axis(own_imag, index_a, axis=0)
                        b_real = jnp.take_along_axis(real, index_b, axis=0)
                        b_imag = jnp.take_along_axis(imag, index_b, axis=0)
                        reals.append(a_real * b_real + a_imag * b_imag)
                        imags.append(a_imag * b_real - a_real * b_imag)
                    rows = slice(start, start + slots)
                    for place, values in ((0, reals), (2, imags)):
                        high, low = split_bf16(jnp.concatenate(values, axis=0), 2)
                        cross[place][rows, lanes] = high
                        cross[place + 1][rows, lanes] = low

    def transform(index, which, start):
        step, (high, low) = steps[index][0], sets[index % 2][2 + 2 * which : 4 + 2 * which]
        lanes = slice(start, start + bins_at_once)
        bins = slice(step * band_bins + start, step * band_bins + start + bins_at_once)
        table, total = table_refs[which], sums[which]
        cross, exact = high[:, lanes], table[bins, :half]
        total[...] += dot(
            jnp.concatenate([cross, cross, low[:, lanes]], axis=1),
            jnp.concatenate([exact, table[bins, half:], exact], axis=0),
        )

    prepare(0)
    for part in range(PARTS):
        multiply(0, part)
    for index in range(len(steps)):
        more = index + 1 < len(steps)
        if more:
            prepare(index + 1)
        for part in range(PARTS):
            if more:
                multiply(index + 1, part)
            if part < len(pieces):
                transform(index, *pieces[part])


def placed_blocks(array_refs, layout, groups):
    me = lax.axis_index("grp").astype(jnp.int32)
    blocks = [(array_refs[index], offset) for index, offset, _ in layout]
    return blocks, [moved(me, move, groups) for _, _, move in layout]


def near_kernel(sizes, layout, array_count, depth, steps, *refs):
    groups, stations, rounds, slots = sizes[:4]
    turn_refs, table_refs, refs = refs[:2], refs[2:4], refs[4:]
    array_refs, refs = refs[:array_count], refs[array_count:]
    (first, second, weight, even, odd), scratch = refs[:5], refs[5:]
    blocks, places = placed_blocks(array_refs, layout, groups)
    extras = [ref[offset + depth : offset + depth + SUBLANES, :] for ref, offset in blocks]
    first[...], second[...], weight[...] = pick_slots(
        extras, places, lax.axis_index("grp"), stations, rounds, slots
    )
    even[...] = jnp.zeros_like(even)
    odd[...] = jnp.zeros_like(odd)
    add_bands(
        sizes, steps, places, turn_refs, table_refs, blocks, (first, second), (even, odd), scratch
    )


def next_kernel(sizes, layout, array_count, steps, *refs):
    turn_refs, table_refs, refs = refs[:2], refs[2:4], refs[4:]
    array_refs, refs = refs[:array_count], refs[array_count:]
    (first, second, even_in, odd_in, even, odd), scratch = refs[:6], refs[6:]
    even[...] = even_in[...]
    odd[...] = odd_in[...]
    blocks, places = placed_blocks(array_refs, layout, sizes[0])
    add_bands(
        sizes, steps, places, turn_refs, table_refs, blocks, (first, second), (even, odd), scratch
    )


def last_kernel(sizes, layout, array_count, steps, *refs):
    turn_refs, table_refs, refs = refs[:2], refs[2:4], refs[4:]
    array_refs, refs = refs[:array_count], refs[array_count:]
    first, second, even_in, odd_in, weight, out_ref, even, odd, result, sems = refs[:10]
    even[...] = even_in[...]
    odd[...] = odd_in[...]
    blocks, places = placed_blocks(array_refs, layout, sizes[0])
    add_bands(
        sizes, steps, places, turn_refs, table_refs, blocks, (first, second), (even, odd), refs[10:]
    )
    half = even.shape[1]
    mirror = (iota((half, half), 0) + iota((half, half), 1) == half - 1).astype(jnp.bfloat16)
    copies = []
    block = even.shape[0] // PARTS
    for part in range(PARTS):
        lines = slice(part * block, (part + 1) * block)
        row_weight = weight[lines, 0:1]
        high, low = split_bf16((even[lines, :] + odd[lines, :]) * row_weight, 2)
        result[lines, :half] = dot(high, mirror) + dot(low, mirror)
        result[lines, half:] = (even[lines, :] - odd[lines, :]) * row_weight
        copies.append(pltpu.make_async_copy(result.at[lines], out_ref.at[lines], sems.at[part]))
        copies[part].start()
    for copy in copies:
        copy.wait()


def moved(me, move, size):
    return me ^ move if size & (size - 1) == 0 else lax.rem(me + size - move, size)


def moved_index(me, move, size):
    return me ^ move if size & (size - 1) == 0 else (me - move) % size


def fetched(block, group_move, band_move):
    groups, shards = lax.axis_size("grp"), lax.axis_size("freq")
    route = [
        (
            moved_index(group, group_move, groups) * shards + moved_index(band, band_move, shards),
            group * shards + band,
        )
        for group in range(groups)
        for band in range(shards)
    ]
    return lax.ppermute(block, ("grp", "freq"), route)


def exchange(column, parts):
    groups = lax.axis_size("grp")
    if groups != 4:
        near = [column] + [fetched(column, move, 0) for move in range(1, groups)]
        layout = [(move, 0, move) for move in range(groups)]
        far = [fetched(column, move, 1) for move in range(groups)]
        return near, layout, far, [[] for _ in parts]
    across, core = fetched(column, 2, 0), fetched(column, 1, 0)
    beside = fetched(longer(column), 0, 1)
    across, core = lax.optimization_barrier((across, core))
    near = [column, core, across, fetched(across, 1, 0)]
    diagonals = [[fetched(across[start:stop], 0, 1)] for start, stop in parts]
    far = [beside, fetched(beside, 1, 0)]
    return near, [(place, 0, place) for place in range(4)], far, diagonals


def longer(block):
    return jnp.concatenate([block, block[-SUBLANES:]], axis=0)


def across_cores(far, diagonal, first_row):
    arrays = far + [block for own in diagonal for block in (own, fetched(own, 1, 0))]
    layout = [
        (place, 0 if place < len(far) else -first_row, place) for place in range(len(arrays))
    ]
    return arrays, layout


def per_device(spectra, station_mask, owners):
    stations, _, band_bins = spectra.shape
    groups = lax.axis_size("grp")
    shards = lax.axis_size("freq")
    rounds = owners.shape[1]
    pairs = stations * stations
    bin_total = band_bins * shards
    capacity = (2 * pairs + groups - 1) // groups
    slots = padded(capacity, 2 * SUBLANES)
    lag_band = LAGS // shards
    half_band = lag_band // 2
    chunks = band_bins // LANES
    rows = rounds * groups * slots

    vector = pl.BlockSpec(memory_space=pltpu.VMEM)
    in_hbm = pl.BlockSpec(memory_space=pltpu.HBM)

    def call(kernel, name, arrays, out_shape, scratch, cost, others=()):
        arrays = [pltpu.with_memory_space_constraint(array, pltpu.VMEM) for array in arrays]
        others = [pltpu.with_memory_space_constraint(array, pltpu.HBM) for array in others]
        to_hbm = isinstance(out_shape, jax.ShapeDtypeStruct)
        return pl.pallas_call(
            kernel,
            out_shape=out_shape,
            in_specs=[in_hbm] * len(others) + [vector] * len(arrays),
            out_specs=in_hbm if to_hbm else [vector] * len(out_shape),
            scratch_shapes=scratch,
            compiler_params=pltpu.CompilerParams(vmem_limit_bytes=24 * 1024 * 1024),
            cost_estimate=cost,
            name=name,
        )(*others, *arrays)

    steps = shards // 2
    tiles = spectra.reshape(stations, 2, chunks, LANES).transpose(1, 2, 0, 3)
    tiles = tiles.reshape(2 * chunks * stations, LANES)
    column = [fetched(tiles, 0, move) if move else tiles for move in band_moves(shards)]

    table = pltpu.VMEM((steps * band_bins, lag_band), jnp.bfloat16)
    turn = pltpu.VMEM((steps, chunks, LANES), jnp.float32)
    base = pltpu.VMEM((64, half_band), jnp.float32)
    table_cost = pl.CostEstimate(
        flops=0, bytes_accessed=4 * bin_total * half_band, transcendentals=0
    )
    *band_tables, extras = call(
        functools.partial(table_kernel, bin_total),
        "tables",
        [],
        ([table] * 2 + [turn] * 2) * 2 + [pltpu.VMEM((SUBLANES, LANES), jnp.float32)],
        [base] * 2
        + [
            pltpu.VMEM((1, rounds, 1, pairs), jnp.int32),
            pltpu.VMEM((1, stations), jnp.int32),
            pltpu.SemaphoreType.DMA((2,)),
        ],
        table_cost,
        [owners.transpose(0, 1, 3, 2), station_mask.reshape(1, stations)],
    )
    column = jnp.concatenate(column + [extras], axis=0)
    depth = 2 * chunks * stations
    split = middle = steps // 2
    parts = [(0, middle * depth), (middle * depth, steps * depth)]
    near, layout, far, diagonals = exchange(column, parts)

    sizes = (groups, stations, rounds, slots, band_bins)
    spectrum = pltpu.VMEM((groups, 2 * chunks, stations, LANES), jnp.float32)
    cross = pltpu.VMEM((rows, band_bins), jnp.bfloat16)
    scratch = ([spectrum] * 2 + [cross] * 4) * 2

    def cost(count):
        flops = 6 * rows * band_bins * lag_band * count
        return pl.CostEstimate(flops=flops, bytes_accessed=2 * 1024 * 1024, transcendentals=0)

    total = pltpu.VMEM((rows, half_band), jnp.float32)
    index = pltpu.VMEM((rows, LANES), jnp.int32)
    near_table = [band_tables[place] for place in (2, 3, 0, 1)]
    far_table = [band_tables[place] for place in (6, 7, 4, 5)]

    first, second, weight, even, odd = call(
        functools.partial(
            near_kernel, sizes, layout, len(near), steps * depth, [(i, i) for i in range(split)]
        ),
        "near_first",
        near_table + near,
        [index] * 2 + [pltpu.VMEM((rows, LANES), jnp.float32)] + [total] * 2,
        scratch,
        cost(split),
    )
    def add(name, layout, arrays, tables, some, sums):
        return call(
            functools.partial(next_kernel, sizes, layout, len(arrays), [(i, i) for i in some]),
            name,
            [*tables, *arrays, first, second, *sums],
            [total] * 2,
            scratch,
            cost(len(some)),
        )

    *diagonal, even = lax.optimization_barrier((*diagonals[0], even))
    far_first, layout_first = across_cores(far, diagonal, parts[0][0])
    even, odd = add("near_next", layout, near, near_table, range(split, steps), (even, odd))
    *diagonal, even = lax.optimization_barrier((*diagonals[1], even))
    far_next, layout_next = across_cores(far, diagonal, parts[1][0])
    even, odd = add("far_first", layout_first, far_first, far_table, range(middle), (even, odd))
    some = [(i, i) for i in range(middle, steps)]
    out = call(
        functools.partial(last_kernel, sizes, layout_next, len(far_next), some),
        "far_next",
        [*far_table, *far_next, first, second, even, odd, weight],
        jax.ShapeDtypeStruct((rows, lag_band), jnp.float32),
        [total] * 2 + [pltpu.VMEM((rows, lag_band), jnp.float32), pltpu.SemaphoreType.DMA((PARTS,))] + scratch,
        cost(len(some)),
    )
    out = out.reshape(1, rounds, groups, slots, lag_band)
    return out[:, :, :, :capacity]


def solution(mesh):
    placed = (P("grp", None, "freq"), P("grp"), P("grp", None, None, None))
    return jax.shard_map(
        per_device,
        mesh=mesh,
        in_specs=placed,
        out_specs=P("grp", None, None, None, "freq"),
        check_vma=False,
    )
```
